32 devices in a mesh: grp: 2 (over x), span: 16 (over z, y, core).
Axes of the slice: x: 2, y: 2, z: 4, core: 2. Of those that a mesh axis runs over, the one named last changes fastest.
Arguments:
- first_exposure: bfloat16 [1920, 96, 192], P(('grp', 'span')), parts along dimension 0, may hold values from 0 to 30
- second_exposure: bfloat16 [1920, 96, 192], P(('grp', 'span')), parts along dimension 0, may hold values from 0 to 30
- windows: int32 [256], P(('grp', 'span')), parts along dimension 0, may hold values from 0 to 10239, as said below
- shifts: int32 [3, 256], P(None, ('grp', 'span')), parts along dimension 1, may hold values from -8 to 8, as said below
Outputs:
- smoothed_update: float32 [3, 160, 128], P(None, ('grp', 'span')), parts along dimension 1
The draws below stay inside these ranges and needn't reach their ends.
There are 2 independent parts, one for each index of `grp`. The reference program is written for one: setup_inputs(seed, part) draws one part's arguments, and reference() takes and returns one part's arrays. A program takes and returns all parts, laid end to end along the dimension named above; each array names one. Nothing has to cross between parts.
Inputs may be any that keep to these rules, and one draw needn't show every extreme that they name: The windows of one device are distinct nodes whose spanwise grid row j has j // 5 equal to that device's index along span; exactly 4 of them have j % 5 < 2. `shifts`: row 0 is the spanwise shift (at most 3 in size), row 1 the wall-normal one (at most 4 in size), row 2 the streamwise one (at most 8 in size).
All inputs are finite; a program needn't handle non-finite values.
Results may differ from the reference program's by a relative error of at most 0.0022.
Values may be sent and summed in bfloat16 or wider, within the bound.
No kernel may reach another device: no remote copies, remote signals or barrier semaphores. Data moves between devices by JAX's collectives and lax.ppermute only.
A program may use at most 128 MiB of HBM per device.

```python
import jax
import jax.numpy as jnp
from jax import lax

W = 48
STRIDE = 12
CY = 60
NZ = 96
NX = 192
WIN_DEV = 8
DYM = 3
DZM = 4
DXM = 8
CAP = 4
NY = 960
GY = 80
GZ = 8
GX = 16
GZX = 128
WINDOWS = 128


def field_plan(key):
    base = jax.random.fold_in(key, 6173)
    keys = jax.random.split(base, 4)
    span_base = jax.random.randint(keys[0], (GY, 1, 1), -DYM, DYM + 1, dtype=jnp.int32)
    deep_base = jax.random.randint(keys[1], (GY, 1, 1), -DZM, DZM + 1, dtype=jnp.int32)
    along_base = jax.random.randint(keys[2], (GY, GZ, 1), -DXM, DXM + 1, dtype=jnp.int32)
    jitter = jax.random.randint(keys[3], (3, GY, GZ, GX), -1, 2, dtype=jnp.int32)
    shift_y = jnp.clip(span_base + jitter[0], -DYM, DYM)
    shift_z = jnp.clip(deep_base + jitter[1], -DZM, DZM)
    shift_x = jnp.clip(along_base + jitter[2], -DXM, DXM)
    return jnp.stack([shift_y, shift_z, shift_x]).astype(jnp.int32)


def window_plan(key):
    base = jax.random.fold_in(key, 4051)
    devices = WINDOWS // WIN_DEV
    tile_rows = CY // STRIDE
    lower_count = 2 * GZX
    upper_count = 3 * GZX
    keys = jax.random.split(base, 3)
    lower_scores = jax.random.randint(keys[0], (devices, lower_count), 0, 4096, dtype=jnp.int32) * lower_count
    lower_scores = lower_scores + jnp.arange(lower_count, dtype=jnp.int32)[None, :]
    lower_pick = jnp.argsort(lower_scores, axis=1)[:, :CAP].astype(jnp.int32)
    upper_scores = jax.random.randint(keys[1], (devices, upper_count), 0, 4096, dtype=jnp.int32) * upper_count
    upper_scores = upper_scores + jnp.arange(upper_count, dtype=jnp.int32)[None, :]
    upper_pick = jnp.argsort(upper_scores, axis=1)[:, :WIN_DEV - CAP].astype(jnp.int32) + lower_count
    chosen = jnp.concatenate([lower_pick, upper_pick], axis=1)
    order_scores = jax.random.randint(keys[2], (devices, WIN_DEV), 0, 4096, dtype=jnp.int32) * WIN_DEV
    order_scores = order_scores + jnp.arange(WIN_DEV, dtype=jnp.int32)[None, :]
    order = jnp.argsort(order_scores, axis=1).astype(jnp.int32)
    chosen = jnp.take_along_axis(chosen, order, axis=1)
    device_ids = jnp.arange(devices, dtype=jnp.int32)[:, None]
    nodes = (device_ids * tile_rows * GZX + chosen).reshape(-1)
    field = field_plan(key).reshape(3, -1)
    return (nodes, field[:, nodes])


def draw_windows(key, part):
    return window_plan(key)[0]


def draw_shifts(key, part):
    return window_plan(key)[1]


def lattice(key):
    margin_y = DYM + 1
    margin_z = DZM + 1
    margin_x = DXM + 1
    base = jax.random.fold_in(key, 7919)
    coarse = (GY + 6, GZ + 6, GX + 6)
    level = jax.random.uniform(base, coarse, jnp.float32, 0.0, jnp.log(10.0))
    cells = jnp.exp(level)
    cells = jnp.repeat(jnp.repeat(jnp.repeat(cells, STRIDE, 0), STRIDE, 1), STRIDE, 2)
    cells = cells[3 * STRIDE - margin_y:3 * STRIDE + NY + margin_y, 3 * STRIDE - margin_z:3 * STRIDE + NZ + margin_z, 3 * STRIDE - margin_x:3 * STRIDE + NX + margin_x]
    noise = jax.random.uniform(jax.random.fold_in(key, 1), cells.shape, jnp.float32)
    return (cells * noise, cells)


def draw_first_exposure(key, part):
    margin_y = DYM + 1
    margin_z = DZM + 1
    margin_x = DXM + 1
    field, cells = lattice(key)
    return field[margin_y:margin_y + NY, margin_z:margin_z + NZ, margin_x:margin_x + NX].astype(jnp.bfloat16)


def draw_second_exposure(key, part):
    margin_y = DYM + 1
    margin_z = DZM + 1
    margin_x = DXM + 1
    field, cells = lattice(key)
    whole_shift = field_plan(key)
    residual = jax.random.uniform(jax.random.fold_in(key, 5), (3, GY, GZ, GX), jnp.float32)
    slab_shape = (STRIDE + 2 * margin_y, NZ + 2 * margin_z, NX + 2 * margin_x)

    def one_row(row):
        slab = lax.dynamic_slice(field, (row * STRIDE, 0, 0), slab_shape)
        row_shift = jnp.repeat(jnp.repeat(whole_shift[:, row], STRIDE, 1), STRIDE, 2)
        row_rest = jnp.repeat(jnp.repeat(residual[:, row], STRIDE, 1), STRIDE, 2)
        span_idx = jnp.arange(STRIDE, dtype=jnp.int32)[:, None, None] + margin_y - row_shift[0][None]
        deep_idx = jnp.arange(NZ, dtype=jnp.int32)[None, :, None] + margin_z - row_shift[1][None]
        along_idx = jnp.arange(NX, dtype=jnp.int32)[None, None, :] + margin_x - row_shift[2][None]
        span_idx = jnp.broadcast_to(span_idx, (STRIDE, NZ, NX))
        deep_idx = jnp.broadcast_to(deep_idx, (STRIDE, NZ, NX))
        along_idx = jnp.broadcast_to(along_idx, (STRIDE, NZ, NX))
        rest_y = row_rest[0][None]
        rest_z = row_rest[1][None]
        rest_x = row_rest[2][None]
        total = jnp.zeros((STRIDE, NZ, NX), jnp.float32)
        for corner_y in range(2):
            weight_y = rest_y if corner_y == 0 else 1.0 - rest_y
            for corner_z in range(2):
                weight_z = rest_z if corner_z == 0 else 1.0 - rest_z
                for corner_x in range(2):
                    weight_x = rest_x if corner_x == 0 else 1.0 - rest_x
                    picked = slab[span_idx - 1 + corner_y, deep_idx - 1 + corner_z, along_idx - 1 + corner_x]
                    total = total + weight_y * weight_z * weight_x * picked
        return total
    rows = lax.map(one_row, jnp.arange(GY, dtype=jnp.int32)).reshape(NY, NZ, NX)
    inner_cells = cells[margin_y:margin_y + NY, margin_z:margin_z + NZ, margin_x:margin_x + NX]
    fresh = jax.random.uniform(jax.random.fold_in(key, 3), (NY, NZ, NX), jnp.float32)
    return (0.9 * rows + 0.1 * inner_cells * fresh).astype(jnp.bfloat16)


def setup_inputs(seed: int = 0, part: int = 0) -> dict:
    key_of = jax.random.split(jax.random.key(seed), 5)
    own_keys = jax.random.split(jax.random.fold_in(key_of[4], part), 5)
    first_exposure = draw_first_exposure(jax.random.fold_in(jax.random.fold_in(key_of[4], part), 71), part)
    second_exposure = draw_second_exposure(jax.random.fold_in(jax.random.fold_in(key_of[4], part), 71), part)
    windows = draw_windows(jax.random.fold_in(jax.random.fold_in(key_of[4], part), 71), part)
    shifts = draw_shifts(jax.random.fold_in(jax.random.fold_in(key_of[4], part), 71), part)
    return {"first_exposure": first_exposure, "second_exposure": second_exposure, "windows": windows, "shifts": shifts}


SHARP = 80.0
EPSILON = 1e-06

def window_terms(first_pad, second_pad, node, shift):
    half_width = W // 2
    node_row = node // GZX
    node_rest = node % GZX
    node_deep = node_rest // GX
    node_along = node_rest % GX
    centre_y = STRIDE * node_row + STRIDE // 2
    centre_z = STRIDE * node_deep + STRIDE // 2
    centre_x = STRIDE * node_along + STRIDE // 2
    first_window = lax.dynamic_slice(first_pad, (centre_y, centre_z, centre_x), (W, W, W))
    pad_y = 3 * CY
    pad_z = half_width + 1 + DZM
    pad_x = half_width + 1 + DXM
    start_y = (centre_y + shift[0] - half_width - 1 + pad_y).astype(jnp.int32)
    start_z = (centre_z + shift[1] - half_width - 1 + pad_z).astype(jnp.int32)
    start_x = (centre_x + shift[2] - half_width - 1 + pad_x).astype(jnp.int32)
    second_block = lax.dynamic_slice(second_pad, (start_y, start_z, start_x), (W + 2, W + 2, W + 2))
    first_wide = first_window.astype(jnp.float32)
    first_centred = (first_wide - jnp.mean(first_wide)).astype(jnp.bfloat16)
    second_wide = second_block.astype(jnp.float32)
    second_centred = (second_wide - jnp.mean(second_wide)).astype(jnp.bfloat16)
    first_back = first_centred.astype(jnp.float32)
    second_back = second_centred.astype(jnp.float32)
    energy_first = jnp.mean(first_back * first_back)
    energy_second = jnp.mean(second_back * second_back)
    normaliser = float(W) ** 3 * jnp.sqrt((energy_first + EPSILON) * (energy_second + EPSILON))
    collected = []
    for lag_y in range(3):
        for lag_z in range(3):
            for lag_x in range(3):
                shifted_piece = lax.slice(second_back, (lag_y, lag_z, lag_x), (lag_y + W, lag_z + W, lag_x + W))
                collected.append(jnp.sum(first_back * shifted_piece))
    coherence = jnp.stack(collected).reshape(3, 3, 3) / normaliser
    weights = jnp.exp(SHARP * coherence)
    weight_sum = jnp.sum(weights)
    lag_values = jnp.array([-1.0, 0.0, 1.0], jnp.float32)
    along_y = jnp.sum(weights * lag_values[:, None, None]) / weight_sum
    along_z = jnp.sum(weights * lag_values[None, :, None]) / weight_sum
    along_x = jnp.sum(weights * lag_values[None, None, :]) / weight_sum
    return jnp.stack([along_y, along_z, along_x])

def reference(first_exposure, second_exposure, windows, shifts):
    half_width = W // 2
    first_pad = jnp.pad(first_exposure, half_width)
    pad_z = half_width + 1 + DZM
    pad_x = half_width + 1 + DXM
    second_pad = jnp.pad(second_exposure, ((3 * CY, 3 * CY), (pad_z, pad_z), (pad_x, pad_x)))

    def one_window(window_item):
        return window_terms(first_pad, second_pad, window_item[0], window_item[1])
    corrections = lax.map(one_window, (windows, shifts.T))
    update = jnp.zeros((3, GY * GZX), jnp.float32).at[:, windows].set(corrections.T)
    field_grid = update.reshape(3, GY, GZ, GX)
    padded = jnp.pad(field_grid, ((0, 0), (1, 1), (1, 1), (1, 1)))
    neighbours = padded[:, 2:, 1:-1, 1:-1] + padded[:, :-2, 1:-1, 1:-1]
    neighbours = neighbours + padded[:, 1:-1, 2:, 1:-1] + padded[:, 1:-1, :-2, 1:-1]
    neighbours = neighbours + padded[:, 1:-1, 1:-1, 2:] + padded[:, 1:-1, 1:-1, :-2]
    smoothed = 0.4 * field_grid + 0.1 * neighbours
    return smoothed.reshape(3, GY, GZX)
```

```python
import jax
import jax.numpy as jnp
from jax import lax
from jax.experimental import pallas as pl
from jax.experimental.pallas import tpu as pltpu
from jax.sharding import PartitionSpec as P

W = 48
STRIDE = 12
DYM = 3
GX = 16
GZX = 128
SHARP = 80.0
EPSILON = 1e-06

HALF = W // 2
BLOCK = W + 2
REACH = DYM + 1
LANES = 128
HOP = 64
CHUNK = 6
ROWS_A = 64
ROWS_B = 80
PAD_A = CHUNK
PAD_B = CHUNK + REACH
PIECES = 4
SLOT = 4


def window_of(s, own, win_ref, shift_ref, low_ref, high_ref):
    group = s // own
    idx = s - group * own

    def pick(mine, below, above):
        return jnp.where(group == 0, mine, jnp.where(group == 1, below, above))

    node = pick(win_ref[idx], low_ref[0, idx], high_ref[0, idx])
    dy = pick(shift_ref[0, idx], low_ref[1, idx], high_ref[1, idx])
    dz = pick(shift_ref[1, idx], low_ref[2, idx], high_ref[2, idx])
    dx = pick(shift_ref[2, idx], low_ref[3, idx], high_ref[3, idx])
    return group, node, dy, dz, dx


def correlate_kernel(
    win_ref, shift_ref, low_ref, high_ref, first_hbm, second_hbm, below_hbm, above_hbm,
    out_ref, raw_a, raw_b, fr_a, fr_b, acc, sum_a, sq_a, sum_b, sq_b, sem_a, sem_b, sem_h,
):
    own = win_ref.shape[0]
    planes, deep, along = first_hbm.shape
    tile_rows = planes // STRIDE
    device = lax.axis_index("span")
    last = lax.axis_size("span") - 1
    piece = planes // PIECES

    def copy_a(i):
        return pltpu.make_async_copy(
            first_hbm.at[pl.ds(i * piece, piece)], raw_a.at[pl.ds(i * piece, piece)], sem_a.at[i])

    def copy_b(i):
        return pltpu.make_async_copy(
            second_hbm.at[pl.ds(i * piece, piece)],
            raw_b.at[pl.ds(REACH + i * piece, piece)], sem_b.at[i])

    copy_below = pltpu.make_async_copy(below_hbm, raw_b.at[pl.ds(0, REACH)], sem_h.at[0])
    copy_above = pltpu.make_async_copy(above_hbm, raw_b.at[pl.ds(REACH + planes, REACH)], sem_h.at[1])
    for i in range(PIECES):
        copy_a(i).start()
    copy_below.start()
    for i in range(PIECES):
        copy_b(i).start()
    copy_above.start()

    zero_a = jnp.zeros((2, CHUNK, deep, LANES), jnp.bfloat16)
    fr_a[:, 0:PAD_A] = zero_a
    fr_a[:, PAD_A + planes:] = zero_a
    fr_b[:, 0:CHUNK] = zero_a
    fr_b[:, PAD_B + planes + REACH:] = zero_a
    out_ref[...] = jnp.zeros(out_ref.shape, jnp.float32)

    def frame_a(p, carry):
        v = raw_a[p]
        fr_a[0, p + PAD_A] = v[:, :LANES]
        fr_a[1, p + PAD_A] = v[:, HOP:]
        return carry

    def frame_b(p, carry):
        v = raw_b[p]
        fr_b[0, p + CHUNK] = v[:, :LANES]
        fr_b[1, p + CHUNK] = v[:, HOP:]
        return carry

    for i in range(PIECES):
        copy_a(i).wait()
        lax.fori_loop(i * piece, (i + 1) * piece, frame_a, 0)
    copy_below.wait()
    lax.fori_loop(0, REACH, frame_b, 0)
    for i in range(PIECES):
        copy_b(i).wait()
        lax.fori_loop(REACH + i * piece, REACH + (i + 1) * piece, frame_b, 0)
    copy_above.wait()
    lax.fori_loop(REACH + planes, 2 * REACH + planes, frame_b, 0)

    def slot(s, carry):
        group, node, dy, dz, dx = window_of(s, own, win_ref, shift_ref, low_ref, high_ref)
        row = node // GZX - device * tile_rows
        rest = node % GZX
        cy = STRIDE * row + STRIDE // 2
        cz = STRIDE * (rest // GX) + STRIDE // 2
        cx = STRIDE * (rest % GX) + STRIDE // 2
        start = jnp.maximum(cy - HALF, jnp.where(device == 0, -CHUNK, 0))
        stop = jnp.minimum(cy + HALF, jnp.where(device == last, planes + CHUNK, planes))
        wanted = (
            (group == 0)
            | ((group == 1) & (row < 0) & (row >= -tile_rows))
            | ((group == 2) & (row >= tile_rows) & (row < 2 * tile_rows))
        )
        count = jnp.where(wanted, jnp.maximum(stop - start, 0) // CHUNK, 0)

        @pl.when(count > 0)
        def _():
            z_a = pl.multiple_of(jnp.clip((cz - HALF) // 16 * 16, 0, deep - ROWS_A), 16)
            sz = cz + dz - HALF - 1
            z_b = pl.multiple_of(jnp.where(sz + BLOCK <= ROWS_B, 0, deep - ROWS_B), 16)
            sx = cx + dx - HALF - 1
            f_a = jnp.where(cx + HALF <= LANES, 0, 1)
            f_b = jnp.where(sx + BLOCK <= LANES, 0, 1)
            lane16 = lax.broadcasted_iota(jnp.int32, (16, LANES), 1)
            row16 = lax.broadcasted_iota(jnp.int32, (16, LANES), 0)
            source = lane16 + HOP * f_b - dx
            turns = []
            masks = []
            for lag in range(3):
                turns.append((dx + lag - 1 + HOP * (f_a - f_b) + 2 * LANES) % LANES)
                at = source - (lag - 1)
                inside = (at >= cx - HALF) & (at < cx + HALF) & (at >= 0) & (at < along)
                tile = jnp.where(inside, 1.0, 0.0).astype(jnp.bfloat16)
                masks.append(jnp.concatenate([tile] * (ROWS_A // 16), axis=0))
            at = source - (row16 - 1)
            inside = (at >= cx - HALF) & (at < cx + HALF) & (row16 < 3)
            ones = jnp.where(inside, 1.0, 0.0).astype(jnp.bfloat16)
            ones = jnp.concatenate([ones] * CHUNK, axis=1)

            acc[...] = jnp.zeros(acc.shape, jnp.float32)
            sum_a[...] = jnp.zeros(sum_a.shape, jnp.float32)
            sq_a[...] = jnp.zeros(sq_a.shape, jnp.float32)
            sum_b[...] = jnp.zeros(sum_b.shape, jnp.float32)
            sq_b[...] = jnp.zeros(sq_b.shape, jnp.float32)

            def chunk(c, inner):
                y = start + c * CHUNK
                a = [fr_a[f_a, y + PAD_A + p, pl.ds(z_a, ROWS_A), :] for p in range(CHUNK)]
                b = [
                    fr_b[f_b, y + dy - 1 + PAD_B + p, pl.ds(z_b, ROWS_B), :]
                    for p in range(CHUNK + 2)
                ]
                left = [
                    jnp.concatenate(
                        [pltpu.roll(v, turns[lag], 1) * masks[lag] for v in a], axis=1)
                    for lag in range(3)
                ]
                left = jnp.concatenate(left + [ones], axis=0)
                right = jnp.concatenate(
                    [jnp.concatenate(b[lag:lag + CHUNK], axis=1) for lag in range(3)], axis=0)
                acc[...] += lax.dot_general(
                    left, right, (((1,), (1,)), ((), ())), preferred_element_type=jnp.float32)
                wide = [v.astype(jnp.float32) for v in a]
                sum_a[...] += sum(wide)
                sq_a[...] += sum([v * v for v in wide])
                wide = [v.astype(jnp.float32) for v in b[1:-1]]
                sum_b[...] += sum(wide)
                sq_b[...] += sum([v * v for v in wide])
                return inner

            lax.fori_loop(0, count, chunk, 0)

            for has, at in (
                (start == cy - HALF, start + dy - 1 + PAD_B),
                (stop == cy + HALF, stop + dy + PAD_B),
            ):
                @pl.when(has)
                def _():
                    v = fr_b[f_b, at, pl.ds(z_b, ROWS_B), :].astype(jnp.float32)
                    sum_b[...] += v
                    sq_b[...] += v * v

            cols = 3 * ROWS_B
            col = lax.broadcasted_iota(jnp.int32, (ROWS_A, cols), 1)
            z_row = lax.broadcasted_iota(jnp.int32, (ROWS_A, cols), 0) + z_a
            col_lag = jnp.where(col >= ROWS_B, 1, 0) + jnp.where(col >= 2 * ROWS_B, 1, 0)
            z_col = col - col_lag * ROWS_B + z_b
            z_in = (z_row >= cz - HALF) & (z_row < cz + HALF)
            gap = jnp.where(z_in, z_col - z_row - dz, 99)
            z_one = z_col[0:3] - dz
            tops = []
            lows = []
            for lag_z in range(3):
                hit = gap == lag_z - 1
                for lag_x in range(3):
                    tops.append(jnp.sum(
                        jnp.where(hit, acc[lag_x * ROWS_A:(lag_x + 1) * ROWS_A, :], 0.0),
                        axis=0, keepdims=True))
                at = z_one - (lag_z - 1)
                hit = (at >= cz - HALF) & (at < cz + HALF)
                lows.append(jnp.where(hit, acc[3 * ROWS_A:3 * ROWS_A + 3, :], 0.0))
            stack = jnp.concatenate(tops + lows, axis=0)

            lane = lax.broadcasted_iota(jnp.int32, (ROWS_A, LANES), 1) + HOP * f_a
            deep_at = lax.broadcasted_iota(jnp.int32, (ROWS_A, LANES), 0) + z_a
            hit_a = (
                (lane >= cx - HALF) & (lane < cx + HALF)
                & (deep_at >= cz - HALF) & (deep_at < cz + HALF)
            )
            lane = lax.broadcasted_iota(jnp.int32, (ROWS_B, LANES), 1) + HOP * f_b
            deep_at = lax.broadcasted_iota(jnp.int32, (ROWS_B, LANES), 0) + z_b
            hit_b = (
                (lane >= sx) & (lane < sx + BLOCK) & (deep_at >= sz) & (deep_at < sz + BLOCK)
            )
            sums = [
                jnp.sum(jnp.where(hit, ref[...], 0.0), axis=0, keepdims=True)
                for hit, ref in ((hit_a, sum_a), (hit_a, sq_a), (hit_b, sum_b), (hit_b, sq_b))
            ]
            sums = jnp.sum(jnp.concatenate(sums, axis=0), axis=1, keepdims=True)
            lag_18 = col_lag[0:18]
            out_lane = lax.broadcasted_iota(jnp.int32, (18, LANES), 1) - SLOT * s
            total = jnp.zeros((18, LANES), jnp.float32)
            for lag_y in range(3):
                part = jnp.sum(jnp.where(lag_18 == lag_y, stack, 0.0), axis=1, keepdims=True)
                total = total + jnp.where(out_lane == lag_y, part, 0.0)
            out_ref[0:18] += total
            out_ref[18:22] += jnp.where(out_lane[0:4] == 0, sums, 0.0)

        return carry

    lax.fori_loop(0, 3 * own, slot, 0)


def update_kernel(win_ref, low_ref, high_ref, mine_ref, below_ref, above_ref, out_ref):
    own = win_ref.shape[0]
    tile_rows = out_ref.shape[1]
    device = lax.axis_index("span")
    span = SLOT * own
    mine = mine_ref[...]
    below = below_ref[...]
    above = above_ref[...]
    lane = lax.broadcasted_iota(jnp.int32, mine.shape, 1)
    total = mine
    total = total + jnp.where(
        lane < span,
        pltpu.roll(below, LANES - 2 * span, 1) + pltpu.roll(above, LANES - span, 1),
        jnp.where(
            lane < 2 * span, pltpu.roll(below, span, 1),
            jnp.where(lane < 3 * span, pltpu.roll(above, 2 * span, 1), 0.0)))

    def lead(v):
        return v + pltpu.roll(v, LANES - 1, 1) + pltpu.roll(v, LANES - 2, 1)

    def spread(v):
        return v + pltpu.roll(v, 1, 1) + pltpu.roll(v, 2, 1)

    lag_lane = lane % SLOT
    stats = spread(jnp.where(lag_lane[0:4] == 0, total[18:22], 0.0))
    voxels = float(W) ** 3
    block_voxels = float(BLOCK) ** 3
    mean_a = stats[0:1] / voxels
    energy_a = jnp.maximum(stats[1:2] / voxels - mean_a * mean_a, 0.0)
    mean_b = stats[2:3] / block_voxels
    energy_b = jnp.maximum(stats[3:4] / block_voxels - mean_b * mean_b, 0.0)
    normaliser = voxels * jnp.sqrt((energy_a + EPSILON) * (energy_b + EPSILON))
    scaled = SHARP * ((total[0:9] - mean_a * total[9:18]) / normaliser)
    used = lag_lane[0:9] < 3
    scaled = jnp.where(used, scaled, -1e30)
    top = jnp.max(scaled, axis=0, keepdims=True)
    top = jnp.maximum(top, jnp.maximum(pltpu.roll(top, LANES - 1, 1), pltpu.roll(top, LANES - 2, 1)))
    top = spread(jnp.where(lag_lane[0:1] == 0, top, 0.0))
    weights = jnp.where(used, jnp.exp(scaled - top), 0.0)
    lag_row = lax.broadcasted_iota(jnp.int32, weights.shape, 0)
    lag_z = (lag_row // 3 - 1).astype(jnp.float32)
    lag_x = (lag_row % 3 - 1).astype(jnp.float32)
    column = jnp.sum(weights, axis=0, keepdims=True)
    weight_sum = lead(column)
    along_y = lead(column * (lag_lane[0:1] - 1).astype(jnp.float32)) / weight_sum
    along_z = lead(jnp.sum(weights * lag_z, axis=0, keepdims=True)) / weight_sum
    along_x = lead(jnp.sum(weights * lag_x, axis=0, keepdims=True)) / weight_sum
    corrections = (along_y, along_z, along_x)

    grid_row = lax.broadcasted_iota(jnp.int32, (8, LANES), 0) - 1
    grid_lane = lax.broadcasted_iota(jnp.int32, (8, LANES), 1)
    fields = [jnp.zeros((8, LANES), jnp.float32) for _ in range(3)]
    for s in range(3 * own):
        ref = win_ref if s < own else (low_ref if s < 2 * own else high_ref)
        node = ref[s] if s < own else ref[0, s % own]
        row = node // GZX - device * tile_rows
        if s >= 2 * own:
            row = jnp.where(row == tile_rows, row, -9)
        elif s >= own:
            row = jnp.where(row == -1, row, -9)
        hit = (grid_row == row) & (grid_lane == node % GZX)
        for comp in range(3):
            fields[comp] = jnp.where(
                hit, corrections[comp][:, SLOT * s:SLOT * s + 1], fields[comp])
    lane_z = grid_lane // GX
    lane_x = grid_lane % GX
    for comp in range(3):
        field = fields[comp]
        near = jnp.where(lane_z >= 1, pltpu.roll(field, GX, 1), 0.0)
        near = near + jnp.where(lane_z < GZX // GX - 1, pltpu.roll(field, LANES - GX, 1), 0.0)
        near = near + jnp.where(lane_x >= 1, pltpu.roll(field, 1, 1), 0.0)
        near = near + jnp.where(lane_x < GX - 1, pltpu.roll(field, LANES - 1, 1), 0.0)
        near = near[1:1 + tile_rows] + field[0:tile_rows] + field[2:2 + tile_rows]
        out_ref[comp] = 0.4 * field[1:1 + tile_rows] + 0.1 * near


def shards(first, second, windows, shifts):
    planes, deep, along = first.shape
    own = windows.shape[0]
    count = lax.axis_size("span")
    upward = [(i, i + 1) for i in range(count - 1)]
    downward = [(i + 1, i) for i in range(count - 1)]
    plan = jnp.concatenate([windows[None], shifts], axis=0)
    low_plan = lax.ppermute(plan, "span", upward)
    high_plan = lax.ppermute(plan, "span", downward)
    below = lax.ppermute(second[planes - REACH:], "span", upward)
    above = lax.ppermute(second[:REACH], "span", downward)
    smem = pl.BlockSpec(memory_space=pltpu.SMEM)
    vmem = pl.BlockSpec(memory_space=pltpu.VMEM)
    hbm = pl.BlockSpec(memory_space=pl.ANY)
    sums = pl.pallas_call(
        correlate_kernel,
        out_shape=jax.ShapeDtypeStruct((24, LANES), jnp.float32),
        in_specs=[smem] * 4 + [hbm] * 4,
        out_specs=vmem,
        scratch_shapes=[
            pltpu.VMEM((planes, deep, along), jnp.bfloat16),
            pltpu.VMEM((planes + 2 * REACH, deep, along), jnp.bfloat16),
            pltpu.VMEM((2, planes + 2 * PAD_A, deep, LANES), jnp.bfloat16),
            pltpu.VMEM((2, planes + 2 * PAD_B, deep, LANES), jnp.bfloat16),
            pltpu.VMEM((3 * ROWS_A + 16, 3 * ROWS_B), jnp.float32),
            pltpu.VMEM((ROWS_A, LANES), jnp.float32),
            pltpu.VMEM((ROWS_A, LANES), jnp.float32),
            pltpu.VMEM((ROWS_B, LANES), jnp.float32),
            pltpu.VMEM((ROWS_B, LANES), jnp.float32),
            pltpu.SemaphoreType.DMA((PIECES,)),
            pltpu.SemaphoreType.DMA((PIECES,)),
            pltpu.SemaphoreType.DMA((2,)),
        ],
        compiler_params=pltpu.CompilerParams(vmem_limit_bytes=48 << 20),
        name="partial_sums",
    )(windows, shifts, low_plan, high_plan, first, second, below, above)
    below_sums = lax.ppermute(sums, "span", upward)
    above_sums = lax.ppermute(sums, "span", downward)
    return pl.pallas_call(
        update_kernel,
        out_shape=jax.ShapeDtypeStruct((3, planes // STRIDE, GZX), jnp.float32),
        in_specs=[smem] * 3 + [vmem] * 3,
        out_specs=vmem,
        name="smoothed_update",
    )(windows, low_plan, high_plan, sums, below_sums, above_sums)


def solution(mesh):
    in_specs = (
        P(("grp", "span"), None, None),
        P(("grp", "span"), None, None),
        P(("grp", "span")),
        P(None, ("grp", "span")),
    )
    out_specs = P(None, ("grp", "span"), None)
    return jax.shard_map(shards, mesh=mesh, in_specs=in_specs, out_specs=out_specs, check_vma=False)
```

```python
import functools

import jax
import jax.numpy as jnp
from jax import lax
from jax.experimental import pallas as pl
from jax.experimental.pallas import tpu as pltpu
from jax.sharding import PartitionSpec as P

W = 48
STRIDE = 12
DYM = 3
GX = 16
GZX = 128
SHARP = 80.0
EPSILON = 1e-06

HALF = W // 2
BLOCK = W + 2
REACH = DYM + 1
LANES = 128
HOP = 64
CHUNK = 6
ROWS_A = 64
ROWS_B = 80
PAD_A = CHUNK
PAD_B = CHUNK + REACH
PIECES = 4
SLOT = 4
PLAN_ROWS = 16
FIELDS = 16
PAIR = 2


def send_kernel(win_ref, shift_ref, second_hbm, pair_ref, other_ref, sems):
    planes = second_hbm.shape[0]
    even = lax.axis_index("span") % 2 == 0
    top = planes - REACH

    def fetch(start, target, i):
        return pltpu.make_async_copy(
            second_hbm.at[pl.ds(start, REACH)], target.at[pl.ds(0, REACH)], sems.at[i])

    to_pair = fetch(jnp.where(even, top, 0), pair_ref, 0)
    to_other = fetch(jnp.where(even, 0, top), other_ref, 1)
    to_pair.start()
    to_other.start()
    node = win_ref[...]
    rows = jnp.concatenate([node // 256, node % 256, shift_ref[...]], axis=0)
    rows = rows.astype(jnp.float32).astype(jnp.bfloat16)
    for ref in (pair_ref, other_ref):
        ref[REACH, 0:PLAN_ROWS, :] = jnp.zeros((PLAN_ROWS, ref.shape[2]), jnp.bfloat16)
        ref[REACH, 0:rows.shape[0], 0:node.shape[1]] = rows
    to_pair.wait()
    to_other.wait()


def correlate_kernel(
    win_ref, shift_ref, first_hbm, second_hbm, pair_hbm, other_hbm,
    out_ref, raw_a, raw_b, fr_a, fr_b, acc, sum_a, sq_a, sum_b, sq_b, masks, plan_in, plan_int,
    plan, table, units, sem_a, sem_b, sem_h, sem_p,
):
    own = win_ref.shape[0]
    planes, deep, along = first_hbm.shape
    tile_rows = planes // STRIDE
    device = lax.axis_index("span")
    last = lax.axis_size("span") - 1
    even = device % 2 == 0
    piece = planes // PIECES

    def copy_a(i):
        return pltpu.make_async_copy(
            first_hbm.at[pl.ds(i * piece, piece)], raw_a.at[pl.ds(i * piece, piece)], sem_a.at[i])

    def copy_b(i):
        return pltpu.make_async_copy(
            second_hbm.at[pl.ds(i * piece, piece)],
            raw_b.at[pl.ds(REACH + i * piece, piece)], sem_b.at[i])

    low_at, high_at = 0, REACH + planes
    pair_at = jnp.where(even, high_at, low_at)
    other_at = jnp.where(even, low_at, high_at)
    pair_side = jnp.where(even, 1, 0)
    halo = [
        pltpu.make_async_copy(
            ref.at[pl.ds(0, REACH)], raw_b.at[pl.ds(at, REACH)], sem_h.at[i])
        for i, (ref, at) in enumerate(((pair_hbm, pair_at), (other_hbm, other_at)))
    ]
    plans = [
        pltpu.make_async_copy(
            ref.at[REACH, pl.ds(0, PLAN_ROWS)], plan_in.at[side], sem_p.at[i])
        for i, (ref, side) in enumerate(((pair_hbm, pair_side), (other_hbm, 1 - pair_side)))
    ]
    for c in plans:
        c.start()
    for i in range(PIECES):
        copy_a(i).start()
    for i in range(PIECES):
        copy_b(i).start()
    for c in halo:
        c.start()
    for c in plans:
        c.wait()
    plan_int[...] = plan_in[:, 0:8, 0:LANES].astype(jnp.float32).astype(jnp.int32)
    to_scalar = pltpu.make_async_copy(plan_int, plan, sem_p.at[2])
    to_scalar.start()

    @pl.when((device == 0) | (device == last))
    def _():
        zero = jnp.zeros((2, CHUNK, deep, LANES), jnp.bfloat16)
        fr_a[:, 0:PAD_A] = zero
        fr_a[:, PAD_A + planes:] = zero
        fr_b[:, 0:CHUNK] = zero
        fr_b[:, PAD_B + planes + REACH:] = zero

    out_ref[...] = jnp.zeros(out_ref.shape, jnp.float32)
    to_scalar.wait()

    def prepare(s, total):
        group = s // own
        idx = s - group * own
        side = jnp.maximum(group - 1, 0)
        mine = group == 0

        def pick(own_value, row):
            return jnp.where(mine, own_value, plan[side, row, idx])

        node = jnp.where(mine, win_ref[idx], plan[side, 0, idx] * 256 + plan[side, 1, idx])
        dy = pick(shift_ref[0, idx], 2)
        dz = pick(shift_ref[1, idx], 3)
        dx = pick(shift_ref[2, idx], 4)
        row = node // GZX - device * tile_rows
        rest = node % GZX
        cy = STRIDE * row + STRIDE // 2
        cz = STRIDE * (rest // GX) + STRIDE // 2
        cx = STRIDE * (rest % GX) + STRIDE // 2
        start = jnp.maximum(cy - HALF, jnp.where(device == 0, -CHUNK, 0))
        stop = jnp.minimum(cy + HALF, jnp.where(device == last, planes + CHUNK, planes))
        wanted = (
            mine
            | ((group == 1) & (row < 0) & (row >= -tile_rows))
            | ((group == 2) & (row >= tile_rows) & (row < 2 * tile_rows))
        )
        count = jnp.where(wanted, jnp.maximum(stop - start, 0) // CHUNK, 0)
        target = jnp.where(
            mine | ((group == 1) & (row == -1)) | ((group == 2) & (row == tile_rows)),
            (row + 1) * GZX + rest, -1)
        lane_out = lax.broadcasted_iota(jnp.int32, (1, LANES), 1)
        out_ref[22:23, :] = jnp.where(
            lane_out == SLOT * s, target.astype(jnp.float32), out_ref[22:23, :])
        table[s, 0] = count

        @pl.when(count > 0)
        def _():
            z_a = jnp.clip((cz - HALF) // 16 * 16, 0, deep - ROWS_A)
            sz = cz + dz - HALF - 1
            z_b = jnp.where(sz + BLOCK <= ROWS_B, 0, deep - ROWS_B)
            sx = cx + dx - HALF - 1
            f_a = jnp.where(cx + HALF <= LANES, 0, 1)
            f_b = jnp.where(sx + BLOCK <= LANES, 0, 1)
            for at, value in enumerate((f_a, z_a, f_b, z_b, dy, dz, dx, cy, cz, cx, start, stop)):
                table[s, at + 1] = value
            lane16 = lax.broadcasted_iota(jnp.int32, (16, LANES), 1)
            row16 = lax.broadcasted_iota(jnp.int32, (16, LANES), 0)
            source = lane16 + jnp.where(lane16 < HOP, LANES * f_b, 0) - dx
            for lag in range(3):
                at = source - (lag - 1)
                inside = (at >= cx - HALF) & (at < cx + HALF) & (at >= 0) & (at < along)
                masks[s, lag] = jnp.where(inside, 1.0, 0.0).astype(jnp.bfloat16)
            at = source - (row16 - 1)
            inside = (at >= cx - HALF) & (at < cx + HALF) & (row16 < 3)
            masks[s, 3] = jnp.where(inside, 1.0, 0.0).astype(jnp.bfloat16)
            for ref in (acc, sum_a, sq_a, sum_b, sq_b):
                ref[s] = jnp.zeros(ref.shape[1:], jnp.float32)

            def unit(c, at):
                units[0, at] = s
                units[1, at] = start + c * CHUNK
                return at + 1

            lax.fori_loop(0, count, unit, total)

        return total + count

    total = lax.fori_loop(0, 3 * own, prepare, 0)
    spare = 3 * own
    for at in range(FIELDS):
        table[spare, at] = 0
    for at in range(PAIR - 1):
        units[0, total + at] = spare
        units[1, total + at] = 0

    def frame(raw, fr, shift):
        def body(p, carry):
            v = raw[p]
            fr[0, p + shift] = v[:, :LANES]
            fr[1, p + shift] = jnp.concatenate([v[:, LANES:], v[:, HOP:LANES]], axis=1)
            return carry
        return body

    frame_a = frame(raw_a, fr_a, PAD_A)
    frame_b = frame(raw_b, fr_b, CHUNK)
    for i in range(PIECES):
        copy_a(i).wait()
        lax.fori_loop(i * piece, (i + 1) * piece, frame_a, 0, unroll=5)
    for i in range(PIECES):
        copy_b(i).wait()
        lax.fori_loop(REACH + i * piece, REACH + (i + 1) * piece, frame_b, 0, unroll=5)
    for c in halo:
        c.wait()
    lax.fori_loop(0, REACH, frame_b, 0, unroll=4)
    lax.fori_loop(REACH + planes, 2 * REACH + planes, frame_b, 0, unroll=4)

    def step(t, carry):
        for h in range(PAIR):
            s = units[0, PAIR * t + h]
            y = units[1, PAIR * t + h]
            f_a = table[s, 1]
            z_a = pl.multiple_of(table[s, 2], 16)
            f_b = table[s, 3]
            z_b = pl.multiple_of(table[s, 4], 16)
            dy = table[s, 5]
            dx = table[s, 7]
            a = [fr_a[f_a, y + PAD_A + p, pl.ds(z_a, ROWS_A), :] for p in range(CHUNK)]
            b = [
                fr_b[f_b, y + dy - 1 + PAD_B + p, pl.ds(z_b, ROWS_B), :]
                for p in range(CHUNK + 2)
            ]
            left = []
            for lag in range(3):
                mask = jnp.concatenate([masks[s, lag]] * (ROWS_A // 16), axis=0)
                turn = (dx + lag - 1 + LANES) % LANES
                left.append(jnp.concatenate(
                    [pltpu.roll(v, turn, 1) * mask for v in a], axis=1))
            left.append(jnp.concatenate([masks[s, 3]] * CHUNK, axis=1))
            left = jnp.concatenate(left, axis=0)
            right = jnp.concatenate(
                [jnp.concatenate(b[lag:lag + CHUNK], axis=1) for lag in range(3)], axis=0)
            acc[s] += lax.dot_general(
                left, right, (((1,), (1,)), ((), ())), preferred_element_type=jnp.float32)
            wide = [v.astype(jnp.float32) for v in a]
            sum_a[s] += sum(wide)
            sq_a[s] += sum([v * v for v in wide])
            wide = [v.astype(jnp.float32) for v in b[1:-1]]
            sum_b[s] += sum(wide)
            sq_b[s] += sum([v * v for v in wide])
        return carry

    lax.fori_loop(0, (total + PAIR - 1) // PAIR, step, 0)

    def finish(s, carry):
        @pl.when(table[s, 0] > 0)
        def _():
            f_a, z_a, f_b, z_b, dy, dz, dx, cy, cz, cx, start, stop = [
                table[s, at + 1] for at in range(12)]
            z_b = pl.multiple_of(z_b, 16)
            sz = cz + dz - HALF - 1
            sx = cx + dx - HALF - 1
            for has, at in (
                (start == cy - HALF, start + dy - 1 + PAD_B),
                (stop == cy + HALF, stop + dy + PAD_B),
            ):
                @pl.when(has)
                def _():
                    v = fr_b[f_b, at, pl.ds(z_b, ROWS_B), :].astype(jnp.float32)
                    sum_b[s] += v
                    sq_b[s] += v * v

            cols = 3 * ROWS_B
            col = lax.broadcasted_iota(jnp.int32, (ROWS_A, cols), 1)
            z_row = lax.broadcasted_iota(jnp.int32, (ROWS_A, cols), 0) + z_a
            col_lag = jnp.where(col >= ROWS_B, 1, 0) + jnp.where(col >= 2 * ROWS_B, 1, 0)
            z_col = col - col_lag * ROWS_B + z_b
            z_in = (z_row >= cz - HALF) & (z_row < cz + HALF)
            gap = jnp.where(z_in, z_col - z_row - dz, 99)
            z_one = z_col[0:3] - dz
            tops = []
            lows = []
            for lag_z in range(3):
                hit = gap == lag_z - 1
                for lag_x in range(3):
                    tops.append(jnp.sum(
                        jnp.where(hit, acc[s, lag_x * ROWS_A:(lag_x + 1) * ROWS_A, :], 0.0),
                        axis=0, keepdims=True))
                at = z_one - (lag_z - 1)
                hit = (at >= cz - HALF) & (at < cz + HALF)
                lows.append(jnp.where(hit, acc[s, 3 * ROWS_A:3 * ROWS_A + 3, :], 0.0))
            stack = jnp.concatenate(tops + lows, axis=0)

            def inside(rows, frame_at, x_from, x_count, z_at, z_from, z_count):
                lane = lax.broadcasted_iota(jnp.int32, (rows, LANES), 1)
                lane = lane + jnp.where(lane < HOP, LANES * frame_at, 0)
                z = lax.broadcasted_iota(jnp.int32, (rows, LANES), 0) + z_at
                return (
                    (lane >= x_from) & (lane < x_from + x_count)
                    & (z >= z_from) & (z < z_from + z_count)
                )

            hit_a = inside(ROWS_A, f_a, cx - HALF, W, z_a, cz - HALF, W)
            hit_b = inside(ROWS_B, f_b, sx, BLOCK, z_b, sz, BLOCK)
            sums = [
                jnp.sum(jnp.where(hit, ref[s], 0.0), axis=0, keepdims=True)
                for hit, ref in ((hit_a, sum_a), (hit_a, sq_a), (hit_b, sum_b), (hit_b, sq_b))
            ]
            sums = jnp.sum(jnp.concatenate(sums, axis=0), axis=1, keepdims=True)
            lag_18 = col_lag[0:18]
            out_lane = lax.broadcasted_iota(jnp.int32, (18, LANES), 1) - SLOT * s
            total = jnp.zeros((18, LANES), jnp.float32)
            for lag_y in range(3):
                part = jnp.sum(jnp.where(lag_18 == lag_y, stack, 0.0), axis=1, keepdims=True)
                total = total + jnp.where(out_lane == lag_y, part, 0.0)
            out_ref[0:18] += total
            out_ref[18:22] += jnp.where(out_lane[0:4] == 0, sums, 0.0)

        return carry

    lax.fori_loop(0, 3 * own, finish, 0)


def update_kernel(own, mine_ref, pair_ref, other_ref, out_ref):
    tile_rows = out_ref.shape[0]
    even = lax.axis_index("span") % 2 == 0
    mine = mine_ref[...]
    pair = pair_ref[...]
    other = other_ref[...]
    below = jnp.where(even, other, pair)
    above = jnp.where(even, pair, other)
    span = SLOT * own
    lane = lax.broadcasted_iota(jnp.int32, mine.shape, 1)
    total = mine
    total = total + jnp.where(
        lane < span,
        pltpu.roll(below, LANES - 2 * span, 1) + pltpu.roll(above, LANES - span, 1),
        jnp.where(
            lane < 2 * span, pltpu.roll(below, span, 1),
            jnp.where(lane < 3 * span, pltpu.roll(above, 2 * span, 1), 0.0)))

    def lead(v):
        return v + pltpu.roll(v, LANES - 1, 1) + pltpu.roll(v, LANES - 2, 1)

    def spread(v):
        return v + pltpu.roll(v, 1, 1) + pltpu.roll(v, 2, 1)

    lag_lane = lane % SLOT
    stats = spread(jnp.where(lag_lane[0:4] == 0, total[18:22], 0.0))
    voxels = float(W) ** 3
    block_voxels = float(BLOCK) ** 3
    mean_a = stats[0:1] / voxels
    energy_a = jnp.maximum(stats[1:2] / voxels - mean_a * mean_a, 0.0)
    mean_b = stats[2:3] / block_voxels
    energy_b = jnp.maximum(stats[3:4] / block_voxels - mean_b * mean_b, 0.0)
    normaliser = voxels * jnp.sqrt((energy_a + EPSILON) * (energy_b + EPSILON))
    scaled = SHARP * ((total[0:9] - mean_a * total[9:18]) / normaliser)
    used = lag_lane[0:9] < 3
    scaled = jnp.where(used, scaled, -1e30)
    top = jnp.max(scaled, axis=0, keepdims=True)
    top = jnp.maximum(top, jnp.maximum(pltpu.roll(top, LANES - 1, 1), pltpu.roll(top, LANES - 2, 1)))
    top = spread(jnp.where(lag_lane[0:1] == 0, top, 0.0))
    weights = jnp.where(used, jnp.exp(scaled - top), 0.0)
    lag_row = lax.broadcasted_iota(jnp.int32, weights.shape, 0)
    lag_z = (lag_row // 3 - 1).astype(jnp.float32)
    lag_x = (lag_row % 3 - 1).astype(jnp.float32)
    column = jnp.sum(weights, axis=0, keepdims=True)
    weight_sum = lead(column)
    along_y = lead(column * (lag_lane[0:1] - 1).astype(jnp.float32)) / weight_sum
    along_z = lead(jnp.sum(weights * lag_z, axis=0, keepdims=True)) / weight_sum
    along_x = lead(jnp.sum(weights * lag_x, axis=0, keepdims=True)) / weight_sum
    corrections = (along_y, along_z, along_x)

    grid_lane = lax.broadcasted_iota(jnp.int32, (8, LANES), 1)
    place = lax.broadcasted_iota(jnp.int32, (8, LANES), 0) * GZX + grid_lane
    target = mine[22:23].astype(jnp.int32)
    fields = [jnp.zeros((8, LANES), jnp.float32) for _ in range(3)]
    for s in range(3 * own):
        hit = place == target[:, SLOT * s:SLOT * s + 1]
        for comp in range(3):
            fields[comp] = jnp.where(
                hit, corrections[comp][:, SLOT * s:SLOT * s + 1], fields[comp])
    lane_z = grid_lane // GX
    lane_x = grid_lane % GX
    for comp in range(3):
        field = fields[comp]
        near = jnp.where(lane_z >= 1, pltpu.roll(field, GX, 1), 0.0)
        near = near + jnp.where(lane_z < GZX // GX - 1, pltpu.roll(field, LANES - GX, 1), 0.0)
        near = near + jnp.where(lane_x >= 1, pltpu.roll(field, 1, 1), 0.0)
        near = near + jnp.where(lane_x < GX - 1, pltpu.roll(field, LANES - 1, 1), 0.0)
        near = near[1:1 + tile_rows] + field[0:tile_rows] + field[2:2 + tile_rows]
        out_ref[:, comp, :] = 0.4 * field[1:1 + tile_rows] + 0.1 * near


def shards(first, second, windows, shifts):
    planes, deep, along = first.shape
    own = windows.shape[0]
    count = lax.axis_size("span")
    pairs = [(i, i ^ 1) for i in range(count)]
    others = [(i, i + 1) for i in range(1, count - 1, 2)]
    others = others + [(b, a) for a, b in others]
    smem = pl.BlockSpec(memory_space=pltpu.SMEM)
    vmem = pl.BlockSpec(memory_space=pltpu.VMEM)
    hbm = pl.BlockSpec(memory_space=pl.ANY)
    message = jax.ShapeDtypeStruct((REACH + 1, deep, along), second.dtype)
    to_pair, to_other = pl.pallas_call(
        send_kernel,
        out_shape=(message, message),
        in_specs=[vmem, vmem, hbm],
        out_specs=(vmem, vmem),
        scratch_shapes=[pltpu.SemaphoreType.DMA((2,))],
        name="planes_to_send",
    )(windows[None], shifts, second)
    to_other = lax.ppermute(to_other, "span", others)
    to_pair = lax.ppermute(to_pair, "span", pairs)
    sums = pl.pallas_call(
        correlate_kernel,
        out_shape=jax.ShapeDtypeStruct((24, LANES), jnp.float32),
        in_specs=[smem] * 2 + [hbm] * 4,
        out_specs=vmem,
        scratch_shapes=[
            pltpu.VMEM((planes, deep, along), jnp.bfloat16),
            pltpu.VMEM((planes + 2 * REACH, deep, along), jnp.bfloat16),
            pltpu.VMEM((2, planes + 2 * PAD_A, deep, LANES), jnp.bfloat16),
            pltpu.VMEM((2, planes + 2 * PAD_B, deep, LANES), jnp.bfloat16),
            pltpu.VMEM((3 * own + 1, 3 * ROWS_A + 16, 3 * ROWS_B), jnp.float32),
            pltpu.VMEM((3 * own + 1, ROWS_A, LANES), jnp.float32),
            pltpu.VMEM((3 * own + 1, ROWS_A, LANES), jnp.float32),
            pltpu.VMEM((3 * own + 1, ROWS_B, LANES), jnp.float32),
            pltpu.VMEM((3 * own + 1, ROWS_B, LANES), jnp.float32),
            pltpu.VMEM((3 * own + 1, 4, 16, LANES), jnp.bfloat16),
            pltpu.VMEM((2, PLAN_ROWS, along), jnp.bfloat16),
            pltpu.VMEM((2, 8, LANES), jnp.int32),
            pltpu.SMEM((2, 8, LANES), jnp.int32),
            pltpu.SMEM((3 * own + 1, FIELDS), jnp.int32),
            pltpu.SMEM((2, 3 * own * (W // CHUNK + 1) + PAIR), jnp.int32),
            pltpu.SemaphoreType.DMA((PIECES,)),
            pltpu.SemaphoreType.DMA((PIECES,)),
            pltpu.SemaphoreType.DMA((2,)),
            pltpu.SemaphoreType.DMA((3,)),
        ],
        compiler_params=pltpu.CompilerParams(vmem_limit_bytes=60 << 20),
        name="partial_sums",
    )(windows, shifts, first, second, to_pair, to_other)
    other_sums = lax.ppermute(sums, "span", others)
    pair_sums = lax.ppermute(sums, "span", pairs)
    field = pl.pallas_call(
        functools.partial(update_kernel, own),
        out_shape=jax.ShapeDtypeStruct((planes // STRIDE, 3, GZX), jnp.float32),
        in_specs=[vmem] * 3,
        out_specs=vmem,
        name="smoothed_update",
    )(sums, pair_sums, other_sums)
    return jnp.transpose(field, (1, 0, 2))


def solution(mesh):
    in_specs = (
        P(("grp", "span"), None, None),
        P(("grp", "span"), None, None),
        P(("grp", "span")),
        P(None, ("grp", "span")),
    )
    out_specs = P(None, ("grp", "span"), None)
    return jax.shard_map(shards, mesh=mesh, in_specs=in_specs, out_specs=out_specs, check_vma=False)
```

```python
import functools

import jax
import jax.numpy as jnp
from jax import lax
from jax.experimental import pallas as pl
from jax.experimental.pallas import tpu as pltpu
from jax.sharding import PartitionSpec as P

W = 48
STRIDE = 12
DYM = 3
GX = 16
GZX = 128
SHARP = 80.0
EPSILON = 1e-06

HALF = W // 2
BLOCK = W + 2
REACH = DYM + 1
LANES = 128
HOP = 64
CHUNK = 6
ROWS_A = 64
ROWS_B = 80
PAD_A = CHUNK
PAD_B = CHUNK + REACH
PIECES = 4
SLOT = 4
PLAN_ROWS = 16
FIELDS = 16
PAIR = 4
CLOSE = 2
FAR = 4096


def send_kernel(win_ref, shift_ref, second_hbm, pair_ref, other_ref, sems):
    planes = second_hbm.shape[0]
    even = lax.axis_index("span") % 2 == 0
    top = planes - REACH

    def fetch(start, target, i):
        return pltpu.make_async_copy(
            second_hbm.at[pl.ds(start, REACH)], target.at[pl.ds(0, REACH)], sems.at[i])

    to_pair = fetch(jnp.where(even, top, 0), pair_ref, 0)
    to_other = fetch(jnp.where(even, 0, top), other_ref, 1)
    to_pair.start()
    to_other.start()
    node = win_ref[...]
    rows = jnp.concatenate([node // 256, node % 256, shift_ref[...]], axis=0)
    rows = rows.astype(jnp.float32).astype(jnp.bfloat16)
    for ref in (pair_ref, other_ref):
        ref[REACH, 0:PLAN_ROWS, :] = jnp.zeros((PLAN_ROWS, ref.shape[2]), jnp.bfloat16)
        ref[REACH, 0:rows.shape[0], 0:node.shape[1]] = rows
    to_pair.wait()
    to_other.wait()


def correlate_kernel(
    win_ref, shift_ref, first_hbm, second_hbm, pair_hbm, other_hbm,
    out_ref, raw_a, raw_b, fr_a, fr_b, acc, sq_a, sq_b, masks, gap_base, plan_in,
    plan_int, plan, table, units, active, sem_a, sem_b, sem_h, sem_p,
):
    own = win_ref.shape[0]
    planes, deep, along = first_hbm.shape
    tile_rows = planes // STRIDE
    device = lax.axis_index("span")
    last = lax.axis_size("span") - 1
    even = device % 2 == 0
    piece = planes // PIECES

    def copy_a(i):
        return pltpu.make_async_copy(
            first_hbm.at[pl.ds(i * piece, piece)], raw_a.at[pl.ds(i * piece, piece)], sem_a.at[i])

    def copy_b(i):
        return pltpu.make_async_copy(
            second_hbm.at[pl.ds(i * piece, piece)],
            raw_b.at[pl.ds(REACH + i * piece, piece)], sem_b.at[i])

    low_at, high_at = 0, REACH + planes
    pair_at = jnp.where(even, high_at, low_at)
    other_at = jnp.where(even, low_at, high_at)
    pair_side = jnp.where(even, 1, 0)
    halo = [
        pltpu.make_async_copy(
            ref.at[pl.ds(0, REACH)], raw_b.at[pl.ds(at, REACH)], sem_h.at[i])
        for i, (ref, at) in enumerate(((pair_hbm, pair_at), (other_hbm, other_at)))
    ]
    plans = [
        pltpu.make_async_copy(
            ref.at[REACH, pl.ds(0, PLAN_ROWS)], plan_in.at[side], sem_p.at[i])
        for i, (ref, side) in enumerate(((pair_hbm, pair_side), (other_hbm, 1 - pair_side)))
    ]
    for c in plans:
        c.start()
    for i in range(PIECES):
        copy_a(i).start()
    for i in range(PIECES):
        copy_b(i).start()
    for c in halo:
        c.start()

    @pl.when((device == 0) | (device == last))
    def _():
        zero = jnp.zeros((2, 2, CHUNK, deep, LANES), jnp.bfloat16)
        fr_a[:, :, 0:PAD_A] = zero
        fr_a[:, :, PAD_A + planes:] = zero
        fr_b[:, :, 0:CHUNK] = zero
        fr_b[:, :, PAD_B + planes + REACH:] = zero

    out_ref[...] = jnp.zeros(out_ref.shape, jnp.float32)
    col = lax.broadcasted_iota(jnp.int32, gap_base.shape, 1)
    col_lag = jnp.where(col >= ROWS_B, 1, 0) + jnp.where(col >= 2 * ROWS_B, 1, 0)
    gap_base[...] = jnp.where(
        col < 3 * ROWS_B,
        col - col_lag * ROWS_B - lax.broadcasted_iota(jnp.int32, gap_base.shape, 0), FAR)

    def prepare(s, carry):
        total, alive = carry
        group = s // own
        idx = s - group * own
        side = jnp.maximum(group - 1, 0)
        mine = group == 0

        def pick(own_value, row):
            return jnp.where(mine, own_value, plan[side, row, idx])

        node = jnp.where(mine, win_ref[idx], plan[side, 0, idx] * 256 + plan[side, 1, idx])
        dy = pick(shift_ref[0, idx], 2)
        dz = pick(shift_ref[1, idx], 3)
        dx = pick(shift_ref[2, idx], 4)
        row = node // GZX - device * tile_rows
        rest = node % GZX
        cy = STRIDE * row + STRIDE // 2
        cz = STRIDE * (rest // GX) + STRIDE // 2
        cx = STRIDE * (rest % GX) + STRIDE // 2
        start = jnp.maximum(cy - HALF, jnp.where(device == 0, -CHUNK, 0))
        stop = jnp.minimum(cy + HALF, jnp.where(device == last, planes + CHUNK, planes))
        wanted = (
            mine
            | ((group == 1) & (row < 0) & (row >= -tile_rows))
            | ((group == 2) & (row >= tile_rows) & (row < 2 * tile_rows))
        )
        count = jnp.where(wanted, jnp.maximum(stop - start, 0) // CHUNK, 0)
        target = jnp.where(
            mine | ((group == 1) & (row == -1)) | ((group == 2) & (row == tile_rows)),
            (row + 1) * GZX + rest, -1)
        lane_out = lax.broadcasted_iota(jnp.int32, (1, LANES), 1)
        out_ref[22:23, :] = jnp.where(
            lane_out == SLOT * s, target.astype(jnp.float32), out_ref[22:23, :])

        @pl.when(count > 0)
        def _():
            z_a = jnp.clip((cz - HALF) // 16 * 16, 0, deep - ROWS_A)
            sz = cz + dz - HALF - 1
            z_b = jnp.where(sz + BLOCK <= ROWS_B, 0, deep - ROWS_B)
            sx = cx + dx - HALF - 1
            f_a = jnp.where(cx + HALF <= LANES, 0, 1)
            f_b = jnp.where(sx + BLOCK <= LANES, 0, 1)
            has_first = jnp.where(start == cy - HALF, 1, 0)
            has_last = jnp.where(stop == cy + HALF, 1, 0)
            for at, value in enumerate(
                (f_a, z_a, f_b, z_b, dy, dz, (dx + LANES) % LANES, cz,
                 start + dy - 1 + PAD_B, stop + dy + PAD_B, has_first, has_last)
            ):
                table[s, at] = value
            active[alive] = s
            lane16 = lax.broadcasted_iota(jnp.int32, (16, LANES), 1)
            row16 = lax.broadcasted_iota(jnp.int32, (16, LANES), 0)
            lag16 = row16 - 1
            wide16 = row16 == 3
            from16 = jnp.where(wide16, sx, cx + dx + lag16 - HALF)
            upto16 = from16 + jnp.where(wide16, BLOCK, jnp.where(row16 < 3, W, 0))
            for half in range(2):
                lane = (lane16 + half * HOP) % LANES
                low = jnp.where(lane < HOP, LANES, 0)
                x_a = lane + low * f_a
                x_b = lane + low * f_b
                inside = (x_a >= cx - HALF) & (x_a < cx + HALF)
                masks[s, half] = jnp.where(inside, 1.0, 0.0).astype(jnp.bfloat16)
                inside = (x_b >= sx) & (x_b < sx + BLOCK)
                masks[s, 2 + half] = jnp.where(inside, 1.0, 0.0).astype(jnp.bfloat16)
                inside = (x_b >= from16) & (x_b < upto16)
                masks[s, 4 + half] = jnp.where(inside, 1.0, 0.0).astype(jnp.bfloat16)
            for ref in (acc, sq_a, sq_b):
                ref[s] = jnp.zeros(ref.shape[1:], jnp.float32)
            for c in range(W // CHUNK // 2):
                both = jnp.where(2 * c + 1 < count, 1, 0)
                units[total + c] = s + (start + 2 * CHUNK * c + 64) * 256 + both * 65536

        return total + (count + 1) // 2, alive + jnp.where(count > 0, 1, 0)

    carry = lax.fori_loop(0, own, prepare, (0, 0))
    for c in plans:
        c.wait()
    plan_int[...] = plan_in[:, 0:8, 0:LANES].astype(jnp.float32).astype(jnp.int32)
    to_scalar = pltpu.make_async_copy(plan_int, plan, sem_p.at[2])
    to_scalar.start()

    def frame(raw, fr, shift):
        def body(p, carry):
            v = raw[p]
            low = v[:, :LANES]
            high = jnp.concatenate([v[:, LANES:], v[:, HOP:LANES]], axis=1)
            fr[0, 0, p + shift] = low
            fr[0, 1, p + shift] = high
            fr[1, 0, p + shift] = pltpu.roll(low, HOP, 1)
            fr[1, 1, p + shift] = pltpu.roll(high, HOP, 1)
            return carry
        return body

    frame_a = frame(raw_a, fr_a, PAD_A)
    frame_b = frame(raw_b, fr_b, CHUNK)
    for i in range(PIECES):
        copy_a(i).wait()
        lax.fori_loop(i * piece, (i + 1) * piece, frame_a, 0, unroll=piece)
    to_scalar.wait()
    total, alive = lax.fori_loop(own, 3 * own, prepare, carry)
    spare = 3 * own
    for at in range(FIELDS):
        table[spare, at] = 0
    for at in range(PAIR - 1):
        units[total + at] = spare + 64 * 256
    for at in range(CLOSE - 1):
        active[alive + at] = spare
    for i in range(PIECES):
        copy_b(i).wait()
        lax.fori_loop(REACH + i * piece, REACH + (i + 1) * piece, frame_b, 0, unroll=piece)
    for c in halo:
        c.wait()
    lax.fori_loop(0, REACH, frame_b, 0, unroll=REACH)
    lax.fori_loop(REACH + planes, 2 * REACH + planes, frame_b, 0, unroll=REACH)

    ones = jnp.where(
        lax.broadcasted_iota(jnp.int32, (16, CHUNK * LANES), 0) == 0, 1.0, 0.0
    ).astype(jnp.bfloat16)

    def step(t, carry):
        for h in range(PAIR):
            code = units[PAIR * t + h]
            s = code % 256
            y = (code // 256) % 256 - 64
            both = code // 65536
            y_two = y + both * CHUNK
            keep = both.astype(jnp.float32).astype(jnp.bfloat16)
            f_a = table[s, 0]
            z_a = pl.multiple_of(table[s, 1], 16)
            f_b = table[s, 2]
            z_b = pl.multiple_of(table[s, 3], 16)
            dy = table[s, 4]
            dx = table[s, 6]

            def tall(at, rows, scale=None):
                v = masks[s, at]
                v = v if scale is None else v * scale
                return jnp.concatenate([v] * (rows // 16), axis=0)

            one_a, two_a = tall(0, ROWS_A), tall(1, ROWS_A, keep)
            one_b, two_b = tall(2, ROWS_B), tall(3, ROWS_B, keep)
            a = [
                fr_a[0, f_a, y + PAD_A + p, pl.ds(z_a, ROWS_A), :] * one_a
                + fr_a[1, f_a, y_two + PAD_A + p, pl.ds(z_a, ROWS_A), :] * two_a
                for p in range(CHUNK)
            ]
            b = [
                fr_b[0, f_b, y + dy - 1 + PAD_B + p, pl.ds(z_b, ROWS_B), :] * one_b
                + fr_b[1, f_b, y_two + dy - 1 + PAD_B + p, pl.ds(z_b, ROWS_B), :] * two_b
                for p in range(CHUNK + 2)
            ]
            left = [
                jnp.concatenate(
                    [pltpu.roll(v, (dx + lag - 1 + LANES) % LANES, 1) for v in a], axis=1)
                for lag in range(3)
            ]
            left.append(jnp.concatenate([masks[s, 4] + masks[s, 5] * keep] * CHUNK, axis=1))
            left = jnp.concatenate(left, axis=0)
            right = [jnp.concatenate(b[lag:lag + CHUNK], axis=1) for lag in range(3)]
            right = jnp.concatenate(right + [ones], axis=0)
            acc[s] += lax.dot_general(
                left, right, (((1,), (1,)), ((), ())), preferred_element_type=jnp.float32)
            wide = [v.astype(jnp.float32) for v in a]
            sq_a[s] += sum([v * v for v in wide])
            wide = [v.astype(jnp.float32) for v in b[1:-1]]
            sq_b[s] += sum([v * v for v in wide])
        return carry

    lax.fori_loop(0, (total + PAIR - 1) // PAIR, step, 0)

    cols = 2 * LANES
    z_row = lax.broadcasted_iota(jnp.int32, (ROWS_A, LANES), 0)
    col_one = lax.broadcasted_iota(jnp.int32, (1, cols), 1)
    lag_one = jnp.where(col_one >= ROWS_B, 1, 0) + jnp.where(col_one >= 2 * ROWS_B, 1, 0)
    lag_one = lag_one + jnp.where(col_one >= 3 * ROWS_B, 1, 0)
    z_one = col_one - lag_one * ROWS_B
    lag_18 = jnp.broadcast_to(lag_one, (18, cols))
    lane_18 = lax.broadcasted_iota(jnp.int32, (18, LANES), 1)
    lane_4 = lax.broadcasted_iota(jnp.int32, (4, LANES), 1)
    z_b_row = lax.broadcasted_iota(jnp.int32, (ROWS_B, LANES), 0)

    def finish(t, carry):
        for h in range(CLOSE):
            s = active[CLOSE * t + h]
            f_a, z_a, f_b, z_b, dy, dz, dx, cz, at_first, at_last, has_first, has_last = [
                table[s, at] for at in range(12)]
            z_b = pl.multiple_of(z_b, 16)
            sz = cz + dz - HALF - 1
            z_from = cz - HALF - z_a
            z_in = (z_row >= z_from) & (z_row < z_from + W)
            gap = [
                jnp.where(z_in, gap_base[:, i * LANES:(i + 1) * LANES], FAR) for i in range(2)
            ]
            offset = z_a + dz - z_b
            tops = []
            lows = []
            for lag_z in range(3):
                hit = [g == offset + lag_z - 1 for g in gap]
                for lag_x in range(3):
                    part = [
                        jnp.sum(jnp.where(
                            hit[i],
                            acc[s, lag_x * ROWS_A:(lag_x + 1) * ROWS_A,
                                i * LANES:(i + 1) * LANES], 0.0), axis=0, keepdims=True)
                        for i in range(2)
                    ]
                    tops.append(jnp.concatenate(part, axis=1))
                low = cz - HALF + dz + lag_z - 1 - z_b
                inside = (z_one >= low) & (z_one < low + W)
                lows.append(jnp.where(inside, acc[s, 3 * ROWS_A:3 * ROWS_A + 3, :], 0.0))
            stack = jnp.concatenate(tops + lows, axis=0)

            z_b_in = (z_b_row >= sz - z_b) & (z_b_row < sz - z_b + BLOCK)
            mask = jnp.concatenate([masks[s, 2].astype(jnp.float32)] * (ROWS_B // 16), axis=0)
            mask = jnp.where(z_b_in, mask, 0.0)
            ends = [
                fr_b[0, f_b, at, pl.ds(z_b, ROWS_B), :].astype(jnp.float32)
                * (mask * has.astype(jnp.float32))
                for at, has in ((at_first, has_first), (at_last, has_last))
            ]
            low = sz - z_b
            inside = (z_one >= low) & (z_one < low + BLOCK) & (lag_one == 1)
            row_b = jnp.where(inside, acc[s, 3 * ROWS_A + 3:3 * ROWS_A + 4, :], 0.0)
            row_a = jnp.sum(jnp.where(
                z_in & (z_row * 0 + lax.broadcasted_iota(
                    jnp.int32, (ROWS_A, LANES), 1) == 3 * ROWS_B - LANES),
                acc[s, ROWS_A:2 * ROWS_A, LANES:], 0.0), axis=0, keepdims=True)
            sums = [
                row_a,
                jnp.sum(jnp.where(z_in, sq_a[s], 0.0), axis=0, keepdims=True),
                jnp.sum(ends[0] + ends[1], axis=0, keepdims=True)
                + row_b[:, :LANES] + row_b[:, LANES:],
                jnp.sum(
                    jnp.where(z_b_in, sq_b[s], 0.0) + (ends[0] * ends[0] + ends[1] * ends[1]),
                    axis=0, keepdims=True),
            ]
            sums = jnp.sum(jnp.concatenate(sums, axis=0), axis=1, keepdims=True)
            total_18 = jnp.zeros((18, LANES), jnp.float32)
            for lag_y in range(3):
                part = jnp.sum(jnp.where(lag_18 == lag_y, stack, 0.0), axis=1, keepdims=True)
                total_18 = total_18 + jnp.where(lane_18 == SLOT * s + lag_y, part, 0.0)
            out_ref[0:18] += total_18
            out_ref[18:22] += jnp.where(lane_4 == SLOT * s, sums, 0.0)
        return carry

    lax.fori_loop(0, (alive + CLOSE - 1) // CLOSE, finish, 0)


def update_kernel(own, mine_ref, pair_ref, other_ref, out_ref):
    tile_rows = out_ref.shape[0]
    even = lax.axis_index("span") % 2 == 0
    mine = mine_ref[...]
    pair = pair_ref[...]
    other = other_ref[...]
    below = jnp.where(even, other, pair)
    above = jnp.where(even, pair, other)
    span = SLOT * own
    lane = lax.broadcasted_iota(jnp.int32, mine.shape, 1)
    total = mine
    total = total + jnp.where(
        lane < span,
        pltpu.roll(below, LANES - 2 * span, 1) + pltpu.roll(above, LANES - span, 1),
        jnp.where(
            lane < 2 * span, pltpu.roll(below, span, 1),
            jnp.where(lane < 3 * span, pltpu.roll(above, 2 * span, 1), 0.0)))

    def lead(v):
        return v + pltpu.roll(v, LANES - 1, 1) + pltpu.roll(v, LANES - 2, 1)

    def spread(v):
        return v + pltpu.roll(v, 1, 1) + pltpu.roll(v, 2, 1)

    lag_lane = lane % SLOT
    stats = spread(jnp.where(lag_lane[0:4] == 0, total[18:22], 0.0))
    voxels = float(W) ** 3
    block_voxels = float(BLOCK) ** 3
    mean_a = stats[0:1] / voxels
    energy_a = jnp.maximum(stats[1:2] / voxels - mean_a * mean_a, 0.0)
    mean_b = stats[2:3] / block_voxels
    energy_b = jnp.maximum(stats[3:4] / block_voxels - mean_b * mean_b, 0.0)
    normaliser = voxels * jnp.sqrt((energy_a + EPSILON) * (energy_b + EPSILON))
    scaled = SHARP * ((total[0:9] - mean_a * total[9:18]) / normaliser)
    used = lag_lane[0:9] < 3
    scaled = jnp.where(used, scaled, -1e30)
    top = jnp.max(scaled, axis=0, keepdims=True)
    top = jnp.maximum(top, jnp.maximum(pltpu.roll(top, LANES - 1, 1), pltpu.roll(top, LANES - 2, 1)))
    top = spread(jnp.where(lag_lane[0:1] == 0, top, 0.0))
    weights = jnp.where(used, jnp.exp(scaled - top), 0.0)
    lag_row = lax.broadcasted_iota(jnp.int32, weights.shape, 0)
    lag_z = (lag_row // 3 - 1).astype(jnp.float32)
    lag_x = (lag_row % 3 - 1).astype(jnp.float32)
    column = jnp.sum(weights, axis=0, keepdims=True)
    weight_sum = lead(column)
    along_y = lead(column * (lag_lane[0:1] - 1).astype(jnp.float32)) / weight_sum
    along_z = lead(jnp.sum(weights * lag_z, axis=0, keepdims=True)) / weight_sum
    along_x = lead(jnp.sum(weights * lag_x, axis=0, keepdims=True)) / weight_sum
    corrections = (along_y, along_z, along_x)

    grid_lane = lax.broadcasted_iota(jnp.int32, (8, LANES), 1)
    place = lax.broadcasted_iota(jnp.int32, (8, LANES), 0) * GZX + grid_lane
    target = mine[22:23].astype(jnp.int32)
    fields = [jnp.zeros((8, LANES), jnp.float32) for _ in range(3)]
    for s in range(3 * own):
        hit = place == target[:, SLOT * s:SLOT * s + 1]
        for comp in range(3):
            fields[comp] = jnp.where(
                hit, corrections[comp][:, SLOT * s:SLOT * s + 1], fields[comp])
    lane_z = grid_lane // GX
    lane_x = grid_lane % GX
    for comp in range(3):
        field = fields[comp]
        near = jnp.where(lane_z >= 1, pltpu.roll(field, GX, 1), 0.0)
        near = near + jnp.where(lane_z < GZX // GX - 1, pltpu.roll(field, LANES - GX, 1), 0.0)
        near = near + jnp.where(lane_x >= 1, pltpu.roll(field, 1, 1), 0.0)
        near = near + jnp.where(lane_x < GX - 1, pltpu.roll(field, LANES - 1, 1), 0.0)
        near = near[1:1 + tile_rows] + field[0:tile_rows] + field[2:2 + tile_rows]
        out_ref[:, comp, :] = 0.4 * field[1:1 + tile_rows] + 0.1 * near


def shards(first, second, windows, shifts):
    planes, deep, along = first.shape
    own = windows.shape[0]
    count = lax.axis_size("span")
    pairs = [(i, i ^ 1) for i in range(count)]
    others = [(i, i + 1) for i in range(1, count - 1, 2)]
    others = others + [(b, a) for a, b in others]
    smem = pl.BlockSpec(memory_space=pltpu.SMEM)
    vmem = pl.BlockSpec(memory_space=pltpu.VMEM)
    hbm = pl.BlockSpec(memory_space=pl.ANY)
    message = jax.ShapeDtypeStruct((REACH + 1, deep, along), second.dtype)
    to_pair, to_other = pl.pallas_call(
        send_kernel,
        out_shape=(message, message),
        in_specs=[vmem, vmem, hbm],
        out_specs=(vmem, vmem),
        scratch_shapes=[pltpu.SemaphoreType.DMA((2,))],
        name="planes_to_send",
    )(windows[None], shifts, second)
    to_other = lax.ppermute(to_other, "span", others)
    to_pair = lax.ppermute(to_pair, "span", pairs)
    sums = pl.pallas_call(
        correlate_kernel,
        out_shape=jax.ShapeDtypeStruct((24, LANES), jnp.float32),
        in_specs=[smem] * 2 + [hbm] * 4,
        out_specs=vmem,
        scratch_shapes=[
            pltpu.VMEM((planes, deep, along), jnp.bfloat16),
            pltpu.VMEM((planes + 2 * REACH, deep, along), jnp.bfloat16),
            pltpu.VMEM((2, 2, planes + 2 * PAD_A, deep, LANES), jnp.bfloat16),
            pltpu.VMEM((2, 2, planes + 2 * PAD_B, deep, LANES), jnp.bfloat16),
            pltpu.VMEM((3 * own + 1, 3 * ROWS_A + 16, 2 * LANES), jnp.float32),
            pltpu.VMEM((3 * own + 1, ROWS_A, LANES), jnp.float32),
            pltpu.VMEM((3 * own + 1, ROWS_B, LANES), jnp.float32),
            pltpu.VMEM((3 * own + 1, 6, 16, LANES), jnp.bfloat16),
            pltpu.VMEM((ROWS_A, 2 * LANES), jnp.int32),
            pltpu.VMEM((2, PLAN_ROWS, along), jnp.bfloat16),
            pltpu.VMEM((2, 8, LANES), jnp.int32),
            pltpu.SMEM((2, 8, LANES), jnp.int32),
            pltpu.SMEM((3 * own + 1, FIELDS), jnp.int32),
            pltpu.SMEM((3 * own * (W // CHUNK) + PAIR,), jnp.int32),
            pltpu.SMEM((3 * own + CLOSE,), jnp.int32),
            pltpu.SemaphoreType.DMA((PIECES,)),
            pltpu.SemaphoreType.DMA((PIECES,)),
            pltpu.SemaphoreType.DMA((2,)),
            pltpu.SemaphoreType.DMA((3,)),
        ],
        compiler_params=pltpu.CompilerParams(vmem_limit_bytes=60 << 20),
        name="partial_sums",
    )(windows, shifts, first, second, to_pair, to_other)
    other_sums = lax.ppermute(sums, "span", others)
    pair_sums = lax.ppermute(sums, "span", pairs)
    field = pl.pallas_call(
        functools.partial(update_kernel, own),
        out_shape=jax.ShapeDtypeStruct((planes // STRIDE, 3, GZX), jnp.float32),
        in_specs=[vmem] * 3,
        out_specs=vmem,
        name="smoothed_update",
    )(sums, pair_sums, other_sums)
    return jnp.transpose(field, (1, 0, 2))


def solution(mesh):
    in_specs = (
        P(("grp", "span"), None, None),
        P(("grp", "span"), None, None),
        P(("grp", "span")),
        P(None, ("grp", "span")),
    )
    out_specs = P(None, ("grp", "span"), None)
    return jax.shard_map(shards, mesh=mesh, in_specs=in_specs, out_specs=out_specs, check_vma=False)
```

```python
import functools

import jax
import jax.numpy as jnp
from jax import lax
from jax.experimental import pallas as pl
from jax.experimental.pallas import tpu as pltpu
from jax.sharding import PartitionSpec as P

W = 48
STRIDE = 12
DYM = 3
GX = 16
GZX = 128
SHARP = 80.0
EPSILON = 1e-06

HALF = W // 2
BLOCK = W + 2
REACH = DYM + 1
LANES = 128
HOP = 64
CHUNK = 6
ROWS_A = 64
ROWS_B = 80
PAD_A = CHUNK
PAD_B = CHUNK + REACH
PIECES = 4
SLOT = 4
PLAN_ROWS = 16
FIELDS = 16
PAIR = 4
CLOSE = 2
FAR = 4096


def table_kernel(gap_ref):
    row = lax.broadcasted_iota(jnp.int32, gap_ref.shape, 0)
    col = lax.broadcasted_iota(jnp.int32, gap_ref.shape, 1)
    lag = jnp.where(col >= ROWS_B, 1, 0) + jnp.where(col >= 2 * ROWS_B, 1, 0)
    gap_ref[...] = jnp.where(col < 3 * ROWS_B, col - lag * ROWS_B - row, FAR)


def send_kernel(win_ref, shift_ref, gap_ref, second_hbm, pair_ref, other_ref, plan_ref, sems):
    planes, deep, along = second_hbm.shape
    even = lax.axis_index("span") % 2 == 0
    top = planes - REACH
    copies = [
        pltpu.make_async_copy(
            second_hbm.at[start + p], target.at[pl.ds(p * deep, deep)], sems.at[side, p])
        for side, (start, target) in enumerate((
            (jnp.where(even, top, 0), pair_ref), (jnp.where(even, 0, top), other_ref)))
        for p in range(REACH)
    ]
    for c in copies:
        c.start()
    node = win_ref[...]
    own = node.shape[1]
    plan_ref[...] = jnp.zeros(plan_ref.shape, jnp.int32)
    plan_ref[0:5, 0:own] = jnp.concatenate([node // 256, node % 256, shift_ref[...]], axis=0)
    plan = plan_ref[...].astype(jnp.float32).astype(jnp.bfloat16)
    base = REACH * deep
    for ref in (pair_ref, other_ref):
        ref[base:base + 8, 0:LANES] = plan
    for c in copies:
        c.wait()


def plan_of(plan, group, idx):
    node = plan[group, 0, idx] * 256 + plan[group, 1, idx]
    return node, plan[group, 2, idx], plan[group, 3, idx], plan[group, 4, idx]


def decode(plan, s, own, planes):
    device = lax.axis_index("span")
    last = lax.axis_size("span") - 1
    tile_rows = planes // STRIDE
    group = s // own
    node, dy, dz, dx = plan_of(plan, group, s - group * own)
    row = node // GZX - device * tile_rows
    rest = node % GZX
    cy = STRIDE * row + STRIDE // 2
    cz = STRIDE * (rest // GX) + STRIDE // 2
    cx = STRIDE * (rest % GX) + STRIDE // 2
    start = jnp.maximum(cy - HALF, jnp.where(device == 0, -CHUNK, 0))
    stop = jnp.minimum(cy + HALF, jnp.where(device == last, planes + CHUNK, planes))
    mine = group == 0
    wanted = (
        mine
        | ((group == 1) & (row < 0) & (row >= -tile_rows))
        | ((group == 2) & (row >= tile_rows) & (row < 2 * tile_rows))
    )
    stop = jnp.where(wanted, jnp.maximum(stop, start), start)
    target = jnp.where(
        mine | ((group == 1) & (row == -1)) | ((group == 2) & (row == tile_rows)),
        (row + 1) * GZX + rest, -1)
    return dy, dz, dx, cy, cz, cx, start, stop, target


def set_table(table, s, deep, dy, dz, dx, cy, cz, cx, start, stop):
    z_a = jnp.clip((cz - HALF) // 16 * 16, 0, deep - ROWS_A)
    sz = cz + dz - HALF - 1
    z_b = jnp.where(sz + BLOCK <= ROWS_B, 0, deep - ROWS_B)
    sx = cx + dx - HALF - 1
    f_a = jnp.where(cx + HALF <= LANES, 0, 1)
    f_b = jnp.where(sx + BLOCK <= LANES, 0, 1)
    has_first = jnp.where(start == cy - HALF, 1, 0)
    has_last = jnp.where(stop == cy + HALF, 1, 0)
    for at, value in enumerate(
        (f_a, z_a, f_b, z_b, dy, dz, (dx + LANES) % LANES, cz,
         start + dy - 1 + PAD_B, stop + dy + PAD_B, has_first, has_last)
    ):
        table[s, at] = value
    return f_a, f_b, sx


def set_masks(masks, s, f_a, f_b, sx, cx, dx):
    lane16 = lax.broadcasted_iota(jnp.int32, (16, LANES), 1)
    row16 = lax.broadcasted_iota(jnp.int32, (16, LANES), 0)
    wide16 = row16 == 3
    from16 = jnp.where(wide16, sx, cx + dx + row16 - 1 - HALF)
    upto16 = from16 + jnp.where(wide16, BLOCK, jnp.where(row16 < 3, W, 0))
    for half in range(2):
        lane = (lane16 + half * HOP) % LANES
        low = jnp.where(lane < HOP, LANES, 0)
        x_a = lane + low * f_a
        x_b = lane + low * f_b
        inside = (x_a >= cx - HALF) & (x_a < cx + HALF)
        masks[s, half] = jnp.where(inside, 1.0, 0.0).astype(jnp.bfloat16)
        inside = (x_b >= sx) & (x_b < sx + BLOCK)
        masks[s, 2 + half] = jnp.where(inside, 1.0, 0.0).astype(jnp.bfloat16)
        inside = (x_b >= from16) & (x_b < upto16)
        masks[s, 4 + half] = jnp.where(inside, 1.0, 0.0).astype(jnp.bfloat16)


def set_units(units, total, s, low, count, most):
    for c in range(most):
        both = jnp.where(2 * c + 1 < count, 1, 0)
        units[total + c] = s + (low + 2 * CHUNK * c + 64) * 256 + both * 65536
    return total + (count + 1) // 2


def frame(v, fr, at):
    low = v[:, :LANES]
    high = jnp.concatenate([v[:, LANES:], v[:, HOP:LANES]], axis=1)
    fr[0, 0, at] = low
    fr[0, 1, at] = high
    fr[1, 0, at] = pltpu.roll(low, HOP, 1)
    fr[1, 1, at] = pltpu.roll(high, HOP, 1)


def run_units(total, units, table, spare, fr_a, fr_b, acc, sq_a, sq_b, masks):
    for at in range(PAIR - 1):
        units[total + at] = spare + 64 * 256
    for at in range(FIELDS):
        table[spare, at] = 0
    ones = jnp.where(
        lax.broadcasted_iota(jnp.int32, (16, CHUNK * LANES), 0) == 0, 1.0, 0.0
    ).astype(jnp.bfloat16)

    def step(t, carry):
        for h in range(PAIR):
            code = units[PAIR * t + h]
            s = code % 256
            y = (code // 256) % 256 - 64
            both = code // 65536
            y_two = y + both * CHUNK
            keep = both.astype(jnp.float32).astype(jnp.bfloat16)
            f_a = table[s, 0]
            z_a = pl.multiple_of(table[s, 1], 16)
            f_b = table[s, 2]
            z_b = pl.multiple_of(table[s, 3], 16)
            dy = table[s, 4]
            dx = table[s, 6]

            def tall(at, rows, scale=None):
                v = masks[s, at]
                v = v if scale is None else v * scale
                return jnp.concatenate([v] * (rows // 16), axis=0)

            one_a, two_a = tall(0, ROWS_A), tall(1, ROWS_A, keep)
            one_b, two_b = tall(2, ROWS_B), tall(3, ROWS_B, keep)
            a = [
                fr_a[0, f_a, y + PAD_A + p, pl.ds(z_a, ROWS_A), :] * one_a
                + fr_a[1, f_a, y_two + PAD_A + p, pl.ds(z_a, ROWS_A), :] * two_a
                for p in range(CHUNK)
            ]
            b = [
                fr_b[0, f_b, y + dy - 1 + PAD_B + p, pl.ds(z_b, ROWS_B), :] * one_b
                + fr_b[1, f_b, y_two + dy - 1 + PAD_B + p, pl.ds(z_b, ROWS_B), :] * two_b
                for p in range(CHUNK + 2)
            ]
            left = [
                jnp.concatenate(
                    [pltpu.roll(v, (dx + lag - 1 + LANES) % LANES, 1) for v in a], axis=1)
                for lag in range(3)
            ]
            left.append(jnp.concatenate([masks[s, 4] + masks[s, 5] * keep] * CHUNK, axis=1))
            left = jnp.concatenate(left, axis=0)
            right = [jnp.concatenate(b[lag:lag + CHUNK], axis=1) for lag in range(3)]
            right = jnp.concatenate(right + [ones], axis=0)
            acc[s] += lax.dot_general(
                left, right, (((1,), (1,)), ((), ())), preferred_element_type=jnp.float32)
            wide = [v.astype(jnp.float32) for v in a]
            sq_a[s] += sum([v * v for v in wide])
            wide = [v.astype(jnp.float32) for v in b[1:-1]]
            sq_b[s] += sum([v * v for v in wide])
        return carry

    lax.fori_loop(0, (total + PAIR - 1) // PAIR, step, 0)


def inner_kernel(
    plan_ref, first_ref, second_ref, fr_a, fr_b, acc, sq_a, sq_b, masks,
    plan, table, units, sem_p,
):
    planes, deep, along = first_ref.shape
    own = (acc.shape[0] - 1) // 3
    device = lax.axis_index("span")
    last = lax.axis_size("span") - 1
    piece = planes // PIECES
    plan_copy = pltpu.make_async_copy(plan_ref, plan.at[0], sem_p)
    plan_copy.start()

    @pl.when((device == 0) | (device == last))
    def _():
        zero = jnp.zeros((2, 2, CHUNK, deep, LANES), jnp.bfloat16)
        fr_a[:, :, 0:PAD_A] = zero
        fr_a[:, :, PAD_A + planes:] = zero
        fr_b[:, :, 0:CHUNK] = zero
        fr_b[:, :, PAD_B + planes + REACH:] = zero

    for ref, fr, pad in ((first_ref, fr_a, PAD_A), (second_ref, fr_b, PAD_B)):
        def body(i, carry, ref=ref, fr=fr, pad=pad):
            for p in range(piece):
                at = i * piece + p
                frame(ref[at], fr, at + pad)
            return carry

        lax.fori_loop(0, PIECES, body, 0)

    plan_copy.wait()

    def prepare(s, total):
        dy, dz, dx, cy, cz, cx, start, stop, target = decode(plan, s, own, planes)
        f_a, f_b, sx = set_table(table, s, deep, dy, dz, dx, cy, cz, cx, start, stop)
        set_masks(masks, s, f_a, f_b, sx, cx, dx)
        for ref in (acc, sq_a, sq_b):
            ref[s] = jnp.zeros(ref.shape[1:], jnp.float32)
        low = jnp.maximum(start, CHUNK)
        count = (jnp.minimum(stop, planes - CHUNK) - low) // CHUNK
        return set_units(units, total, s, low, count, W // CHUNK // 2)

    total = lax.fori_loop(0, own, prepare, 0)
    run_units(total, units, table, 3 * own, fr_a, fr_b, acc, sq_a, sq_b, masks)


def outer_kernel(
    plan_ref, pair_ref, other_ref, gap_base, fr_a, fr_b_in, acc_in, sq_a_in, sq_b_in, masks_in,
    out_ref, fr_b, acc, sq_a, sq_b, masks,
    plan_int, plan, table, units, active, sem_p,
):
    deep = fr_a.shape[3]
    planes = fr_a.shape[2] - 2 * PAD_A
    own = (acc.shape[0] - 1) // 3
    even = lax.axis_index("span") % 2 == 0
    base = REACH * deep
    below_side = jnp.where(even, 2, 1)
    plan_int[0] = plan_ref[...]
    for ref, side in ((pair_ref, below_side), (other_ref, 3 - below_side)):
        plan_int[side] = ref[base:base + 8, 0:LANES].astype(jnp.float32).astype(jnp.int32)
    to_scalar = pltpu.make_async_copy(plan_int, plan, sem_p)
    to_scalar.start()
    low_at, high_at = CHUNK, PAD_B + planes
    pair_at = jnp.where(even, high_at, low_at)
    other_at = jnp.where(even, low_at, high_at)
    for p in range(REACH):
        frame(pair_ref[p * deep:(p + 1) * deep, :], fr_b, pair_at + p)
        frame(other_ref[p * deep:(p + 1) * deep, :], fr_b, other_at + p)
    out_ref[...] = jnp.zeros(out_ref.shape, jnp.float32)
    to_scalar.wait()

    def place(s, target):
        lane_out = lax.broadcasted_iota(jnp.int32, (1, LANES), 1)
        out_ref[22:23, :] = jnp.where(
            lane_out == SLOT * s, target.astype(jnp.float32), out_ref[22:23, :])

    def prepare_own(s, total):
        dy, dz, dx, cy, cz, cx, start, stop, target = decode(plan, s, own, planes)
        place(s, target)
        set_table(table, s, deep, dy, dz, dx, cy, cz, cx, start, stop)
        active[s] = s
        below = start < CHUNK
        low = jnp.where(below, start, planes - CHUNK)
        high = jnp.where(below, CHUNK, stop)
        count = jnp.maximum(high - low, 0) // CHUNK
        return set_units(units, total, s, low, count, 1)

    def prepare(s, carry):
        total, alive = carry
        dy, dz, dx, cy, cz, cx, start, stop, target = decode(plan, s, own, planes)
        place(s, target)
        count = (stop - start) // CHUNK

        @pl.when(count > 0)
        def _():
            f_a, f_b, sx = set_table(table, s, deep, dy, dz, dx, cy, cz, cx, start, stop)
            set_masks(masks, s, f_a, f_b, sx, cx, dx)
            for ref in (acc, sq_a, sq_b):
                ref[s] = jnp.zeros(ref.shape[1:], jnp.float32)
            active[alive] = s
            set_units(units, total, s, start, count, 2)

        return total + (count + 1) // 2, alive + jnp.where(count > 0, 1, 0)

    total = lax.fori_loop(0, own, prepare_own, 0)
    total, alive = lax.fori_loop(own, 3 * own, prepare, (total, own))
    spare = 3 * own
    for at in range(CLOSE - 1):
        active[alive + at] = spare
    run_units(total, units, table, spare, fr_a, fr_b, acc, sq_a, sq_b, masks)

    cols = 2 * LANES
    z_row = lax.broadcasted_iota(jnp.int32, (ROWS_A, LANES), 0)
    col_one = lax.broadcasted_iota(jnp.int32, (1, cols), 1)
    lag_one = jnp.where(col_one >= ROWS_B, 1, 0) + jnp.where(col_one >= 2 * ROWS_B, 1, 0)
    lag_one = lag_one + jnp.where(col_one >= 3 * ROWS_B, 1, 0)
    z_one = col_one - lag_one * ROWS_B
    lag_18 = jnp.broadcast_to(lag_one, (18, cols))
    lane_18 = lax.broadcasted_iota(jnp.int32, (18, LANES), 1)
    lane_4 = lax.broadcasted_iota(jnp.int32, (4, LANES), 1)
    z_b_row = lax.broadcasted_iota(jnp.int32, (ROWS_B, LANES), 0)

    def finish(t, carry):
        for h in range(CLOSE):
            s = active[CLOSE * t + h]
            f_a, z_a, f_b, z_b, dy, dz, dx, cz, at_first, at_last, has_first, has_last = [
                table[s, at] for at in range(12)]
            z_b = pl.multiple_of(z_b, 16)
            sz = cz + dz - HALF - 1
            z_from = cz - HALF - z_a
            z_in = (z_row >= z_from) & (z_row < z_from + W)
            gap = [
                jnp.where(z_in, gap_base[:, i * LANES:(i + 1) * LANES], FAR) for i in range(2)
            ]
            offset = z_a + dz - z_b
            tops = []
            lows = []
            for lag_z in range(3):
                hit = [g == offset + lag_z - 1 for g in gap]
                for lag_x in range(3):
                    part = [
                        jnp.sum(jnp.where(
                            hit[i],
                            acc[s, lag_x * ROWS_A:(lag_x + 1) * ROWS_A,
                                i * LANES:(i + 1) * LANES], 0.0), axis=0, keepdims=True)
                        for i in range(2)
                    ]
                    tops.append(jnp.concatenate(part, axis=1))
                low = cz - HALF + dz + lag_z - 1 - z_b
                inside = (z_one >= low) & (z_one < low + W)
                lows.append(jnp.where(inside, acc[s, 3 * ROWS_A:3 * ROWS_A + 3, :], 0.0))
            stack = jnp.concatenate(tops + lows, axis=0)

            z_b_in = (z_b_row >= sz - z_b) & (z_b_row < sz - z_b + BLOCK)
            mask = jnp.concatenate([masks[s, 2].astype(jnp.float32)] * (ROWS_B // 16), axis=0)
            mask = jnp.where(z_b_in, mask, 0.0)
            ends = [
                fr_b[0, f_b, at, pl.ds(z_b, ROWS_B), :].astype(jnp.float32)
                * (mask * has.astype(jnp.float32))
                for at, has in ((at_first, has_first), (at_last, has_last))
            ]
            low = sz - z_b
            inside = (z_one >= low) & (z_one < low + BLOCK) & (lag_one == 1)
            row_b = jnp.where(inside, acc[s, 3 * ROWS_A + 3:3 * ROWS_A + 4, :], 0.0)
            row_a = jnp.sum(jnp.where(
                z_in & (z_row * 0 + lax.broadcasted_iota(
                    jnp.int32, (ROWS_A, LANES), 1) == 3 * ROWS_B - LANES),
                acc[s, ROWS_A:2 * ROWS_A, LANES:], 0.0), axis=0, keepdims=True)
            sums = [
                row_a,
                jnp.sum(jnp.where(z_in, sq_a[s], 0.0), axis=0, keepdims=True),
                jnp.sum(ends[0] + ends[1], axis=0, keepdims=True)
                + row_b[:, :LANES] + row_b[:, LANES:],
                jnp.sum(
                    jnp.where(z_b_in, sq_b[s], 0.0) + (ends[0] * ends[0] + ends[1] * ends[1]),
                    axis=0, keepdims=True),
            ]
            sums = jnp.sum(jnp.concatenate(sums, axis=0), axis=1, keepdims=True)
            total_18 = jnp.zeros((18, LANES), jnp.float32)
            for lag_y in range(3):
                part = jnp.sum(jnp.where(lag_18 == lag_y, stack, 0.0), axis=1, keepdims=True)
                total_18 = total_18 + jnp.where(lane_18 == SLOT * s + lag_y, part, 0.0)
            out_ref[0:18] += total_18
            out_ref[18:22] += jnp.where(lane_4 == SLOT * s, sums, 0.0)
        return carry

    lax.fori_loop(0, (alive + CLOSE - 1) // CLOSE, finish, 0)


def update_kernel(own, mine_ref, pair_ref, other_ref, out_ref):
    tile_rows = out_ref.shape[0]
    even = lax.axis_index("span") % 2 == 0
    mine = mine_ref[...]
    pair = pair_ref[...]
    other = other_ref[...]
    below = jnp.where(even, other, pair)
    above = jnp.where(even, pair, other)
    span = SLOT * own
    lane = lax.broadcasted_iota(jnp.int32, mine.shape, 1)
    total = mine
    total = total + jnp.where(
        lane < span,
        pltpu.roll(below, LANES - 2 * span, 1) + pltpu.roll(above, LANES - span, 1),
        jnp.where(
            lane < 2 * span, pltpu.roll(below, span, 1),
            jnp.where(lane < 3 * span, pltpu.roll(above, 2 * span, 1), 0.0)))

    def lead(v):
        return v + pltpu.roll(v, LANES - 1, 1) + pltpu.roll(v, LANES - 2, 1)

    def spread(v):
        return v + pltpu.roll(v, 1, 1) + pltpu.roll(v, 2, 1)

    lag_lane = lane % SLOT
    stats = spread(jnp.where(lag_lane[0:4] == 0, total[18:22], 0.0))
    voxels = float(W) ** 3
    block_voxels = float(BLOCK) ** 3
    mean_a = stats[0:1] / voxels
    energy_a = jnp.maximum(stats[1:2] / voxels - mean_a * mean_a, 0.0)
    mean_b = stats[2:3] / block_voxels
    energy_b = jnp.maximum(stats[3:4] / block_voxels - mean_b * mean_b, 0.0)
    normaliser = voxels * jnp.sqrt((energy_a + EPSILON) * (energy_b + EPSILON))
    scaled = SHARP * ((total[0:9] - mean_a * total[9:18]) / normaliser)
    used = lag_lane[0:9] < 3
    scaled = jnp.where(used, scaled, -1e30)
    top = jnp.max(scaled, axis=0, keepdims=True)
    top = jnp.maximum(top, jnp.maximum(pltpu.roll(top, LANES - 1, 1), pltpu.roll(top, LANES - 2, 1)))
    top = spread(jnp.where(lag_lane[0:1] == 0, top, 0.0))
    weights = jnp.where(used, jnp.exp(scaled - top), 0.0)
    lag_row = lax.broadcasted_iota(jnp.int32, weights.shape, 0)
    lag_z = (lag_row // 3 - 1).astype(jnp.float32)
    lag_x = (lag_row % 3 - 1).astype(jnp.float32)
    column = jnp.sum(weights, axis=0, keepdims=True)
    weight_sum = lead(column)
    along_y = lead(column * (lag_lane[0:1] - 1).astype(jnp.float32)) / weight_sum
    along_z = lead(jnp.sum(weights * lag_z, axis=0, keepdims=True)) / weight_sum
    along_x = lead(jnp.sum(weights * lag_x, axis=0, keepdims=True)) / weight_sum
    corrections = (along_y, along_z, along_x)

    grid_lane = lax.broadcasted_iota(jnp.int32, (8, LANES), 1)
    place = lax.broadcasted_iota(jnp.int32, (8, LANES), 0) * GZX + grid_lane
    target = mine[22:23].astype(jnp.int32)
    fields = [jnp.zeros((8, LANES), jnp.float32) for _ in range(3)]
    for s in range(3 * own):
        hit = place == target[:, SLOT * s:SLOT * s + 1]
        for comp in range(3):
            fields[comp] = jnp.where(
                hit, corrections[comp][:, SLOT * s:SLOT * s + 1], fields[comp])
    lane_z = grid_lane // GX
    lane_x = grid_lane % GX
    for comp in range(3):
        field = fields[comp]
        near = jnp.where(lane_z >= 1, pltpu.roll(field, GX, 1), 0.0)
        near = near + jnp.where(lane_z < GZX // GX - 1, pltpu.roll(field, LANES - GX, 1), 0.0)
        near = near + jnp.where(lane_x >= 1, pltpu.roll(field, 1, 1), 0.0)
        near = near + jnp.where(lane_x < GX - 1, pltpu.roll(field, LANES - 1, 1), 0.0)
        near = near[1:1 + tile_rows] + field[0:tile_rows] + field[2:2 + tile_rows]
        out_ref[:, comp, :] = 0.4 * field[1:1 + tile_rows] + 0.1 * near


def shards(first, second, windows, shifts):
    planes, deep, along = first.shape
    own = windows.shape[0]
    slots = 3 * own + 1
    count = lax.axis_size("span")
    pairs = [(i, i ^ 1) for i in range(count)]
    others = [(i, i + 1) for i in range(1, count - 1, 2)]
    others = others + [(b, a) for a, b in others]
    vmem = pl.BlockSpec(memory_space=pltpu.VMEM)
    hbm = pl.BlockSpec(memory_space=pltpu.HBM)

    def limit(mib):
        return pltpu.CompilerParams(vmem_limit_bytes=mib << 20)

    busy = pl.CostEstimate(flops=20 * 10**9, bytes_accessed=0, transcendentals=0)
    message = jax.ShapeDtypeStruct((REACH * deep + PLAN_ROWS, along), second.dtype)
    gap = pl.pallas_call(
        table_kernel,
        out_shape=jax.ShapeDtypeStruct((ROWS_A, 2 * LANES), jnp.int32),
        out_specs=vmem,
        compiler_params=limit(4),
        cost_estimate=busy,
        name="gap_table",
    )()
    to_pair, to_other, plan = pl.pallas_call(
        send_kernel,
        out_shape=(message, message, jax.ShapeDtypeStruct((8, LANES), jnp.int32)),
        in_specs=[vmem] * 3 + [hbm],
        out_specs=(vmem,) * 3,
        scratch_shapes=[pltpu.SemaphoreType.DMA((2, REACH))],
        compiler_params=limit(4),
        cost_estimate=busy,
        name="planes_to_send",
    )(windows[None], shifts, gap, second)
    from_other = lax.ppermute(to_other, "span", others)
    from_pair = lax.ppermute(to_pair, "span", pairs)
    state = (
        jax.ShapeDtypeStruct((2, 2, planes + 2 * PAD_B, deep, LANES), jnp.bfloat16),
        jax.ShapeDtypeStruct((slots, 3 * ROWS_A + 16, 2 * LANES), jnp.float32),
        jax.ShapeDtypeStruct((slots, ROWS_A, LANES), jnp.float32),
        jax.ShapeDtypeStruct((slots, ROWS_B, LANES), jnp.float32),
        jax.ShapeDtypeStruct((slots, 6, 16, LANES), jnp.bfloat16),
    )
    scalars = [
        pltpu.SMEM((3, 8, LANES), jnp.int32),
        pltpu.SMEM((slots, FIELDS), jnp.int32),
        pltpu.SMEM((3 * own * (W // CHUNK) + PAIR,), jnp.int32),
    ]
    fr_a, *held = pl.pallas_call(
        inner_kernel,
        out_shape=(
            jax.ShapeDtypeStruct((2, 2, planes + 2 * PAD_A, deep, LANES), jnp.bfloat16), *state),
        in_specs=[vmem] * 3,
        out_specs=(vmem,) * 6,
        scratch_shapes=[
            *scalars,
            pltpu.SemaphoreType.DMA,
        ],
        compiler_params=limit(12),
        cost_estimate=pl.CostEstimate(
            flops=20 * 10**9, bytes_accessed=10 * 10**6, transcendentals=0),
        name="inner_sums",
    )(plan, first, second)
    sums, *_ = pl.pallas_call(
        outer_kernel,
        out_shape=(jax.ShapeDtypeStruct((24, LANES), jnp.float32), *state),
        in_specs=[vmem] * 10,
        out_specs=(vmem,) * 6,
        input_output_aliases={5 + i: 1 + i for i in range(5)},
        scratch_shapes=[
            pltpu.VMEM((3, 8, LANES), jnp.int32),
            *scalars,
            pltpu.SMEM((slots + CLOSE,), jnp.int32),
            pltpu.SemaphoreType.DMA,
        ],
        compiler_params=limit(12),
        name="outer_sums",
    )(plan, from_pair, from_other, gap, fr_a, *held)
    other_sums = lax.ppermute(sums, "span", others)
    pair_sums = lax.ppermute(sums, "span", pairs)
    field = pl.pallas_call(
        functools.partial(update_kernel, own),
        out_shape=jax.ShapeDtypeStruct((planes // STRIDE, 3, GZX), jnp.float32),
        in_specs=[vmem] * 3,
        out_specs=vmem,
        compiler_params=limit(4),
        name="smoothed_update",
    )(sums, pair_sums, other_sums)
    return jnp.transpose(field, (1, 0, 2))


def solution(mesh):
    in_specs = (
        P(("grp", "span"), None, None),
        P(("grp", "span"), None, None),
        P(("grp", "span")),
        P(None, ("grp", "span")),
    )
    out_specs = P(None, ("grp", "span"), None)
    return jax.shard_map(shards, mesh=mesh, in_specs=in_specs, out_specs=out_specs, check_vma=False)
```

```python
import functools

import jax
import jax.numpy as jnp
from jax import lax
from jax.experimental import pallas as pl
from jax.experimental.pallas import tpu as pltpu
from jax.sharding import PartitionSpec as P

W = 48
STRIDE = 12
DYM = 3
GX = 16
GZX = 128
SHARP = 80.0
EPSILON = 1e-06

HALF = W // 2
BLOCK = W + 2
REACH = DYM + 1
LANES = 128
HOP = 64
CHUNK = 6
ROWS_A = 64
ROWS_B = 80
PAD_A = CHUNK
PAD_B = CHUNK + REACH
PIECES = 2
SLOT = 4
PLAN_ROWS = 16
FIELDS = 24
PAIR = 8
REST = 4
CLOSE = 2
FAR = 4096


def table_kernel(low_ref, gap_ref):
    row = lax.broadcasted_iota(jnp.int32, gap_ref.shape, 0)
    col = lax.broadcasted_iota(jnp.int32, gap_ref.shape, 1)
    lag = jnp.where(col >= ROWS_B, 1, 0) + jnp.where(col >= 2 * ROWS_B, 1, 0)
    gap_ref[...] = jnp.where(col < 3 * ROWS_B, col - lag * ROWS_B - row, FAR)


def send_kernel(win_ref, shift_ref, gap_ref, low_ref, high_ref, pair_ref, other_ref, plan_ref):
    reach, deep, along = low_ref.shape
    even = lax.axis_index("span") % 2 == 0
    node = win_ref[...]
    own = node.shape[1]
    plan_ref[...] = jnp.zeros(plan_ref.shape, jnp.int32)
    plan_ref[0:1, 0:own] = node >> 8
    plan_ref[1:2, 0:own] = node & 255
    plan_ref[2:5, 0:own] = shift_ref[...]
    plan = plan_ref[...].astype(jnp.float32).astype(jnp.bfloat16)
    for ref in (pair_ref, other_ref):
        ref[reach * deep:reach * deep + 8, 0:LANES] = plan

    def fill(to_low, to_high):
        for p in range(reach):
            to_low[p * deep:(p + 1) * deep, :] = low_ref[p]
            to_high[p * deep:(p + 1) * deep, :] = high_ref[p]

    @pl.when(even)
    def _():
        fill(other_ref, pair_ref)

    @pl.when(jnp.logical_not(even))
    def _():
        fill(pair_ref, other_ref)


def decode(plan, own, planes, deep, inner, table):
    device = lax.axis_index("span")
    last = lax.axis_size("span") - 1
    tile_rows = planes // STRIDE
    slot = lax.broadcasted_iota(jnp.int32, (1, LANES), 1)
    node = plan[0:1] * 256 + plan[1:2]
    dy, dz, dx = plan[2:3], plan[3:4], plan[4:5]
    row = (node >> (GZX.bit_length() - 1)) - device * tile_rows
    rest = node & (GZX - 1)
    cy = STRIDE * row + STRIDE // 2
    cz = STRIDE * (rest >> (GX.bit_length() - 1)) + STRIDE // 2
    cx = STRIDE * (rest & (GX - 1)) + STRIDE // 2
    start = jnp.maximum(cy - HALF, jnp.where(device == 0, -CHUNK, 0))
    stop = jnp.minimum(cy + HALF, jnp.where(device == last, planes + CHUNK, planes))
    mine = slot < own
    lower = (slot >= own) & (slot < 2 * own)
    upper = (slot >= 2 * own) & (slot < 3 * own)
    wanted = (
        mine | (lower & (row < 0) & (row >= -tile_rows))
        | (upper & (row >= tile_rows) & (row < 2 * tile_rows))
    )
    if inner:
        low = jnp.maximum(start, CHUNK)
        high = jnp.minimum(stop, planes - CHUNK)
        wanted = mine
    else:
        below = start < CHUNK
        low = jnp.where(mine & jnp.logical_not(below), planes - CHUNK, start)
        high = jnp.where(mine & below, CHUNK, stop)
    width = jnp.where(wanted, high - low, 0)
    count = sum([jnp.where(width > CHUNK * c, 1, 0) for c in range(W // CHUNK)])
    sx = cx + dx - HALF - 1
    sz = cz + dz - HALF - 1
    z_a = jnp.minimum(jnp.maximum(cz - HALF, 0) & -16, deep - ROWS_A)
    z_b = jnp.where(sz + BLOCK <= ROWS_B, 0, deep - ROWS_B)
    values = (
        jnp.where(cx + HALF <= LANES, 0, 1),
        z_a,
        jnp.where(sx + BLOCK <= LANES, 0, 1),
        z_b,
        dy,
        z_a + dz - z_b,
        (dx + LANES) & (LANES - 1),
        cz - HALF - z_a,
        start + dy - 1 + PAD_B,
        stop + dy + PAD_B,
        jnp.where(start == cy - HALF, 1, 0),
        jnp.where(stop == cy + HALF, 1, 0),
        low,
        count,
        cx - HALF,
        sx,
        sz - z_b,
    )
    for at, value in enumerate(values):
        table[at:at + 1, :] = jnp.where(slot < 3 * own, value, 0)
    return jnp.where(
        mine | (lower & (row == -1)) | (upper & (row == tile_rows)),
        (row + 1) * GZX + rest, -1)


def set_masks(masks, s, table):
    f_a, f_b = table[0, s], table[2, s]
    z_from, x_from = table[7, s], table[14, s]
    sx, zb_from = table[15, s], table[16, s]
    reach_x = sx + 1

    def in_x(rows, half, frame_at, low, high):
        lane = (lax.broadcasted_iota(jnp.int32, (rows, LANES), 1) + half * HOP) & (LANES - 1)
        x = lane + jnp.where(lane < HOP, LANES * frame_at, 0)
        return (x >= low) & (x < high)

    def in_z(rows, low, count):
        z = lax.broadcasted_iota(jnp.int32, (rows, LANES), 0)
        return (z >= low) & (z < low + count)

    row = lax.broadcasted_iota(jnp.int32, (16, LANES), 0)
    wide = row == 3
    low = jnp.where(wide, sx, reach_x + row - 1)
    high = low + jnp.where(wide, BLOCK, jnp.where(row < 3, W, 0))
    z_a = in_z(ROWS_A, z_from, W)
    z_b = in_z(ROWS_B, zb_from, BLOCK)
    at = 0
    for rows, frame_at, x_low, x_high, z in (
        (ROWS_A, f_a, x_from, x_from + W, z_a),
        (ROWS_B, f_b, sx, sx + BLOCK, z_b),
        (16, f_b, low, high, None),
    ):
        for half in range(2):
            inside = in_x(rows, half, frame_at, x_low, x_high)
            inside = inside if z is None else inside & z
            masks[s, at:at + rows] = jnp.where(inside, 1.0, 0.0).astype(jnp.bfloat16)
            at += rows


def set_units(units, total, s, low, count, most):
    for c in range(most):
        both = jnp.where(2 * c + 1 < count, 1, 0)
        units[total + c] = s + (low + 2 * CHUNK * c + 64) * 256 + both * 65536
    return total + ((count + 1) >> 1)


def frame(v, fr, at):
    low = v[:, :LANES]
    high = jnp.concatenate([v[:, LANES:], v[:, HOP:LANES]], axis=1)
    fr[0, 0, at] = low
    fr[0, 1, at] = high
    fr[1, 0, at] = pltpu.roll(low, HOP, 1)
    fr[1, 1, at] = pltpu.roll(high, HOP, 1)


def run_units(total, units, table, spare, fr_a, fr_b, acc, sq_a, sq_b, masks):
    for at in range(REST - 1):
        units[total + at] = spare + 64 * 256
    ones = jnp.where(
        lax.broadcasted_iota(jnp.int32, (16, CHUNK * LANES), 0) == 0, 1.0, 0.0
    ).astype(jnp.bfloat16)

    def step(first, width):
        for h in range(width):
            code = units[first + h]
            s = code & 255
            y = ((code >> 8) & 255) - 64
            both = code >> 16
            y_two = y + both * CHUNK
            keep = both.astype(jnp.float32).astype(jnp.bfloat16)
            f_a = table[0, s]
            z_a = pl.multiple_of(table[1, s], 16)
            f_b = table[2, s]
            z_b = pl.multiple_of(table[3, s], 16)
            dy = table[4, s]
            dx = table[6, s]
            one_a = masks[s, 0:ROWS_A]
            two_a = masks[s, ROWS_A:2 * ROWS_A] * keep
            at = 2 * ROWS_A
            one_b = masks[s, at:at + ROWS_B]
            two_b = masks[s, at + ROWS_B:at + 2 * ROWS_B] * keep
            at += 2 * ROWS_B
            rows = masks[s, at:at + 16] + masks[s, at + 16:at + 32] * keep
            a = [
                fr_a[0, f_a, y + PAD_A + p, pl.ds(z_a, ROWS_A), :] * one_a
                + fr_a[1, f_a, y_two + PAD_A + p, pl.ds(z_a, ROWS_A), :] * two_a
                for p in range(CHUNK)
            ]
            b = [
                fr_b[0, f_b, y + dy - 1 + PAD_B + p, pl.ds(z_b, ROWS_B), :] * one_b
                + fr_b[1, f_b, y_two + dy - 1 + PAD_B + p, pl.ds(z_b, ROWS_B), :] * two_b
                for p in range(CHUNK + 2)
            ]
            left = [
                jnp.concatenate(
                    [pltpu.roll(v, (dx + lag - 1 + LANES) & (LANES - 1), 1) for v in a], axis=1)
                for lag in range(3)
            ]
            left.append(jnp.concatenate([rows] * CHUNK, axis=1))
            left = jnp.concatenate(left, axis=0)
            right = [jnp.concatenate(b[lag:lag + CHUNK], axis=1) for lag in range(3)]
            right = jnp.concatenate(right + [ones], axis=0)
            acc[s] += lax.dot_general(
                left, right, (((1,), (1,)), ((), ())), preferred_element_type=jnp.float32)
            wide = [v.astype(jnp.float32) for v in a]
            sq_a[s] += sum([v * v for v in wide])
            wide = [v.astype(jnp.float32) for v in b[1:-1]]
            sq_b[s] += sum([v * v for v in wide])

    def wide_step(t, carry):
        step(PAIR * t, PAIR)
        return carry

    full = (total + REST - 1) // PAIR
    lax.fori_loop(0, full, wide_step, 0)

    @pl.when(total > PAIR * full)
    def _():
        step(PAIR * full, REST)


def edge_copies(edge_a, edge_b, fr_a, fr_b, planes, sem):
    far_a = edge_a.shape[2] // 2
    far_b = edge_b.shape[2] // 2
    return (
        (fr_a.at[:, :, pl.ds(PAD_A, far_a)], edge_a.at[:, :, pl.ds(0, far_a)], sem.at[0]),
        (fr_a.at[:, :, pl.ds(PAD_A + planes - far_a, far_a)],
         edge_a.at[:, :, pl.ds(far_a, far_a)], sem.at[1]),
        (fr_b.at[:, :, pl.ds(PAD_B, far_b)], edge_b.at[:, :, pl.ds(0, far_b)], sem.at[2]),
        (fr_b.at[:, :, pl.ds(PAD_B + planes - far_b, far_b)],
         edge_b.at[:, :, pl.ds(far_b, far_b)], sem.at[3]),
    )


def inner_kernel(
    plan_ref, first_ref, second_ref, edge_a, edge_b, edge_masks, acc, sq_a, sq_b,
    fr_a, fr_b, masks, table_v, table, units, sem_t, sem_e,
):
    planes, deep, along = first_ref.shape
    own = (acc.shape[0] - 1) // 3
    piece = planes // PIECES
    decode(plan_ref[...], own, planes, deep, True, table_v)
    to_scalar = pltpu.make_async_copy(table_v, table, sem_t)
    to_scalar.start()
    for ref, fr, pad in ((first_ref, fr_a, PAD_A), (second_ref, fr_b, PAD_B)):
        def body(i, carry, ref=ref, fr=fr, pad=pad):
            for p in range(piece):
                at = i * piece + p
                frame(ref[at], fr, at + pad)
            return carry

        lax.fori_loop(0, PIECES, body, 0)

    hand_on = [
        pltpu.make_async_copy(source, target, sem)
        for source, target, sem in edge_copies(edge_a, edge_b, fr_a, fr_b, planes, sem_e)
    ]
    for c in hand_on:
        c.start()
    to_scalar.wait()

    def prepare(s, total):
        set_masks(masks, s, table)
        for ref in (acc, sq_a, sq_b):
            ref[s] = jnp.zeros(ref.shape[1:], jnp.float32)
        return set_units(units, total, s, table[12, s], table[13, s], W // CHUNK // 2)

    total = lax.fori_loop(0, own, prepare, 0)
    masks_on = pltpu.make_async_copy(masks.at[pl.ds(0, own)], edge_masks, sem_e.at[4])
    masks_on.start()
    run_units(total, units, table, 3 * own, fr_a, fr_b, acc, sq_a, sq_b, masks)
    for c in hand_on:
        c.wait()
    masks_on.wait()


def outer_kernel(
    plan_ref, pair_ref, other_ref, gap_base, edge_a, edge_b, edge_masks, acc_in, sq_a_in, sq_b_in,
    out_ref, acc, sq_a, sq_b,
    fr_a, fr_b, masks, table_v, table, units, active, sem_t, sem_e,
):
    deep = fr_a.shape[3]
    planes = fr_a.shape[2] - 2 * PAD_A
    own = (acc.shape[0] - 1) // 3
    device = lax.axis_index("span")
    last = lax.axis_size("span") - 1
    even = device % 2 == 0
    base = REACH * deep
    bring_in = [
        pltpu.make_async_copy(source, target, sem)
        for target, source, sem in edge_copies(edge_a, edge_b, fr_a, fr_b, planes, sem_e)
    ] + [pltpu.make_async_copy(edge_masks, masks.at[pl.ds(0, own)], sem_e.at[4])]
    for c in bring_in:
        c.start()
    from_pair, from_other = [
        ref[base:base + 8, 0:LANES].astype(jnp.float32).astype(jnp.int32)
        for ref in (pair_ref, other_ref)
    ]
    below = jnp.where(even, from_other, from_pair)
    above = jnp.where(even, from_pair, from_other)
    plan = plan_ref[...] + pltpu.roll(below, own, 1) + pltpu.roll(above, 2 * own, 1)
    target = decode(plan, own, planes, deep, False, table_v)
    to_scalar = pltpu.make_async_copy(table_v, table, sem_t)
    to_scalar.start()
    out_ref[...] = jnp.zeros(out_ref.shape, jnp.float32)
    out_ref[22:23] = target.astype(jnp.float32)

    @pl.when((device == 0) | (device == last))
    def _():
        zero = jnp.zeros((2, 2, CHUNK, deep, LANES), jnp.bfloat16)
        fr_a[:, :, 0:PAD_A] = zero
        fr_a[:, :, PAD_A + planes:] = zero
        fr_b[:, :, 0:CHUNK] = zero
        fr_b[:, :, PAD_B + planes + REACH:] = zero

    low_at, high_at = CHUNK, PAD_B + planes
    pair_at = jnp.where(even, high_at, low_at)
    other_at = jnp.where(even, low_at, high_at)
    for p in range(REACH):
        frame(pair_ref[p * deep:(p + 1) * deep, :], fr_b, pair_at + p)
        frame(other_ref[p * deep:(p + 1) * deep, :], fr_b, other_at + p)
    to_scalar.wait()

    def prepare_own(s, total):
        active[s] = s
        return set_units(units, total, s, table[12, s], table[13, s], 1)

    total = lax.fori_loop(0, own, prepare_own, 0)
    for c in bring_in:
        c.wait()

    def prepare(s, carry):
        total, alive = carry
        count = table[13, s]

        @pl.when(count > 0)
        def _():
            set_masks(masks, s, table)
            for ref in (acc, sq_a, sq_b):
                ref[s] = jnp.zeros(ref.shape[1:], jnp.float32)
            active[alive] = s
            set_units(units, total, s, table[12, s], count, 2)

        return total + ((count + 1) >> 1), alive + jnp.where(count > 0, 1, 0)

    total, alive = lax.fori_loop(own, 3 * own, prepare, (total, own))
    spare = 3 * own
    for at in range(CLOSE - 1):
        active[alive + at] = spare
    run_units(total, units, table, spare, fr_a, fr_b, acc, sq_a, sq_b, masks)

    cols = 2 * LANES
    col_one = lax.broadcasted_iota(jnp.int32, (1, cols), 1)
    lag_one = jnp.where(col_one >= ROWS_B, 1, 0) + jnp.where(col_one >= 2 * ROWS_B, 1, 0)
    lag_one = lag_one + jnp.where(col_one >= 3 * ROWS_B, 1, 0)
    z_one = col_one - lag_one * ROWS_B
    lag_18 = jnp.broadcast_to(lag_one, (18, cols))
    lane_18 = lax.broadcasted_iota(jnp.int32, (18, LANES), 1)
    lane_4 = lax.broadcasted_iota(jnp.int32, (4, LANES), 1)
    slant = lax.broadcasted_iota(jnp.int32, (8, cols), 1)
    slant = slant - lax.broadcasted_iota(jnp.int32, (8, cols), 0)
    mean_lane = lax.broadcasted_iota(jnp.int32, (1, LANES), 1) == 3 * ROWS_B - LANES

    def finish(t, carry):
        for h in range(CLOSE):
            s = active[CLOSE * t + h]
            f_b = table[2, s]
            z_b = pl.multiple_of(table[3, s], 16)
            offset = table[5, s]
            low_z = table[16, s] + 1
            band = (gap_base[...] >= offset - 1) & (gap_base[...] <= offset + 1)
            tops = [None] * 9
            lows = []
            for lag_x in range(3):
                part = jnp.where(band, acc[s, lag_x * ROWS_A:(lag_x + 1) * ROWS_A, :], 0.0)
                part = sum([part[8 * i:8 * i + 8] for i in range(ROWS_A // 8)])
                for lag_z in range(3):
                    hit = ((slant - (offset + lag_z - 1)) & 7) == 0
                    tops[3 * lag_z + lag_x] = jnp.sum(
                        jnp.where(hit, part, 0.0), axis=0, keepdims=True)
            for lag_z in range(3):
                low = low_z + lag_z - 1
                inside = (z_one >= low) & (z_one < low + W)
                lows.append(jnp.where(inside, acc[s, 3 * ROWS_A:3 * ROWS_A + 3, :], 0.0))
            stack = jnp.concatenate(tops + lows, axis=0)

            at = 2 * ROWS_A
            mask = masks[s, at:at + ROWS_B].astype(jnp.float32)
            ends = [
                fr_b[0, f_b, table[8 + i, s], pl.ds(z_b, ROWS_B), :].astype(jnp.float32)
                * (mask * table[10 + i, s].astype(jnp.float32))
                for i in range(2)
            ]
            row_b = jnp.where(
                lag_one == 1, acc[s, 3 * ROWS_A + 3:3 * ROWS_A + 4, :], 0.0)
            row_a = jnp.sum(acc[s, ROWS_A:2 * ROWS_A, LANES:], axis=0, keepdims=True)
            sums = [
                jnp.where(mean_lane, row_a, 0.0),
                jnp.sum(sq_a[s], axis=0, keepdims=True),
                jnp.sum(ends[0] + ends[1], axis=0, keepdims=True)
                + row_b[:, :LANES] + row_b[:, LANES:],
                jnp.sum(
                    sq_b[s] + (ends[0] * ends[0] + ends[1] * ends[1]), axis=0, keepdims=True),
            ]
            sums = jnp.sum(jnp.concatenate(sums, axis=0), axis=1, keepdims=True)
            total_18 = jnp.zeros((18, LANES), jnp.float32)
            for lag_y in range(3):
                part = jnp.sum(jnp.where(lag_18 == lag_y, stack, 0.0), axis=1, keepdims=True)
                total_18 = total_18 + jnp.where(lane_18 == SLOT * s + lag_y, part, 0.0)
            out_ref[0:18] += total_18
            out_ref[18:22] += jnp.where(lane_4 == SLOT * s, sums, 0.0)
        return carry

    lax.fori_loop(0, (alive + CLOSE - 1) // CLOSE, finish, 0)


def update_kernel(own, mine_ref, pair_ref, other_ref, out_ref):
    tile_rows = out_ref.shape[0]
    even = lax.axis_index("span") % 2 == 0
    mine = mine_ref[...]
    pair = pair_ref[...]
    other = other_ref[...]
    below = jnp.where(even, other, pair)
    above = jnp.where(even, pair, other)
    span = SLOT * own
    lane = lax.broadcasted_iota(jnp.int32, mine.shape, 1)
    total = mine
    total = total + jnp.where(
        lane < span,
        pltpu.roll(below, LANES - 2 * span, 1) + pltpu.roll(above, LANES - span, 1),
        jnp.where(
            lane < 2 * span, pltpu.roll(below, span, 1),
            jnp.where(lane < 3 * span, pltpu.roll(above, 2 * span, 1), 0.0)))

    def lead(v):
        return v + pltpu.roll(v, LANES - 1, 1) + pltpu.roll(v, LANES - 2, 1)

    def spread(v):
        return v + pltpu.roll(v, 1, 1) + pltpu.roll(v, 2, 1)

    lag_lane = lane % SLOT
    stats = spread(jnp.where(lag_lane[0:4] == 0, total[18:22], 0.0))
    voxels = float(W) ** 3
    block_voxels = float(BLOCK) ** 3
    mean_a = stats[0:1] / voxels
    energy_a = jnp.maximum(stats[1:2] / voxels - mean_a * mean_a, 0.0)
    mean_b = stats[2:3] / block_voxels
    energy_b = jnp.maximum(stats[3:4] / block_voxels - mean_b * mean_b, 0.0)
    normaliser = voxels * jnp.sqrt((energy_a + EPSILON) * (energy_b + EPSILON))
    scaled = SHARP * ((total[0:9] - mean_a * total[9:18]) / normaliser)
    used = lag_lane[0:9] < 3
    scaled = jnp.where(used, scaled, -1e30)
    top = jnp.max(scaled, axis=0, keepdims=True)
    top = jnp.maximum(top, jnp.maximum(pltpu.roll(top, LANES - 1, 1), pltpu.roll(top, LANES - 2, 1)))
    top = spread(jnp.where(lag_lane[0:1] == 0, top, 0.0))
    weights = jnp.where(used, jnp.exp(scaled - top), 0.0)
    lag_row = lax.broadcasted_iota(jnp.int32, weights.shape, 0)
    lag_z = (lag_row // 3 - 1).astype(jnp.float32)
    lag_x = (lag_row % 3 - 1).astype(jnp.float32)
    column = jnp.sum(weights, axis=0, keepdims=True)
    weight_sum = lead(column)
    along_y = lead(column * (lag_lane[0:1] - 1).astype(jnp.float32)) / weight_sum
    along_z = lead(jnp.sum(weights * lag_z, axis=0, keepdims=True)) / weight_sum
    along_x = lead(jnp.sum(weights * lag_x, axis=0, keepdims=True)) / weight_sum
    corrections = (along_y, along_z, along_x)

    grid_lane = lax.broadcasted_iota(jnp.int32, (8, LANES), 1)
    place = lax.broadcasted_iota(jnp.int32, (8, LANES), 0) * GZX + grid_lane
    target = mine[22:23].astype(jnp.int32)
    fields = [jnp.zeros((8, LANES), jnp.float32) for _ in range(3)]
    for s in range(3 * own):
        hit = place == target[:, s:s + 1]
        for comp in range(3):
            fields[comp] = jnp.where(
                hit, corrections[comp][:, SLOT * s:SLOT * s + 1], fields[comp])
    lane_z = grid_lane // GX
    lane_x = grid_lane % GX
    for comp in range(3):
        field = fields[comp]
        near = jnp.where(lane_z >= 1, pltpu.roll(field, GX, 1), 0.0)
        near = near + jnp.where(lane_z < GZX // GX - 1, pltpu.roll(field, LANES - GX, 1), 0.0)
        near = near + jnp.where(lane_x >= 1, pltpu.roll(field, 1, 1), 0.0)
        near = near + jnp.where(lane_x < GX - 1, pltpu.roll(field, LANES - 1, 1), 0.0)
        near = near[1:1 + tile_rows] + field[0:tile_rows] + field[2:2 + tile_rows]
        out_ref[:, comp, :] = 0.4 * field[1:1 + tile_rows] + 0.1 * near


def shards(first, second, windows, shifts):
    planes, deep, along = first.shape
    own = windows.shape[0]
    slots = 3 * own + 1
    count = lax.axis_size("span")
    pairs = [(i, i ^ 1) for i in range(count)]
    others = [(i, i + 1) for i in range(1, count - 1, 2)]
    others = others + [(b, a) for a, b in others]
    vmem = pl.BlockSpec(memory_space=pltpu.VMEM)

    def limit(mib):
        return pltpu.CompilerParams(vmem_limit_bytes=mib << 20)

    busy = pl.CostEstimate(flops=20 * 10**9, bytes_accessed=0, transcendentals=0)
    low_planes, high_planes = second[:REACH], second[planes - REACH:]
    gap = pl.pallas_call(
        table_kernel,
        out_shape=jax.ShapeDtypeStruct((ROWS_A, 2 * LANES), jnp.int32),
        in_specs=[vmem],
        out_specs=vmem,
        compiler_params=limit(4),
        cost_estimate=busy,
        name="gap_table",
    )(low_planes)
    message = jax.ShapeDtypeStruct((REACH * deep + PLAN_ROWS, along), second.dtype)
    to_pair, to_other, plan = pl.pallas_call(
        send_kernel,
        out_shape=(message, message, jax.ShapeDtypeStruct((8, LANES), jnp.int32)),
        in_specs=[vmem] * 5,
        out_specs=(vmem,) * 3,
        compiler_params=limit(4),
        cost_estimate=busy,
        name="planes_to_send",
    )(windows[None], shifts, gap, low_planes, high_planes)
    from_other = lax.ppermute(to_other, "span", others)
    from_pair = lax.ppermute(to_pair, "span", pairs)
    mask_rows = 2 * (ROWS_A + ROWS_B + 16)
    far = W // 2 - STRIDE // 2
    state = (
        jax.ShapeDtypeStruct((slots, 3 * ROWS_A + 16, 2 * LANES), jnp.float32),
        jax.ShapeDtypeStruct((slots, ROWS_A, LANES), jnp.float32),
        jax.ShapeDtypeStruct((slots, ROWS_B, LANES), jnp.float32),
    )
    held = (
        jax.ShapeDtypeStruct((2, 2, 2 * far, deep, LANES), jnp.bfloat16),
        jax.ShapeDtypeStruct((2, 2, 2 * (far + REACH), deep, LANES), jnp.bfloat16),
        jax.ShapeDtypeStruct((own, mask_rows, LANES), jnp.bfloat16),
    )
    scratch = [
        pltpu.VMEM((2, 2, planes + 2 * PAD_A, deep, LANES), jnp.bfloat16),
        pltpu.VMEM((2, 2, planes + 2 * PAD_B, deep, LANES), jnp.bfloat16),
        pltpu.VMEM((slots, mask_rows, LANES), jnp.bfloat16),
        pltpu.VMEM((FIELDS, LANES), jnp.int32),
        pltpu.SMEM((FIELDS, LANES), jnp.int32),
        pltpu.SMEM((3 * own * (W // CHUNK) + PAIR,), jnp.int32),
    ]
    held = pl.pallas_call(
        inner_kernel,
        out_shape=(*held, *state),
        in_specs=[vmem] * 3,
        out_specs=(vmem,) * 6,
        scratch_shapes=[
            *scratch,
            pltpu.SemaphoreType.DMA,
            pltpu.SemaphoreType.DMA((5,)),
        ],
        compiler_params=limit(20),
        cost_estimate=busy,
        name="inner_sums",
    )(plan, first, second)
    sums, *_ = pl.pallas_call(
        outer_kernel,
        out_shape=(jax.ShapeDtypeStruct((24, LANES), jnp.float32), *state),
        in_specs=[vmem] * 10,
        out_specs=(vmem,) * 4,
        input_output_aliases={7 + i: 1 + i for i in range(3)},
        scratch_shapes=[
            *scratch,
            pltpu.SMEM((slots + CLOSE,), jnp.int32),
            pltpu.SemaphoreType.DMA,
            pltpu.SemaphoreType.DMA((5,)),
        ],
        compiler_params=limit(20),
        name="outer_sums",
    )(plan, from_pair, from_other, gap, *held)
    other_sums = lax.ppermute(sums, "span", others)
    pair_sums = lax.ppermute(sums, "span", pairs)
    field = pl.pallas_call(
        functools.partial(update_kernel, own),
        out_shape=jax.ShapeDtypeStruct((planes // STRIDE, 3, GZX), jnp.float32),
        in_specs=[vmem] * 3,
        out_specs=vmem,
        compiler_params=limit(4),
        name="smoothed_update",
    )(sums, pair_sums, other_sums)
    return jnp.transpose(field, (1, 0, 2))


def solution(mesh):
    in_specs = (
        P(("grp", "span"), None, None),
        P(("grp", "span"), None, None),
        P(("grp", "span")),
        P(None, ("grp", "span")),
    )
    out_specs = P(None, ("grp", "span"), None)
    return jax.shard_map(shards, mesh=mesh, in_specs=in_specs, out_specs=out_specs, check_vma=False)
```

```python
import functools

import jax
import jax.numpy as jnp
from jax import lax
from jax.experimental import pallas as pl
from jax.experimental.pallas import tpu as pltpu
from jax.sharding import PartitionSpec as P

W = 48
STRIDE = 12
DYM = 3
GX = 16
GZX = 128
SHARP = 80.0
EPSILON = 1e-06

HALF = W // 2
BLOCK = W + 2
REACH = DYM + 1
LANES = 128
HOP = 64
CHUNK = 6
ROWS_A = 64
ROWS_B = 80
PAD_A = CHUNK
PAD_B = CHUNK + REACH
PIECES = 2
SLOT = 4
PLAN_ROWS = 16
FIELDS = 24
PAIR = 8
REST = 4
CLOSE = 2
FAR = 4096


def table_kernel(gap_ref):
    row = lax.broadcasted_iota(jnp.int32, gap_ref.shape, 0)
    col = lax.broadcasted_iota(jnp.int32, gap_ref.shape, 1)
    lag = jnp.where(col >= ROWS_B, 1, 0) + jnp.where(col >= 2 * ROWS_B, 1, 0)
    gap_ref[...] = jnp.where(col < 3 * ROWS_B, col - lag * ROWS_B - row, FAR)


def send_kernel(win_ref, shift_ref, gap_ref, low_ref, high_ref, pair_ref, other_ref, plan_ref):
    reach, deep, along = low_ref.shape
    even = lax.axis_index("span") % 2 == 0
    node = win_ref[...]
    own = node.shape[1]
    plan_ref[...] = jnp.zeros(plan_ref.shape, jnp.int32)
    plan_ref[0:1, 0:own] = node >> 8
    plan_ref[1:2, 0:own] = node & 255
    plan_ref[2:5, 0:own] = shift_ref[...]
    plan = plan_ref[...].astype(jnp.float32).astype(jnp.bfloat16)
    for ref in (pair_ref, other_ref):
        ref[reach * deep:reach * deep + 8, 0:LANES] = plan

    def fill(to_low, to_high):
        for p in range(reach):
            to_low[p * deep:(p + 1) * deep, :] = low_ref[p]
            to_high[p * deep:(p + 1) * deep, :] = high_ref[p]

    @pl.when(even)
    def _():
        fill(other_ref, pair_ref)

    @pl.when(jnp.logical_not(even))
    def _():
        fill(pair_ref, other_ref)


def decode(plan, own, planes, deep, inner, table):
    device = lax.axis_index("span")
    last = lax.axis_size("span") - 1
    tile_rows = planes // STRIDE
    slot = lax.broadcasted_iota(jnp.int32, (1, LANES), 1)
    node = plan[0:1] * 256 + plan[1:2]
    dy, dz, dx = plan[2:3], plan[3:4], plan[4:5]
    row = (node >> (GZX.bit_length() - 1)) - device * tile_rows
    rest = node & (GZX - 1)
    cy = STRIDE * row + STRIDE // 2
    cz = STRIDE * (rest >> (GX.bit_length() - 1)) + STRIDE // 2
    cx = STRIDE * (rest & (GX - 1)) + STRIDE // 2
    start = jnp.maximum(cy - HALF, jnp.where(device == 0, -CHUNK, 0))
    stop = jnp.minimum(cy + HALF, jnp.where(device == last, planes + CHUNK, planes))
    mine = slot < own
    lower = (slot >= own) & (slot < 2 * own)
    upper = (slot >= 2 * own) & (slot < 3 * own)
    wanted = (
        mine | (lower & (row < 0) & (row >= -tile_rows))
        | (upper & (row >= tile_rows) & (row < 2 * tile_rows))
    )
    if inner:
        low = jnp.maximum(start, CHUNK)
        high = jnp.minimum(stop, planes - CHUNK)
        wanted = mine
    else:
        below = start < CHUNK
        low = jnp.where(mine & jnp.logical_not(below), planes - CHUNK, start)
        high = jnp.where(mine & below, CHUNK, stop)
    width = jnp.where(wanted, high - low, 0)
    count = sum([jnp.where(width > CHUNK * c, 1, 0) for c in range(W // CHUNK)])
    sx = cx + dx - HALF - 1
    sz = cz + dz - HALF - 1
    z_a = jnp.minimum(jnp.maximum(cz - HALF, 0) & -16, deep - ROWS_A)
    z_b = jnp.where(sz + BLOCK <= ROWS_B, 0, deep - ROWS_B)
    values = (
        jnp.where(cx + HALF <= LANES, 0, 1),
        z_a,
        jnp.where(sx + BLOCK <= LANES, 0, 1),
        z_b,
        dy,
        z_a + dz - z_b,
        (dx + LANES) & (LANES - 1),
        cz - HALF - z_a,
        start + dy - 1 + PAD_B,
        stop + dy + PAD_B,
        jnp.where(start == cy - HALF, 1, 0),
        jnp.where(stop == cy + HALF, 1, 0),
        low,
        count,
        cx - HALF,
        sx,
        sz - z_b,
    )
    for at, value in enumerate(values):
        table[at:at + 1, :] = jnp.where(slot < 3 * own, value, 0)
    return jnp.where(
        mine | (lower & (row == -1)) | (upper & (row == tile_rows)),
        (row + 1) * GZX + rest, -1)


def set_masks(masks, s, table):
    f_a, f_b = table[0, s], table[2, s]
    z_from, x_from = table[7, s], table[14, s]
    sx, zb_from = table[15, s], table[16, s]
    reach_x = sx + 1

    def in_x(rows, half, frame_at, low, high):
        lane = (lax.broadcasted_iota(jnp.int32, (rows, LANES), 1) + half * HOP) & (LANES - 1)
        x = lane + jnp.where(lane < HOP, LANES * frame_at, 0)
        return (x >= low) & (x < high)

    def in_z(rows, low, count):
        z = lax.broadcasted_iota(jnp.int32, (rows, LANES), 0)
        return (z >= low) & (z < low + count)

    row = lax.broadcasted_iota(jnp.int32, (16, LANES), 0)
    wide = row == 3
    low = jnp.where(wide, sx, reach_x + row - 1)
    high = low + jnp.where(wide, BLOCK, jnp.where(row < 3, W, 0))
    z_a = in_z(ROWS_A, z_from, W)
    z_b = in_z(ROWS_B, zb_from, BLOCK)
    at = 0
    for rows, frame_at, x_low, x_high, z in (
        (ROWS_A, f_a, x_from, x_from + W, z_a),
        (ROWS_B, f_b, sx, sx + BLOCK, z_b),
        (16, f_b, low, high, None),
    ):
        for half in range(2):
            inside = in_x(rows, half, frame_at, x_low, x_high)
            inside = inside if z is None else inside & z
            masks[s, at:at + rows] = jnp.where(inside, 1.0, 0.0).astype(jnp.bfloat16)
            at += rows


def set_units(units, total, s, low, planes, most):
    for c in range(most):
        units[total + c] = s + (low + planes * c + 64) * 256


def frame(v, fr, at):
    low = v[:, :LANES]
    high = jnp.concatenate([v[:, LANES:], v[:, HOP:LANES]], axis=1)
    fr[0, 0, at] = low
    fr[0, 1, at] = high
    fr[1, 0, at] = pltpu.roll(low, HOP, 1)
    fr[1, 1, at] = pltpu.roll(high, HOP, 1)


def run_units(half, total, units, table, spare, fr_a, fr_b, acc, sq_a, sq_b, masks):
    for at in range(REST - 1):
        units[total + at] = spare + 64 * 256
    ones = jnp.where(
        lax.broadcasted_iota(jnp.int32, (16, half * LANES), 0) == 0, 1.0, 0.0
    ).astype(jnp.bfloat16)

    def step(first, width):
        for h in range(width):
            code = units[first + h]
            s = code & 255
            y = (code >> 8) - 64
            y_two = y + half
            f_a = table[0, s]
            z_a = pl.multiple_of(table[1, s], 16)
            f_b = table[2, s]
            z_b = pl.multiple_of(table[3, s], 16)
            dy = table[4, s]
            dx = table[6, s]
            one_a = masks[s, 0:ROWS_A]
            two_a = masks[s, ROWS_A:2 * ROWS_A]
            at = 2 * ROWS_A
            one_b = masks[s, at:at + ROWS_B]
            two_b = masks[s, at + ROWS_B:at + 2 * ROWS_B]
            at += 2 * ROWS_B
            rows = masks[s, at:at + 16] + masks[s, at + 16:at + 32]
            a = [
                fr_a[0, f_a, y + PAD_A + p, pl.ds(z_a, ROWS_A), :] * one_a
                + fr_a[1, f_a, y_two + PAD_A + p, pl.ds(z_a, ROWS_A), :] * two_a
                for p in range(half)
            ]
            b = [
                fr_b[0, f_b, y + dy - 1 + PAD_B + p, pl.ds(z_b, ROWS_B), :] * one_b
                + fr_b[1, f_b, y_two + dy - 1 + PAD_B + p, pl.ds(z_b, ROWS_B), :] * two_b
                for p in range(half + 2)
            ]
            left = [
                jnp.concatenate(
                    [pltpu.roll(v, (dx + lag - 1 + LANES) & (LANES - 1), 1) for v in a], axis=1)
                for lag in range(3)
            ]
            left.append(jnp.concatenate([rows] * half, axis=1))
            left = jnp.concatenate(left, axis=0)
            right = [jnp.concatenate(b[lag:lag + half], axis=1) for lag in range(3)]
            right = jnp.concatenate(right + [ones], axis=0)
            acc[s] += lax.dot_general(
                left, right, (((1,), (1,)), ((), ())), preferred_element_type=jnp.float32)
            wide = [v.astype(jnp.float32) for v in a]
            sq_a[s] += sum([v * v for v in wide])
            wide = [v.astype(jnp.float32) for v in b[1:-1]]
            sq_b[s] += sum([v * v for v in wide])

    def wide_step(t, carry):
        step(PAIR * t, PAIR)
        return carry

    full = (total + REST - 1) // PAIR
    lax.fori_loop(0, full, wide_step, 0)

    @pl.when(total > PAIR * full)
    def _():
        step(PAIR * full, REST)


def edge_copies(edge_a, edge_b, fr_a, fr_b, planes, sem):
    far_a = edge_a.shape[2] // 2
    far_b = edge_b.shape[2] // 2
    return (
        (fr_a.at[:, :, pl.ds(PAD_A, far_a)], edge_a.at[:, :, pl.ds(0, far_a)], sem.at[0]),
        (fr_a.at[:, :, pl.ds(PAD_A + planes - far_a, far_a)],
         edge_a.at[:, :, pl.ds(far_a, far_a)], sem.at[1]),
        (fr_b.at[:, :, pl.ds(PAD_B, far_b)], edge_b.at[:, :, pl.ds(0, far_b)], sem.at[2]),
        (fr_b.at[:, :, pl.ds(PAD_B + planes - far_b, far_b)],
         edge_b.at[:, :, pl.ds(far_b, far_b)], sem.at[3]),
    )


def inner_kernel(
    plan_ref, first_ref, second_ref, edge_a, edge_b, edge_masks, acc, sq_a, sq_b,
    fr_a, fr_b, masks, table_v, table, units, sem_t, sem_e,
):
    planes, deep, along = first_ref.shape
    own = (acc.shape[0] - 1) // 3
    piece = planes // PIECES
    decode(plan_ref[...], own, planes, deep, True, table_v)
    to_scalar = pltpu.make_async_copy(table_v, table, sem_t)
    to_scalar.start()
    for ref, fr, pad in ((first_ref, fr_a, PAD_A), (second_ref, fr_b, PAD_B)):
        def body(i, carry, ref=ref, fr=fr, pad=pad):
            for p in range(piece):
                at = i * piece + p
                frame(ref[at], fr, at + pad)
            return carry

        lax.fori_loop(0, PIECES, body, 0)

    hand_on = [
        pltpu.make_async_copy(source, target, sem)
        for source, target, sem in edge_copies(edge_a, edge_b, fr_a, fr_b, planes, sem_e)
    ]
    for c in hand_on:
        c.start()
    to_scalar.wait()

    def prepare(s, total):
        set_masks(masks, s, table)
        for ref in (acc, sq_a, sq_b):
            ref[s] = jnp.zeros(ref.shape[1:], jnp.float32)
        set_units(units, total, s, table[12, s], 2 * CHUNK, W // CHUNK // 2)
        return total + (table[13, s] >> 1)

    total = lax.fori_loop(0, own, prepare, 0)
    masks_on = pltpu.make_async_copy(masks.at[pl.ds(0, own)], edge_masks, sem_e.at[4])
    masks_on.start()
    run_units(CHUNK, total, units, table, 3 * own, fr_a, fr_b, acc, sq_a, sq_b, masks)
    for c in hand_on:
        c.wait()
    masks_on.wait()


def outer_kernel(
    plan_ref, pair_ref, other_ref, gap_base, edge_a, edge_b, edge_masks, acc_in, sq_a_in, sq_b_in,
    out_ref, acc, sq_a, sq_b,
    fr_a, fr_b, masks, table_v, table, units, active, sem_t, sem_e,
):
    deep = fr_a.shape[3]
    planes = fr_a.shape[2] - 2 * PAD_A
    own = (acc.shape[0] - 1) // 3
    device = lax.axis_index("span")
    last = lax.axis_size("span") - 1
    even = device % 2 == 0
    base = REACH * deep
    bring_in = [
        pltpu.make_async_copy(source, target, sem)
        for target, source, sem in edge_copies(edge_a, edge_b, fr_a, fr_b, planes, sem_e)
    ] + [pltpu.make_async_copy(edge_masks, masks.at[pl.ds(0, own)], sem_e.at[4])]
    for c in bring_in:
        c.start()
    from_pair, from_other = [
        ref[base:base + 8, 0:LANES].astype(jnp.float32).astype(jnp.int32)
        for ref in (pair_ref, other_ref)
    ]
    below = jnp.where(even, from_other, from_pair)
    above = jnp.where(even, from_pair, from_other)
    plan = plan_ref[...] + pltpu.roll(below, own, 1) + pltpu.roll(above, 2 * own, 1)
    target = decode(plan, own, planes, deep, False, table_v)
    to_scalar = pltpu.make_async_copy(table_v, table, sem_t)
    to_scalar.start()
    out_ref[...] = jnp.zeros(out_ref.shape, jnp.float32)
    out_ref[22:23] = target.astype(jnp.float32)

    @pl.when((device == 0) | (device == last))
    def _():
        zero = jnp.zeros((2, 2, CHUNK, deep, LANES), jnp.bfloat16)
        fr_a[:, :, 0:PAD_A] = zero
        fr_a[:, :, PAD_A + planes:] = zero
        fr_b[:, :, 0:CHUNK] = zero
        fr_b[:, :, PAD_B + planes + REACH:] = zero

    low_at, high_at = CHUNK, PAD_B + planes
    pair_at = jnp.where(even, high_at, low_at)
    other_at = jnp.where(even, low_at, high_at)
    for p in range(REACH):
        frame(pair_ref[p * deep:(p + 1) * deep, :], fr_b, pair_at + p)
        frame(other_ref[p * deep:(p + 1) * deep, :], fr_b, other_at + p)
    to_scalar.wait()

    def prepare_own(s, total):
        active[s] = s
        set_units(units, total, s, table[12, s], CHUNK, 2)
        return total + table[13, s]

    total = lax.fori_loop(0, own, prepare_own, 0)
    for c in bring_in:
        c.wait()

    def prepare(s, carry):
        total, alive = carry
        count = table[13, s]

        @pl.when(count > 0)
        def _():
            set_masks(masks, s, table)
            for ref in (acc, sq_a, sq_b):
                ref[s] = jnp.zeros(ref.shape[1:], jnp.float32)
            active[alive] = s
            set_units(units, total, s, table[12, s], CHUNK, W // CHUNK)

        return total + count, alive + jnp.where(count > 0, 1, 0)

    total, alive = lax.fori_loop(own, 3 * own, prepare, (total, own))
    spare = 3 * own
    for at in range(CLOSE - 1):
        active[alive + at] = spare
    run_units(CHUNK // 2, total, units, table, spare, fr_a, fr_b, acc, sq_a, sq_b, masks)

    cols = 2 * LANES
    col_one = lax.broadcasted_iota(jnp.int32, (1, cols), 1)
    lag_one = jnp.where(col_one >= ROWS_B, 1, 0) + jnp.where(col_one >= 2 * ROWS_B, 1, 0)
    lag_one = lag_one + jnp.where(col_one >= 3 * ROWS_B, 1, 0)
    z_one = col_one - lag_one * ROWS_B
    lag_18 = jnp.broadcast_to(lag_one, (18, cols))
    lane_18 = lax.broadcasted_iota(jnp.int32, (18, LANES), 1)
    lane_4 = lax.broadcasted_iota(jnp.int32, (4, LANES), 1)
    slant = lax.broadcasted_iota(jnp.int32, (8, cols), 1)
    slant = slant - lax.broadcasted_iota(jnp.int32, (8, cols), 0)
    mean_lane = lax.broadcasted_iota(jnp.int32, (1, LANES), 1) == 3 * ROWS_B - LANES

    def finish(t, carry):
        for h in range(CLOSE):
            s = active[CLOSE * t + h]
            f_b = table[2, s]
            z_b = pl.multiple_of(table[3, s], 16)
            offset = table[5, s]
            low_z = table[16, s] + 1
            band = (gap_base[...] >= offset - 1) & (gap_base[...] <= offset + 1)
            tops = [None] * 9
            lows = []
            for lag_x in range(3):
                part = jnp.where(band, acc[s, lag_x * ROWS_A:(lag_x + 1) * ROWS_A, :], 0.0)
                part = sum([part[8 * i:8 * i + 8] for i in range(ROWS_A // 8)])
                for lag_z in range(3):
                    hit = ((slant - (offset + lag_z - 1)) & 7) == 0
                    tops[3 * lag_z + lag_x] = jnp.sum(
                        jnp.where(hit, part, 0.0), axis=0, keepdims=True)
            for lag_z in range(3):
                low = low_z + lag_z - 1
                inside = (z_one >= low) & (z_one < low + W)
                lows.append(jnp.where(inside, acc[s, 3 * ROWS_A:3 * ROWS_A + 3, :], 0.0))
            stack = jnp.concatenate(tops + lows, axis=0)

            at = 2 * ROWS_A
            mask = masks[s, at:at + ROWS_B].astype(jnp.float32)
            ends = [
                fr_b[0, f_b, table[8 + i, s], pl.ds(z_b, ROWS_B), :].astype(jnp.float32)
                * (mask * table[10 + i, s].astype(jnp.float32))
                for i in range(2)
            ]
            row_b = jnp.where(
                lag_one == 1, acc[s, 3 * ROWS_A + 3:3 * ROWS_A + 4, :], 0.0)
            row_a = jnp.sum(acc[s, ROWS_A:2 * ROWS_A, LANES:], axis=0, keepdims=True)
            sums = [
                jnp.where(mean_lane, row_a, 0.0),
                jnp.sum(sq_a[s], axis=0, keepdims=True),
                jnp.sum(ends[0] + ends[1], axis=0, keepdims=True)
                + row_b[:, :LANES] + row_b[:, LANES:],
                jnp.sum(
                    sq_b[s] + (ends[0] * ends[0] + ends[1] * ends[1]), axis=0, keepdims=True),
            ]
            sums = jnp.sum(jnp.concatenate(sums, axis=0), axis=1, keepdims=True)
            total_18 = jnp.zeros((18, LANES), jnp.float32)
            for lag_y in range(3):
                part = jnp.sum(jnp.where(lag_18 == lag_y, stack, 0.0), axis=1, keepdims=True)
                total_18 = total_18 + jnp.where(lane_18 == SLOT * s + lag_y, part, 0.0)
            out_ref[0:18] += total_18
            out_ref[18:22] += jnp.where(lane_4 == SLOT * s, sums, 0.0)
        return carry

    lax.fori_loop(0, (alive + CLOSE - 1) // CLOSE, finish, 0)


def update_kernel(own, mine_ref, pair_ref, other_ref, out_ref):
    tile_rows = out_ref.shape[0]
    even = lax.axis_index("span") % 2 == 0
    mine = mine_ref[...]
    pair = pair_ref[...]
    other = other_ref[...]
    below = jnp.where(even, other, pair)
    above = jnp.where(even, pair, other)
    span = SLOT * own
    lane = lax.broadcasted_iota(jnp.int32, mine.shape, 1)
    total = mine
    total = total + jnp.where(
        lane < span,
        pltpu.roll(below, LANES - 2 * span, 1) + pltpu.roll(above, LANES - span, 1),
        jnp.where(
            lane < 2 * span, pltpu.roll(below, span, 1),
            jnp.where(lane < 3 * span, pltpu.roll(above, 2 * span, 1), 0.0)))

    def lead(v):
        return v + pltpu.roll(v, LANES - 1, 1) + pltpu.roll(v, LANES - 2, 1)

    def spread(v):
        return v + pltpu.roll(v, 1, 1) + pltpu.roll(v, 2, 1)

    lag_lane = lane % SLOT
    stats = spread(jnp.where(lag_lane[0:4] == 0, total[18:22], 0.0))
    voxels = float(W) ** 3
    block_voxels = float(BLOCK) ** 3
    mean_a = stats[0:1] / voxels
    energy_a = jnp.maximum(stats[1:2] / voxels - mean_a * mean_a, 0.0)
    mean_b = stats[2:3] / block_voxels
    energy_b = jnp.maximum(stats[3:4] / block_voxels - mean_b * mean_b, 0.0)
    normaliser = voxels * jnp.sqrt((energy_a + EPSILON) * (energy_b + EPSILON))
    scaled = SHARP * ((total[0:9] - mean_a * total[9:18]) / normaliser)
    used = lag_lane[0:9] < 3
    scaled = jnp.where(used, scaled, -1e30)
    top = jnp.max(scaled, axis=0, keepdims=True)
    top = jnp.maximum(top, jnp.maximum(pltpu.roll(top, LANES - 1, 1), pltpu.roll(top, LANES - 2, 1)))
    top = spread(jnp.where(lag_lane[0:1] == 0, top, 0.0))
    weights = jnp.where(used, jnp.exp(scaled - top), 0.0)
    lag_row = lax.broadcasted_iota(jnp.int32, weights.shape, 0)
    lag_z = (lag_row // 3 - 1).astype(jnp.float32)
    lag_x = (lag_row % 3 - 1).astype(jnp.float32)
    column = jnp.sum(weights, axis=0, keepdims=True)
    weight_sum = lead(column)
    along_y = lead(column * (lag_lane[0:1] - 1).astype(jnp.float32)) / weight_sum
    along_z = lead(jnp.sum(weights * lag_z, axis=0, keepdims=True)) / weight_sum
    along_x = lead(jnp.sum(weights * lag_x, axis=0, keepdims=True)) / weight_sum
    corrections = (along_y, along_z, along_x)

    grid_lane = lax.broadcasted_iota(jnp.int32, (8, LANES), 1)
    place = lax.broadcasted_iota(jnp.int32, (8, LANES), 0) * GZX + grid_lane
    target = mine[22:23].astype(jnp.int32)
    fields = [jnp.zeros((8, LANES), jnp.float32) for _ in range(3)]
    for s in range(3 * own):
        hit = place == target[:, s:s + 1]
        for comp in range(3):
            fields[comp] = jnp.where(
                hit, corrections[comp][:, SLOT * s:SLOT * s + 1], fields[comp])
    lane_z = grid_lane // GX
    lane_x = grid_lane % GX
    for comp in range(3):
        field = fields[comp]
        near = jnp.where(lane_z >= 1, pltpu.roll(field, GX, 1), 0.0)
        near = near + jnp.where(lane_z < GZX // GX - 1, pltpu.roll(field, LANES - GX, 1), 0.0)
        near = near + jnp.where(lane_x >= 1, pltpu.roll(field, 1, 1), 0.0)
        near = near + jnp.where(lane_x < GX - 1, pltpu.roll(field, LANES - 1, 1), 0.0)
        near = near[1:1 + tile_rows] + field[0:tile_rows] + field[2:2 + tile_rows]
        out_ref[:, comp, :] = 0.4 * field[1:1 + tile_rows] + 0.1 * near


def shards(first, second, windows, shifts):
    planes, deep, along = first.shape
    own = windows.shape[0]
    slots = 3 * own + 1
    count = lax.axis_size("span")
    pairs = [(i, i ^ 1) for i in range(count)]
    others = [(i, i + 1) for i in range(1, count - 1, 2)]
    others = others + [(b, a) for a, b in others]
    vmem = pl.BlockSpec(memory_space=pltpu.VMEM)

    def limit(mib):
        return pltpu.CompilerParams(vmem_limit_bytes=mib << 20)

    busy = pl.CostEstimate(flops=20 * 10**9, bytes_accessed=0, transcendentals=0)
    gap = pl.pallas_call(
        table_kernel,
        out_shape=jax.ShapeDtypeStruct((ROWS_A, 2 * LANES), jnp.int32),
        out_specs=vmem,
        compiler_params=limit(4),
        cost_estimate=pl.CostEstimate(flops=800000000, bytes_accessed=0, transcendentals=0),
        name="gap_table",
    )()
    message = jax.ShapeDtypeStruct((REACH * deep + PLAN_ROWS, along), second.dtype)
    tile, gap = lax.optimization_barrier((second, gap))
    low_planes, high_planes = tile[:REACH], tile[planes - REACH:]
    to_pair, to_other, plan = pl.pallas_call(
        send_kernel,
        out_shape=(message, message, jax.ShapeDtypeStruct((8, LANES), jnp.int32)),
        in_specs=[vmem] * 5,
        out_specs=(vmem,) * 3,
        compiler_params=limit(4),
        cost_estimate=busy,
        name="planes_to_send",
    )(windows[None], shifts, gap, low_planes, high_planes)
    from_other = lax.ppermute(to_other, "span", others)
    from_pair = lax.ppermute(to_pair, "span", pairs)
    mask_rows = 2 * (ROWS_A + ROWS_B + 16)
    far = W // 2 - STRIDE // 2
    state = (
        jax.ShapeDtypeStruct((slots, 3 * ROWS_A + 16, 2 * LANES), jnp.float32),
        jax.ShapeDtypeStruct((slots, ROWS_A, LANES), jnp.float32),
        jax.ShapeDtypeStruct((slots, ROWS_B, LANES), jnp.float32),
    )
    held = (
        jax.ShapeDtypeStruct((2, 2, 2 * far, deep, LANES), jnp.bfloat16),
        jax.ShapeDtypeStruct((2, 2, 2 * (far + REACH), deep, LANES), jnp.bfloat16),
        jax.ShapeDtypeStruct((own, mask_rows, LANES), jnp.bfloat16),
    )
    scratch = [
        pltpu.VMEM((2, 2, planes + 2 * PAD_A, deep, LANES), jnp.bfloat16),
        pltpu.VMEM((2, 2, planes + 2 * PAD_B, deep, LANES), jnp.bfloat16),
        pltpu.VMEM((slots, mask_rows, LANES), jnp.bfloat16),
        pltpu.VMEM((FIELDS, LANES), jnp.int32),
        pltpu.SMEM((FIELDS, LANES), jnp.int32),
        pltpu.SMEM(((3 * own + 1) * (W // CHUNK) + PAIR,), jnp.int32),
    ]
    held = pl.pallas_call(
        inner_kernel,
        out_shape=(*held, *state),
        in_specs=[vmem] * 3,
        out_specs=(vmem,) * 6,
        scratch_shapes=[
            *scratch,
            pltpu.SemaphoreType.DMA,
            pltpu.SemaphoreType.DMA((5,)),
        ],
        compiler_params=limit(20),
        cost_estimate=busy,
        name="inner_sums",
    )(plan, first, second)
    sums, *_ = pl.pallas_call(
        outer_kernel,
        out_shape=(jax.ShapeDtypeStruct((24, LANES), jnp.float32), *state),
        in_specs=[vmem] * 10,
        out_specs=(vmem,) * 4,
        input_output_aliases={7 + i: 1 + i for i in range(3)},
        scratch_shapes=[
            *scratch,
            pltpu.SMEM((slots + CLOSE,), jnp.int32),
            pltpu.SemaphoreType.DMA,
            pltpu.SemaphoreType.DMA((5,)),
        ],
        compiler_params=limit(20),
        name="outer_sums",
    )(plan, from_pair, from_other, gap, *held)
    other_sums = lax.ppermute(sums, "span", others)
    pair_sums = lax.ppermute(sums, "span", pairs)
    field = pl.pallas_call(
        functools.partial(update_kernel, own),
        out_shape=jax.ShapeDtypeStruct((planes // STRIDE, 3, GZX), jnp.float32),
        in_specs=[vmem] * 3,
        out_specs=vmem,
        compiler_params=limit(4),
        name="smoothed_update",
    )(sums, pair_sums, other_sums)
    return jnp.transpose(field, (1, 0, 2))


def solution(mesh):
    in_specs = (
        P(("grp", "span"), None, None),
        P(("grp", "span"), None, None),
        P(("grp", "span")),
        P(None, ("grp", "span")),
    )
    out_specs = P(None, ("grp", "span"), None)
    return jax.shard_map(shards, mesh=mesh, in_specs=in_specs, out_specs=out_specs, check_vma=False)
```

```python
import functools

import jax
import jax.numpy as jnp
from jax import lax
from jax.experimental import pallas as pl
from jax.experimental.pallas import tpu as pltpu
from jax.sharding import PartitionSpec as P

W = 48
STRIDE = 12
DYM = 3
GX = 16
GZX = 128
SHARP = 80.0
EPSILON = 1e-06

HALF = W // 2
BLOCK = W + 2
REACH = DYM + 1
LANES = 128
HOP = 64
CHUNK = 6
ROWS_A = 64
ROWS_B = 80
PAD_A = CHUNK
PAD_B = CHUNK + REACH
PIECES = 2
SLOT = 4
PLAN_ROWS = 16
FIELDS = 24
PAIR = 8
REST = 4
CLOSE = 2
FAR = 4096


def table_kernel(gap_ref):
    row = lax.broadcasted_iota(jnp.int32, gap_ref.shape, 0)
    col = lax.broadcasted_iota(jnp.int32, gap_ref.shape, 1)
    lag = jnp.where(col >= ROWS_B, 1, 0) + jnp.where(col >= 2 * ROWS_B, 1, 0)
    gap_ref[...] = jnp.where(col < 3 * ROWS_B, col - lag * ROWS_B - row, FAR)


def send_kernel(win_ref, shift_ref, gap_ref, low_ref, high_ref, pair_ref, other_ref, plan_ref):
    reach, deep, along = low_ref.shape
    even = lax.axis_index("span") % 2 == 0
    node = win_ref[...]
    own = node.shape[1]
    plan_ref[...] = jnp.zeros(plan_ref.shape, jnp.int32)
    plan_ref[0:1, 0:own] = node >> 8
    plan_ref[1:2, 0:own] = node & 255
    plan_ref[2:5, 0:own] = shift_ref[...]
    plan = plan_ref[...].astype(jnp.float32).astype(jnp.bfloat16)
    for ref in (pair_ref, other_ref):
        ref[reach * deep:reach * deep + 8, 0:LANES] = plan

    def fill(to_low, to_high):
        for p in range(reach):
            to_low[p * deep:(p + 1) * deep, :] = low_ref[p]
            to_high[p * deep:(p + 1) * deep, :] = high_ref[p]

    @pl.when(even)
    def _():
        fill(other_ref, pair_ref)

    @pl.when(jnp.logical_not(even))
    def _():
        fill(pair_ref, other_ref)


def decode(plan, own, planes, deep, inner, table):
    device = lax.axis_index("span")
    last = lax.axis_size("span") - 1
    tile_rows = planes // STRIDE
    slot = lax.broadcasted_iota(jnp.int32, (1, LANES), 1)
    node = plan[0:1] * 256 + plan[1:2]
    dy, dz, dx = plan[2:3], plan[3:4], plan[4:5]
    row = (node >> (GZX.bit_length() - 1)) - device * tile_rows
    rest = node & (GZX - 1)
    cy = STRIDE * row + STRIDE // 2
    cz = STRIDE * (rest >> (GX.bit_length() - 1)) + STRIDE // 2
    cx = STRIDE * (rest & (GX - 1)) + STRIDE // 2
    start = jnp.maximum(cy - HALF, jnp.where(device == 0, -CHUNK, 0))
    stop = jnp.minimum(cy + HALF, jnp.where(device == last, planes + CHUNK, planes))
    mine = slot < own
    lower = (slot >= own) & (slot < 2 * own)
    upper = (slot >= 2 * own) & (slot < 3 * own)
    wanted = (
        mine | (lower & (row < 0) & (row >= -tile_rows))
        | (upper & (row >= tile_rows) & (row < 2 * tile_rows))
    )
    if inner:
        low = jnp.maximum(start, CHUNK)
        high = jnp.minimum(stop, planes - CHUNK)
        wanted = mine
    else:
        below = start < CHUNK
        low = jnp.where(mine & jnp.logical_not(below), planes - CHUNK, start)
        high = jnp.where(mine & below, CHUNK, stop)
    width = jnp.where(wanted, high - low, 0)
    count = sum([jnp.where(width > CHUNK * c, 1, 0) for c in range(W // CHUNK)])
    sx = cx + dx - HALF - 1
    sz = cz + dz - HALF - 1
    z_a = jnp.minimum(jnp.maximum(cz - HALF, 0) & -16, deep - ROWS_A)
    z_b = jnp.where(sz + BLOCK <= ROWS_B, 0, deep - ROWS_B)
    values = (
        jnp.where(cx + HALF <= LANES, 0, 1),
        z_a,
        jnp.where(sx + BLOCK <= LANES, 0, 1),
        z_b,
        dy,
        z_a + dz - z_b,
        (dx + LANES) & (LANES - 1),
        cz - HALF - z_a,
        start + dy - 1 + PAD_B,
        stop + dy + PAD_B,
        jnp.where(start == cy - HALF, 1, 0),
        jnp.where(stop == cy + HALF, 1, 0),
        low,
        count,
        cx - HALF,
        sx,
        sz - z_b,
    )
    for at, value in enumerate(values):
        table[at:at + 1, :] = jnp.where(slot < 3 * own, value, 0)
    return jnp.where(
        mine | (lower & (row == -1)) | (upper & (row == tile_rows)),
        (row + 1) * GZX + rest, -1)


def set_masks(masks, s, table):
    f_a, f_b = table[0, s], table[2, s]
    z_from, x_from = table[7, s], table[14, s]
    sx, zb_from = table[15, s], table[16, s]
    reach_x = sx + 1

    def in_x(rows, half, frame_at, low, high):
        lane = (lax.broadcasted_iota(jnp.int32, (rows, LANES), 1) + half * HOP) & (LANES - 1)
        x = lane + jnp.where(lane < HOP, LANES * frame_at, 0)
        return (x >= low) & (x < high)

    def in_z(rows, low, count):
        z = lax.broadcasted_iota(jnp.int32, (rows, LANES), 0)
        return (z >= low) & (z < low + count)

    row = lax.broadcasted_iota(jnp.int32, (16, LANES), 0)
    wide = row == 3
    low = jnp.where(wide, sx, reach_x + row - 1)
    high = low + jnp.where(wide, BLOCK, jnp.where(row < 3, W, 0))
    z_a = in_z(ROWS_A, z_from, W)
    z_b = in_z(ROWS_B, zb_from, BLOCK)
    at = 0
    for rows, frame_at, x_low, x_high, z in (
        (ROWS_A, f_a, x_from, x_from + W, z_a),
        (ROWS_B, f_b, sx, sx + BLOCK, z_b),
        (16, f_b, low, high, None),
    ):
        for half in range(2):
            inside = in_x(rows, half, frame_at, x_low, x_high)
            inside = inside if z is None else inside & z
            masks[s, at:at + rows] = jnp.where(inside, 1.0, 0.0).astype(jnp.bfloat16)
            at += rows


def set_units(units, total, s, low, planes, most):
    for c in range(most):
        units[total + c] = s + (low + planes * c + 64) * 256


def frame(v, fr, at):
    low = v[:, :LANES]
    high = jnp.concatenate([v[:, LANES:], v[:, HOP:LANES]], axis=1)
    fr[0, 0, at] = low
    fr[0, 1, at] = high
    fr[1, 0, at] = pltpu.roll(low, HOP, 1)
    fr[1, 1, at] = pltpu.roll(high, HOP, 1)


def run_units(half, total, units, table, spare, fr_a, fr_b, acc, sq_a, sq_b, masks):
    for at in range(REST - 1):
        units[total + at] = spare + 64 * 256
    ones = jnp.where(
        lax.broadcasted_iota(jnp.int32, (16, half * LANES), 0) == 0, 1.0, 0.0
    ).astype(jnp.bfloat16)

    def step(first, width):
        for h in range(width):
            code = units[first + h]
            s = code & 255
            y = (code >> 8) - 64
            y_two = y + half
            f_a = table[0, s]
            z_a = pl.multiple_of(table[1, s], 16)
            f_b = table[2, s]
            z_b = pl.multiple_of(table[3, s], 16)
            dy = table[4, s]
            dx = table[6, s]
            one_a = masks[s, 0:ROWS_A]
            two_a = masks[s, ROWS_A:2 * ROWS_A]
            at = 2 * ROWS_A
            one_b = masks[s, at:at + ROWS_B]
            two_b = masks[s, at + ROWS_B:at + 2 * ROWS_B]
            at += 2 * ROWS_B
            rows = masks[s, at:at + 16] + masks[s, at + 16:at + 32]
            a = [
                fr_a[0, f_a, y + PAD_A + p, pl.ds(z_a, ROWS_A), :] * one_a
                + fr_a[1, f_a, y_two + PAD_A + p, pl.ds(z_a, ROWS_A), :] * two_a
                for p in range(half)
            ]
            b = [
                fr_b[0, f_b, y + dy - 1 + PAD_B + p, pl.ds(z_b, ROWS_B), :] * one_b
                + fr_b[1, f_b, y_two + dy - 1 + PAD_B + p, pl.ds(z_b, ROWS_B), :] * two_b
                for p in range(half + 2)
            ]
            left = [
                jnp.concatenate(
                    [pltpu.roll(v, (dx + lag - 1 + LANES) & (LANES - 1), 1) for v in a], axis=1)
                for lag in range(3)
            ]
            left.append(jnp.concatenate([rows] * half, axis=1))
            left = jnp.concatenate(left, axis=0)
            right = [jnp.concatenate(b[lag:lag + half], axis=1) for lag in range(3)]
            right = jnp.concatenate(right + [ones], axis=0)
            acc[s] += lax.dot_general(
                left, right, (((1,), (1,)), ((), ())), preferred_element_type=jnp.float32)
            wide = [v.astype(jnp.float32) for v in a]
            sq_a[s] += sum([v * v for v in wide])
            wide = [v.astype(jnp.float32) for v in b[1:-1]]
            sq_b[s] += sum([v * v for v in wide])

    def wide_step(t, carry):
        step(PAIR * t, PAIR)
        return carry

    full = (total + REST - 1) // PAIR
    lax.fori_loop(0, full, wide_step, 0)

    @pl.when(total > PAIR * full)
    def _():
        step(PAIR * full, REST)


def inner_kernel(
    plan_ref, first_ref, second_ref, fr_a, fr_b, masks, acc, sq_a, sq_b,
    table_v, table, units, sem_t,
):
    planes, deep, along = first_ref.shape
    own = (acc.shape[0] - 1) // 3
    device = lax.axis_index("span")
    last = lax.axis_size("span") - 1
    piece = planes // PIECES
    decode(plan_ref[...], own, planes, deep, True, table_v)
    to_scalar = pltpu.make_async_copy(table_v, table, sem_t)
    to_scalar.start()
    for ref, fr, pad in ((first_ref, fr_a, PAD_A), (second_ref, fr_b, PAD_B)):
        def body(i, carry, ref=ref, fr=fr, pad=pad):
            for p in range(piece):
                at = i * piece + p
                frame(ref[at], fr, at + pad)
            return carry

        lax.fori_loop(0, PIECES, body, 0)

    @pl.when((device == 0) | (device == last))
    def _():
        zero = jnp.zeros((2, 2, CHUNK, deep, LANES), jnp.bfloat16)
        fr_a[:, :, 0:PAD_A] = zero
        fr_a[:, :, PAD_A + planes:] = zero
        fr_b[:, :, 0:CHUNK] = zero
        fr_b[:, :, PAD_B + planes + REACH:] = zero

    to_scalar.wait()

    def prepare(s, total):
        set_masks(masks, s, table)
        for ref in (acc, sq_a, sq_b):
            ref[s] = jnp.zeros(ref.shape[1:], jnp.float32)
        set_units(units, total, s, table[12, s], 2 * CHUNK, W // CHUNK // 2)
        return total + (table[13, s] >> 1)

    total = lax.fori_loop(0, own, prepare, 0)
    run_units(CHUNK, total, units, table, 3 * own, fr_a, fr_b, acc, sq_a, sq_b, masks)


def outer_kernel(
    plan_ref, pair_ref, other_ref, gap_base, fr_a, fr_b_in, masks_in, acc_in, sq_a_in, sq_b_in,
    out_ref, fr_b, masks, acc, sq_a, sq_b, table_v, table, units, active, sem_t,
):
    deep = fr_a.shape[3]
    planes = fr_a.shape[2] - 2 * PAD_A
    own = (acc.shape[0] - 1) // 3
    even = lax.axis_index("span") % 2 == 0
    base = REACH * deep
    from_pair, from_other = [
        ref[base:base + 8, 0:LANES].astype(jnp.float32).astype(jnp.int32)
        for ref in (pair_ref, other_ref)
    ]
    below = jnp.where(even, from_other, from_pair)
    above = jnp.where(even, from_pair, from_other)
    plan = plan_ref[...] + pltpu.roll(below, own, 1) + pltpu.roll(above, 2 * own, 1)
    target = decode(plan, own, planes, deep, False, table_v)
    to_scalar = pltpu.make_async_copy(table_v, table, sem_t)
    to_scalar.start()
    out_ref[...] = jnp.zeros(out_ref.shape, jnp.float32)
    out_ref[22:23] = target.astype(jnp.float32)

    low_at, high_at = CHUNK, PAD_B + planes
    pair_at = jnp.where(even, high_at, low_at)
    other_at = jnp.where(even, low_at, high_at)
    for p in range(REACH):
        frame(pair_ref[p * deep:(p + 1) * deep, :], fr_b, pair_at + p)
        frame(other_ref[p * deep:(p + 1) * deep, :], fr_b, other_at + p)
    to_scalar.wait()

    def prepare_own(s, total):
        active[s] = s
        set_units(units, total, s, table[12, s], CHUNK, 2)
        return total + table[13, s]

    total = lax.fori_loop(0, own, prepare_own, 0)

    def prepare(s, carry):
        total, alive = carry
        count = table[13, s]

        @pl.when(count > 0)
        def _():
            set_masks(masks, s, table)
            for ref in (acc, sq_a, sq_b):
                ref[s] = jnp.zeros(ref.shape[1:], jnp.float32)
            active[alive] = s
            set_units(units, total, s, table[12, s], CHUNK, W // CHUNK)

        return total + count, alive + jnp.where(count > 0, 1, 0)

    total, alive = lax.fori_loop(own, 3 * own, prepare, (total, own))
    spare = 3 * own
    for at in range(CLOSE - 1):
        active[alive + at] = spare
    run_units(CHUNK // 2, total, units, table, spare, fr_a, fr_b, acc, sq_a, sq_b, masks)

    cols = 2 * LANES
    col_one = lax.broadcasted_iota(jnp.int32, (1, cols), 1)
    lag_one = jnp.where(col_one >= ROWS_B, 1, 0) + jnp.where(col_one >= 2 * ROWS_B, 1, 0)
    lag_one = lag_one + jnp.where(col_one >= 3 * ROWS_B, 1, 0)
    z_one = col_one - lag_one * ROWS_B
    lag_18 = jnp.broadcast_to(lag_one, (18, cols))
    lane_18 = lax.broadcasted_iota(jnp.int32, (18, LANES), 1)
    lane_4 = lax.broadcasted_iota(jnp.int32, (4, LANES), 1)
    slant = lax.broadcasted_iota(jnp.int32, (8, cols), 1)
    slant = slant - lax.broadcasted_iota(jnp.int32, (8, cols), 0)
    mean_lane = lax.broadcasted_iota(jnp.int32, (1, LANES), 1) == 3 * ROWS_B - LANES

    def finish(t, carry):
        for h in range(CLOSE):
            s = active[CLOSE * t + h]
            f_b = table[2, s]
            z_b = pl.multiple_of(table[3, s], 16)
            offset = table[5, s]
            low_z = table[16, s] + 1
            band = (gap_base[...] >= offset - 1) & (gap_base[...] <= offset + 1)
            tops = [None] * 9
            lows = []
            for lag_x in range(3):
                part = jnp.where(band, acc[s, lag_x * ROWS_A:(lag_x + 1) * ROWS_A, :], 0.0)
                part = sum([part[8 * i:8 * i + 8] for i in range(ROWS_A // 8)])
                for lag_z in range(3):
                    hit = ((slant - (offset + lag_z - 1)) & 7) == 0
                    tops[3 * lag_z + lag_x] = jnp.sum(
                        jnp.where(hit, part, 0.0), axis=0, keepdims=True)
            for lag_z in range(3):
                low = low_z + lag_z - 1
                inside = (z_one >= low) & (z_one < low + W)
                lows.append(jnp.where(inside, acc[s, 3 * ROWS_A:3 * ROWS_A + 3, :], 0.0))
            stack = jnp.concatenate(tops + lows, axis=0)

            at = 2 * ROWS_A
            mask = masks[s, at:at + ROWS_B].astype(jnp.float32)
            ends = [
                fr_b[0, f_b, table[8 + i, s], pl.ds(z_b, ROWS_B), :].astype(jnp.float32)
                * (mask * table[10 + i, s].astype(jnp.float32))
                for i in range(2)
            ]
            row_b = jnp.where(
                lag_one == 1, acc[s, 3 * ROWS_A + 3:3 * ROWS_A + 4, :], 0.0)
            row_a = jnp.sum(acc[s, ROWS_A:2 * ROWS_A, LANES:], axis=0, keepdims=True)
            sums = [
                jnp.where(mean_lane, row_a, 0.0),
                jnp.sum(sq_a[s], axis=0, keepdims=True),
                jnp.sum(ends[0] + ends[1], axis=0, keepdims=True)
                + row_b[:, :LANES] + row_b[:, LANES:],
                jnp.sum(
                    sq_b[s] + (ends[0] * ends[0] + ends[1] * ends[1]), axis=0, keepdims=True),
            ]
            sums = jnp.sum(jnp.concatenate(sums, axis=0), axis=1, keepdims=True)
            total_18 = jnp.zeros((18, LANES), jnp.float32)
            for lag_y in range(3):
                part = jnp.sum(jnp.where(lag_18 == lag_y, stack, 0.0), axis=1, keepdims=True)
                total_18 = total_18 + jnp.where(lane_18 == SLOT * s + lag_y, part, 0.0)
            out_ref[0:18] += total_18
            out_ref[18:22] += jnp.where(lane_4 == SLOT * s, sums, 0.0)
        return carry

    lax.fori_loop(0, (alive + CLOSE - 1) // CLOSE, finish, 0)


def update_kernel(own, mine_ref, pair_ref, other_ref, out_ref):
    tile_rows = out_ref.shape[0]
    even = lax.axis_index("span") % 2 == 0
    mine = mine_ref[...]
    pair = pair_ref[...]
    other = other_ref[...]
    below = jnp.where(even, other, pair)
    above = jnp.where(even, pair, other)
    span = SLOT * own
    lane = lax.broadcasted_iota(jnp.int32, mine.shape, 1)
    total = mine
    total = total + jnp.where(
        lane < span,
        pltpu.roll(below, LANES - 2 * span, 1) + pltpu.roll(above, LANES - span, 1),
        jnp.where(
            lane < 2 * span, pltpu.roll(below, span, 1),
            jnp.where(lane < 3 * span, pltpu.roll(above, 2 * span, 1), 0.0)))

    def lead(v):
        return v + pltpu.roll(v, LANES - 1, 1) + pltpu.roll(v, LANES - 2, 1)

    def spread(v):
        return v + pltpu.roll(v, 1, 1) + pltpu.roll(v, 2, 1)

    lag_lane = lane % SLOT
    stats = spread(jnp.where(lag_lane[0:4] == 0, total[18:22], 0.0))
    voxels = float(W) ** 3
    block_voxels = float(BLOCK) ** 3
    mean_a = stats[0:1] / voxels
    energy_a = jnp.maximum(stats[1:2] / voxels - mean_a * mean_a, 0.0)
    mean_b = stats[2:3] / block_voxels
    energy_b = jnp.maximum(stats[3:4] / block_voxels - mean_b * mean_b, 0.0)
    normaliser = voxels * jnp.sqrt((energy_a + EPSILON) * (energy_b + EPSILON))
    scaled = SHARP * ((total[0:9] - mean_a * total[9:18]) / normaliser)
    used = lag_lane[0:9] < 3
    scaled = jnp.where(used, scaled, -1e30)
    top = jnp.max(scaled, axis=0, keepdims=True)
    top = jnp.maximum(top, jnp.maximum(pltpu.roll(top, LANES - 1, 1), pltpu.roll(top, LANES - 2, 1)))
    top = spread(jnp.where(lag_lane[0:1] == 0, top, 0.0))
    weights = jnp.where(used, jnp.exp(scaled - top), 0.0)
    lag_row = lax.broadcasted_iota(jnp.int32, weights.shape, 0)
    lag_z = (lag_row // 3 - 1).astype(jnp.float32)
    lag_x = (lag_row % 3 - 1).astype(jnp.float32)
    column = jnp.sum(weights, axis=0, keepdims=True)
    weight_sum = lead(column)
    along_y = lead(column * (lag_lane[0:1] - 1).astype(jnp.float32)) / weight_sum
    along_z = lead(jnp.sum(weights * lag_z, axis=0, keepdims=True)) / weight_sum
    along_x = lead(jnp.sum(weights * lag_x, axis=0, keepdims=True)) / weight_sum
    corrections = (along_y, along_z, along_x)

    grid_lane = lax.broadcasted_iota(jnp.int32, (8, LANES), 1)
    place = lax.broadcasted_iota(jnp.int32, (8, LANES), 0) * GZX + grid_lane
    target = mine[22:23].astype(jnp.int32)
    fields = [jnp.zeros((8, LANES), jnp.float32) for _ in range(3)]
    for s in range(3 * own):
        hit = place == target[:, s:s + 1]
        for comp in range(3):
            fields[comp] = jnp.where(
                hit, corrections[comp][:, SLOT * s:SLOT * s + 1], fields[comp])
    lane_z = grid_lane // GX
    lane_x = grid_lane % GX
    for comp in range(3):
        field = fields[comp]
        near = jnp.where(lane_z >= 1, pltpu.roll(field, GX, 1), 0.0)
        near = near + jnp.where(lane_z < GZX // GX - 1, pltpu.roll(field, LANES - GX, 1), 0.0)
        near = near + jnp.where(lane_x >= 1, pltpu.roll(field, 1, 1), 0.0)
        near = near + jnp.where(lane_x < GX - 1, pltpu.roll(field, LANES - 1, 1), 0.0)
        near = near[1:1 + tile_rows] + field[0:tile_rows] + field[2:2 + tile_rows]
        out_ref[:, comp, :] = 0.4 * field[1:1 + tile_rows] + 0.1 * near


def shards(first, second, windows, shifts):
    planes, deep, along = first.shape
    own = windows.shape[0]
    slots = 3 * own + 1
    count = lax.axis_size("span")
    pairs = [(i, i ^ 1) for i in range(count)]
    others = [(i, i + 1) for i in range(1, count - 1, 2)]
    others = others + [(b, a) for a, b in others]
    vmem = pl.BlockSpec(memory_space=pltpu.VMEM)

    def limit(mib):
        return pltpu.CompilerParams(vmem_limit_bytes=mib << 20)

    busy = pl.CostEstimate(flops=20 * 10**9, bytes_accessed=0, transcendentals=0)
    gap = pl.pallas_call(
        table_kernel,
        out_shape=jax.ShapeDtypeStruct((ROWS_A, 2 * LANES), jnp.int32),
        out_specs=vmem,
        compiler_params=limit(4),
        cost_estimate=pl.CostEstimate(flops=13 * 10**8, bytes_accessed=0, transcendentals=0),
        name="gap_table",
    )()
    message = jax.ShapeDtypeStruct((REACH * deep + PLAN_ROWS, along), second.dtype)
    tile, gap = lax.optimization_barrier((second, gap))
    low_planes, high_planes = tile[:REACH], tile[planes - REACH:]
    to_pair, to_other, plan = pl.pallas_call(
        send_kernel,
        out_shape=(message, message, jax.ShapeDtypeStruct((8, LANES), jnp.int32)),
        in_specs=[vmem] * 5,
        out_specs=(vmem,) * 3,
        compiler_params=limit(4),
        cost_estimate=busy,
        name="planes_to_send",
    )(windows[None], shifts, gap, low_planes, high_planes)
    from_other = lax.ppermute(to_other, "span", others)
    from_pair = lax.ppermute(to_pair, "span", pairs)
    mask_rows = 2 * (ROWS_A + ROWS_B + 16)
    frames_a = jax.ShapeDtypeStruct((2, 2, planes + 2 * PAD_A, deep, LANES), jnp.bfloat16)
    state = (
        jax.ShapeDtypeStruct((2, 2, planes + 2 * PAD_B, deep, LANES), jnp.bfloat16),
        jax.ShapeDtypeStruct((slots, mask_rows, LANES), jnp.bfloat16),
        jax.ShapeDtypeStruct((slots, 3 * ROWS_A + 16, 2 * LANES), jnp.float32),
        jax.ShapeDtypeStruct((slots, ROWS_A, LANES), jnp.float32),
        jax.ShapeDtypeStruct((slots, ROWS_B, LANES), jnp.float32),
    )
    scratch = [
        pltpu.VMEM((FIELDS, LANES), jnp.int32),
        pltpu.SMEM((FIELDS, LANES), jnp.int32),
        pltpu.SMEM(((3 * own + 1) * (W // CHUNK) + PAIR,), jnp.int32),
    ]
    held = pl.pallas_call(
        inner_kernel,
        out_shape=(frames_a, *state),
        in_specs=[vmem] * 3,
        out_specs=(vmem,) * 6,
        scratch_shapes=[*scratch, pltpu.SemaphoreType.DMA],
        compiler_params=limit(8),
        cost_estimate=busy,
        name="inner_sums",
    )(plan, first, second)
    sums, *_ = pl.pallas_call(
        outer_kernel,
        out_shape=(jax.ShapeDtypeStruct((24, LANES), jnp.float32), *state),
        in_specs=[vmem] * 10,
        out_specs=(vmem,) * 6,
        input_output_aliases={5 + i: 1 + i for i in range(5)},
        scratch_shapes=[
            *scratch, pltpu.SMEM((slots + CLOSE,), jnp.int32), pltpu.SemaphoreType.DMA],
        compiler_params=limit(8),
        name="outer_sums",
    )(plan, from_pair, from_other, gap, *held)
    other_sums = lax.ppermute(sums, "span", others)
    pair_sums = lax.ppermute(sums, "span", pairs)
    field = pl.pallas_call(
        functools.partial(update_kernel, own),
        out_shape=jax.ShapeDtypeStruct((planes // STRIDE, 3, GZX), jnp.float32),
        in_specs=[vmem] * 3,
        out_specs=vmem,
        compiler_params=limit(4),
        name="smoothed_update",
    )(sums, pair_sums, other_sums)
    return jnp.transpose(field, (1, 0, 2))


def solution(mesh):
    in_specs = (
        P(("grp", "span"), None, None),
        P(("grp", "span"), None, None),
        P(("grp", "span")),
        P(None, ("grp", "span")),
    )
    out_specs = P(None, ("grp", "span"), None)
    return jax.shard_map(shards, mesh=mesh, in_specs=in_specs, out_specs=out_specs, check_vma=False)
```

```python
import functools

import jax
import jax.numpy as jnp
from jax import lax
from jax.experimental import pallas as pl
from jax.experimental.pallas import tpu as pltpu
from jax.sharding import PartitionSpec as P

W = 48
STRIDE = 12
DYM = 3
GX = 16
GZX = 128
SHARP = 80.0
EPSILON = 1e-06

HALF = W // 2
BLOCK = W + 2
REACH = DYM + 1
LANES = 128
HOP = 64
CHUNK = 6
ROWS_A = 64
ROWS_B = 80
PAD_A = CHUNK
PAD_B = CHUNK + REACH
PIECES = 2
SLOT = 4
PLAN_ROWS = 16
FIELDS = 24
PAIR = 8
REST = 4
CLOSE = 2
FAR = 4096


def table_kernel(gap_ref):
    row = lax.broadcasted_iota(jnp.int32, gap_ref.shape, 0)
    col = lax.broadcasted_iota(jnp.int32, gap_ref.shape, 1)
    lag = jnp.where(col >= ROWS_B, 1, 0) + jnp.where(col >= 2 * ROWS_B, 1, 0)
    gap_ref[...] = jnp.where(col < 3 * ROWS_B, col - lag * ROWS_B - row, FAR)


def send_kernel(win_ref, shift_ref, gap_ref, low_ref, high_ref, pair_ref, other_ref, plan_ref):
    reach, deep, along = low_ref.shape
    even = lax.axis_index("span") % 2 == 0
    node = win_ref[...]
    own = node.shape[1]
    plan_ref[...] = jnp.zeros(plan_ref.shape, jnp.int32)
    plan_ref[0:1, 0:own] = node >> 8
    plan_ref[1:2, 0:own] = node & 255
    plan_ref[2:5, 0:own] = shift_ref[...]
    plan = plan_ref[...].astype(jnp.float32).astype(jnp.bfloat16)
    for ref in (pair_ref, other_ref):
        ref[reach * deep:reach * deep + 8, 0:LANES] = plan

    def fill(to_low, to_high):
        for p in range(reach):
            to_low[p * deep:(p + 1) * deep, :] = low_ref[p]
            to_high[p * deep:(p + 1) * deep, :] = high_ref[p]

    @pl.when(even)
    def _():
        fill(other_ref, pair_ref)

    @pl.when(jnp.logical_not(even))
    def _():
        fill(pair_ref, other_ref)


def decode(plan, own, planes, deep, inner, table):
    device = lax.axis_index("span")
    last = lax.axis_size("span") - 1
    tile_rows = planes // STRIDE
    slot = lax.broadcasted_iota(jnp.int32, (1, LANES), 1)
    node = plan[0:1] * 256 + plan[1:2]
    dy, dz, dx = plan[2:3], plan[3:4], plan[4:5]
    row = (node >> (GZX.bit_length() - 1)) - device * tile_rows
    rest = node & (GZX - 1)
    cy = STRIDE * row + STRIDE // 2
    cz = STRIDE * (rest >> (GX.bit_length() - 1)) + STRIDE // 2
    cx = STRIDE * (rest & (GX - 1)) + STRIDE // 2
    start = jnp.maximum(cy - HALF, jnp.where(device == 0, -CHUNK, 0))
    stop = jnp.minimum(cy + HALF, jnp.where(device == last, planes + CHUNK, planes))
    mine = slot < own
    lower = (slot >= own) & (slot < 2 * own)
    upper = (slot >= 2 * own) & (slot < 3 * own)
    wanted = (
        mine | (lower & (row < 0) & (row >= -tile_rows))
        | (upper & (row >= tile_rows) & (row < 2 * tile_rows))
    )
    if inner:
        low = jnp.maximum(start, CHUNK)
        high = jnp.minimum(stop, planes - CHUNK)
        wanted = mine
    else:
        below = start < CHUNK
        low = jnp.where(mine & jnp.logical_not(below), planes - CHUNK, start)
        high = jnp.where(mine & below, CHUNK, stop)
    width = jnp.where(wanted, high - low, 0)
    count = sum([jnp.where(width > CHUNK * c, 1, 0) for c in range(W // CHUNK)])
    sx = cx + dx - HALF - 1
    sz = cz + dz - HALF - 1
    z_a = jnp.minimum(jnp.maximum(cz - HALF, 0) & -16, deep - ROWS_A)
    z_b = jnp.where(sz + BLOCK <= ROWS_B, 0, deep - ROWS_B)
    values = (
        jnp.where(cx + HALF <= LANES, 0, 1),
        z_a,
        jnp.where(sx + BLOCK <= LANES, 0, 1),
        z_b,
        dy,
        z_a + dz - z_b,
        (dx + LANES) & (LANES - 1),
        cz - HALF - z_a,
        start + dy - 1 + PAD_B,
        stop + dy + PAD_B,
        jnp.where(start == cy - HALF, 1, 0),
        jnp.where(stop == cy + HALF, 1, 0),
        low,
        count,
        cx - HALF,
        sx,
        sz - z_b,
        jnp.where((row == 0) | (row == tile_rows - 1), 1, 0),
    )
    for at, value in enumerate(values):
        table[at:at + 1, :] = jnp.where(slot < 3 * own, value, 0)
    return jnp.where(
        mine | (lower & (row == -1)) | (upper & (row == tile_rows)),
        (row + 1) * GZX + rest, -1)


def set_masks(masks, s, table):
    f_a, f_b = table[0, s], table[2, s]
    z_from, x_from = table[7, s], table[14, s]
    sx, zb_from = table[15, s], table[16, s]
    reach_x = sx + 1

    def in_x(rows, half, frame_at, low, high):
        lane = (lax.broadcasted_iota(jnp.int32, (rows, LANES), 1) + half * HOP) & (LANES - 1)
        x = lane + jnp.where(lane < HOP, LANES * frame_at, 0)
        return (x >= low) & (x < high)

    def in_z(rows, low, count):
        z = lax.broadcasted_iota(jnp.int32, (rows, LANES), 0)
        return (z >= low) & (z < low + count)

    row = lax.broadcasted_iota(jnp.int32, (16, LANES), 0)
    wide = row == 3
    low = jnp.where(wide, sx, reach_x + row - 1)
    high = low + jnp.where(wide, BLOCK, jnp.where(row < 3, W, 0))
    z_a = in_z(ROWS_A, z_from, W)
    z_b = in_z(ROWS_B, zb_from, BLOCK)
    at = 0
    for rows, frame_at, x_low, x_high, z in (
        (ROWS_A, f_a, x_from, x_from + W, z_a),
        (ROWS_B, f_b, sx, sx + BLOCK, z_b),
        (16, f_b, low, high, None),
    ):
        for half in range(2):
            inside = in_x(rows, half, frame_at, x_low, x_high)
            inside = inside if z is None else inside & z
            masks[s, at:at + rows] = jnp.where(inside, 1.0, 0.0).astype(jnp.bfloat16)
            at += rows


def set_units(units, total, s, low, planes, most):
    for c in range(most):
        units[total + c] = s + (low + planes * c + 64) * 256


def frame(v, fr, at):
    low = v[:, :LANES]
    high = jnp.concatenate([v[:, LANES:], v[:, HOP:LANES]], axis=1)
    fr[0, 0, at] = low
    fr[0, 1, at] = high
    fr[1, 0, at] = pltpu.roll(low, HOP, 1)
    fr[1, 1, at] = pltpu.roll(high, HOP, 1)


def run_units(half, total, units, table, spare, fr_a, fr_b, acc, sq_a, sq_b, masks):
    for at in range(REST - 1):
        units[total + at] = spare + 64 * 256
    ones = jnp.where(
        lax.broadcasted_iota(jnp.int32, (16, half * LANES), 0) == 0, 1.0, 0.0
    ).astype(jnp.bfloat16)

    def step(first, width):
        for h in range(width):
            code = units[first + h]
            s = code & 255
            y = (code >> 8) - 64
            y_two = y + half
            f_a = table[0, s]
            z_a = pl.multiple_of(table[1, s], 16)
            f_b = table[2, s]
            z_b = pl.multiple_of(table[3, s], 16)
            dy = table[4, s]
            dx = table[6, s]
            one_a = masks[s, 0:ROWS_A]
            two_a = masks[s, ROWS_A:2 * ROWS_A]
            at = 2 * ROWS_A
            one_b = masks[s, at:at + ROWS_B]
            two_b = masks[s, at + ROWS_B:at + 2 * ROWS_B]
            at += 2 * ROWS_B
            rows = masks[s, at:at + 16] + masks[s, at + 16:at + 32]
            a = [
                fr_a[0, f_a, y + PAD_A + p, pl.ds(z_a, ROWS_A), :] * one_a
                + fr_a[1, f_a, y_two + PAD_A + p, pl.ds(z_a, ROWS_A), :] * two_a
                for p in range(half)
            ]
            b = [
                fr_b[0, f_b, y + dy - 1 + PAD_B + p, pl.ds(z_b, ROWS_B), :] * one_b
                + fr_b[1, f_b, y_two + dy - 1 + PAD_B + p, pl.ds(z_b, ROWS_B), :] * two_b
                for p in range(half + 2)
            ]
            left = [
                jnp.concatenate(
                    [pltpu.roll(v, (dx + lag - 1 + LANES) & (LANES - 1), 1) for v in a], axis=1)
                for lag in range(3)
            ]
            left.append(jnp.concatenate([rows] * half, axis=1))
            left = jnp.concatenate(left, axis=0)
            right = [jnp.concatenate(b[lag:lag + half], axis=1) for lag in range(3)]
            right = jnp.concatenate(right + [ones], axis=0)
            acc[s] += lax.dot_general(
                left, right, (((1,), (1,)), ((), ())), preferred_element_type=jnp.float32)
            wide = [v.astype(jnp.float32) for v in a]
            sq_a[s] += sum([v * v for v in wide])
            wide = [v.astype(jnp.float32) for v in b[1:-1]]
            sq_b[s] += sum([v * v for v in wide])

    def wide_step(t, carry):
        step(PAIR * t, PAIR)
        return carry

    full = (total + REST - 1) // PAIR
    lax.fori_loop(0, full, wide_step, 0)

    @pl.when(total > PAIR * full)
    def _():
        step(PAIR * full, REST)


def inner_kernel(
    plan_ref, first_ref, second_ref, fr_a, fr_b, masks, acc, sq_a, sq_b,
    table_v, table, units, sem_t,
):
    planes, deep, along = first_ref.shape
    own = (acc.shape[0] - 1) // 3
    device = lax.axis_index("span")
    last = lax.axis_size("span") - 1
    piece = planes // PIECES
    decode(plan_ref[...], own, planes, deep, True, table_v)
    to_scalar = pltpu.make_async_copy(table_v, table, sem_t)
    to_scalar.start()
    for ref, fr, pad in ((first_ref, fr_a, PAD_A), (second_ref, fr_b, PAD_B)):
        def body(i, carry, ref=ref, fr=fr, pad=pad):
            for p in range(piece):
                at = i * piece + p
                frame(ref[at], fr, at + pad)
            return carry

        lax.fori_loop(0, PIECES, body, 0)

    @pl.when((device == 0) | (device == last))
    def _():
        zero = jnp.zeros((2, 2, CHUNK, deep, LANES), jnp.bfloat16)
        fr_a[:, :, 0:PAD_A] = zero
        fr_a[:, :, PAD_A + planes:] = zero
        fr_b[:, :, 0:CHUNK] = zero
        fr_b[:, :, PAD_B + planes + REACH:] = zero

    to_scalar.wait()

    def prepare(s, total):
        set_masks(masks, s, table)
        for ref in (acc, sq_a, sq_b):
            ref[s] = jnp.zeros(ref.shape[1:], jnp.float32)
        set_units(units, total, s, table[12, s], 2 * CHUNK, W // CHUNK // 2)
        return total + (table[13, s] >> 1)

    total = lax.fori_loop(0, own, prepare, 0)
    run_units(CHUNK, total, units, table, 3 * own, fr_a, fr_b, acc, sq_a, sq_b, masks)


def finish_slots(alive, active, table, out_ref, gap_base, fr_b, masks, acc, sq_a, sq_b):
    cols = 2 * LANES
    col_one = lax.broadcasted_iota(jnp.int32, (1, cols), 1)
    lag_one = jnp.where(col_one >= ROWS_B, 1, 0) + jnp.where(col_one >= 2 * ROWS_B, 1, 0)
    lag_one = lag_one + jnp.where(col_one >= 3 * ROWS_B, 1, 0)
    z_one = col_one - lag_one * ROWS_B
    lag_18 = jnp.broadcast_to(lag_one, (18, cols))
    lane_18 = lax.broadcasted_iota(jnp.int32, (18, LANES), 1)
    lane_4 = lax.broadcasted_iota(jnp.int32, (4, LANES), 1)
    slant = lax.broadcasted_iota(jnp.int32, (8, cols), 1)
    slant = slant - lax.broadcasted_iota(jnp.int32, (8, cols), 0)
    mean_lane = lax.broadcasted_iota(jnp.int32, (1, LANES), 1) == 3 * ROWS_B - LANES

    def finish(t, carry):
        for h in range(CLOSE):
            s = active[CLOSE * t + h]
            f_b = table[2, s]
            z_b = pl.multiple_of(table[3, s], 16)
            offset = table[5, s]
            low_z = table[16, s] + 1
            band = (gap_base[...] >= offset - 1) & (gap_base[...] <= offset + 1)
            tops = [None] * 9
            lows = []
            for lag_x in range(3):
                part = jnp.where(band, acc[s, lag_x * ROWS_A:(lag_x + 1) * ROWS_A, :], 0.0)
                part = sum([part[8 * i:8 * i + 8] for i in range(ROWS_A // 8)])
                for lag_z in range(3):
                    hit = ((slant - (offset + lag_z - 1)) & 7) == 0
                    tops[3 * lag_z + lag_x] = jnp.sum(
                        jnp.where(hit, part, 0.0), axis=0, keepdims=True)
            for lag_z in range(3):
                low = low_z + lag_z - 1
                inside = (z_one >= low) & (z_one < low + W)
                lows.append(jnp.where(inside, acc[s, 3 * ROWS_A:3 * ROWS_A + 3, :], 0.0))
            stack = jnp.concatenate(tops + lows, axis=0)

            at = 2 * ROWS_A
            mask = masks[s, at:at + ROWS_B].astype(jnp.float32)
            ends = [
                fr_b[0, f_b, table[8 + i, s], pl.ds(z_b, ROWS_B), :].astype(jnp.float32)
                * (mask * table[10 + i, s].astype(jnp.float32))
                for i in range(2)
            ]
            row_b = jnp.where(
                lag_one == 1, acc[s, 3 * ROWS_A + 3:3 * ROWS_A + 4, :], 0.0)
            row_a = jnp.sum(acc[s, ROWS_A:2 * ROWS_A, LANES:], axis=0, keepdims=True)
            sums = [
                jnp.where(mean_lane, row_a, 0.0),
                jnp.sum(sq_a[s], axis=0, keepdims=True),
                jnp.sum(ends[0] + ends[1], axis=0, keepdims=True)
                + row_b[:, :LANES] + row_b[:, LANES:],
                jnp.sum(
                    sq_b[s] + (ends[0] * ends[0] + ends[1] * ends[1]), axis=0, keepdims=True),
            ]
            sums = jnp.sum(jnp.concatenate(sums, axis=0), axis=1, keepdims=True)
            total_18 = jnp.zeros((18, LANES), jnp.float32)
            for lag_y in range(3):
                part = jnp.sum(jnp.where(lag_18 == lag_y, stack, 0.0), axis=1, keepdims=True)
                total_18 = total_18 + jnp.where(lane_18 == SLOT * s + lag_y, part, 0.0)
            out_ref[0:18] += total_18
            out_ref[18:22] += jnp.where(lane_4 == SLOT * s, sums, 0.0)
        return carry

    lax.fori_loop(0, (alive + CLOSE - 1) // CLOSE, finish, 0)


def outer_kernel(
    plan_ref, pair_ref, other_ref, gap_base, fr_a, fr_b_in, masks_in, acc_in, sq_a_in, sq_b_in,
    out_ref, table_v, fr_b, masks, acc, sq_a, sq_b, table, units, active, sem_t,
):
    deep = fr_a.shape[3]
    planes = fr_a.shape[2] - 2 * PAD_A
    own = (acc.shape[0] - 1) // 3
    even = lax.axis_index("span") % 2 == 0
    base = REACH * deep
    from_pair, from_other = [
        ref[base:base + 8, 0:LANES].astype(jnp.float32).astype(jnp.int32)
        for ref in (pair_ref, other_ref)
    ]
    below = jnp.where(even, from_other, from_pair)
    above = jnp.where(even, from_pair, from_other)
    plan = plan_ref[...] + pltpu.roll(below, own, 1) + pltpu.roll(above, 2 * own, 1)
    target = decode(plan, own, planes, deep, False, table_v)
    to_scalar = pltpu.make_async_copy(table_v, table, sem_t)
    to_scalar.start()
    out_ref[...] = jnp.zeros(out_ref.shape, jnp.float32)
    out_ref[22:23] = target.astype(jnp.float32)

    low_at, high_at = CHUNK, PAD_B + planes
    pair_at = jnp.where(even, high_at, low_at)
    other_at = jnp.where(even, low_at, high_at)
    for p in range(REACH):
        frame(pair_ref[p * deep:(p + 1) * deep, :], fr_b, pair_at + p)
        frame(other_ref[p * deep:(p + 1) * deep, :], fr_b, other_at + p)
    to_scalar.wait()

    def prepare_own(s, carry):
        total, alive = carry
        active[alive] = s
        set_units(units, total, s, table[12, s], CHUNK, 2)
        return total + table[13, s], alive + table[17, s]

    carry = lax.fori_loop(0, own, prepare_own, (0, 0))

    def prepare(s, carry):
        total, alive = carry
        count = table[13, s]

        @pl.when(count > 0)
        def _():
            set_masks(masks, s, table)
            for ref in (acc, sq_a, sq_b):
                ref[s] = jnp.zeros(ref.shape[1:], jnp.float32)
            active[alive] = s
            set_units(units, total, s, table[12, s], CHUNK, W // CHUNK)

        return total + count, alive + jnp.where(count > 0, 1, 0)

    total, alive = lax.fori_loop(own, 3 * own, prepare, carry)
    spare = 3 * own
    for at in range(CLOSE - 1):
        active[alive + at] = spare
    run_units(CHUNK // 2, total, units, table, spare, fr_a, fr_b, acc, sq_a, sq_b, masks)
    finish_slots(alive, active, table, out_ref, gap_base, fr_b, masks, acc, sq_a, sq_b)


def rest_kernel(
    table_v, gap_base, fr_b, masks, acc, sq_a, sq_b, out_ref, table, active, sem_t,
):
    own = (acc.shape[0] - 1) // 3
    to_scalar = pltpu.make_async_copy(table_v, table, sem_t)
    to_scalar.start()
    out_ref[...] = jnp.zeros(out_ref.shape, jnp.float32)
    to_scalar.wait()

    def listed(s, alive):
        active[alive] = s
        return alive + 1 - table[17, s]

    alive = lax.fori_loop(0, own, listed, 0)
    for at in range(CLOSE - 1):
        active[alive + at] = 3 * own
    finish_slots(alive, active, table, out_ref, gap_base, fr_b, masks, acc, sq_a, sq_b)


def update_kernel(own, mine_ref, rest_ref, pair_ref, other_ref, out_ref):
    tile_rows = out_ref.shape[0]
    even = lax.axis_index("span") % 2 == 0
    mine = mine_ref[...] + rest_ref[...]
    pair = pair_ref[...]
    other = other_ref[...]
    below = jnp.where(even, other, pair)
    above = jnp.where(even, pair, other)
    span = SLOT * own
    lane = lax.broadcasted_iota(jnp.int32, mine.shape, 1)
    total = mine
    total = total + jnp.where(
        lane < span,
        pltpu.roll(below, LANES - 2 * span, 1) + pltpu.roll(above, LANES - span, 1),
        jnp.where(
            lane < 2 * span, pltpu.roll(below, span, 1),
            jnp.where(lane < 3 * span, pltpu.roll(above, 2 * span, 1), 0.0)))

    def lead(v):
        return v + pltpu.roll(v, LANES - 1, 1) + pltpu.roll(v, LANES - 2, 1)

    def spread(v):
        return v + pltpu.roll(v, 1, 1) + pltpu.roll(v, 2, 1)

    lag_lane = lane % SLOT
    stats = spread(jnp.where(lag_lane[0:4] == 0, total[18:22], 0.0))
    voxels = float(W) ** 3
    block_voxels = float(BLOCK) ** 3
    mean_a = stats[0:1] / voxels
    energy_a = jnp.maximum(stats[1:2] / voxels - mean_a * mean_a, 0.0)
    mean_b = stats[2:3] / block_voxels
    energy_b = jnp.maximum(stats[3:4] / block_voxels - mean_b * mean_b, 0.0)
    normaliser = voxels * jnp.sqrt((energy_a + EPSILON) * (energy_b + EPSILON))
    scaled = SHARP * ((total[0:9] - mean_a * total[9:18]) / normaliser)
    used = lag_lane[0:9] < 3
    scaled = jnp.where(used, scaled, -1e30)
    top = jnp.max(scaled, axis=0, keepdims=True)
    top = jnp.maximum(top, jnp.maximum(pltpu.roll(top, LANES - 1, 1), pltpu.roll(top, LANES - 2, 1)))
    top = spread(jnp.where(lag_lane[0:1] == 0, top, 0.0))
    weights = jnp.where(used, jnp.exp(scaled - top), 0.0)
    lag_row = lax.broadcasted_iota(jnp.int32, weights.shape, 0)
    lag_z = (lag_row // 3 - 1).astype(jnp.float32)
    lag_x = (lag_row % 3 - 1).astype(jnp.float32)
    column = jnp.sum(weights, axis=0, keepdims=True)
    weight_sum = lead(column)
    along_y = lead(column * (lag_lane[0:1] - 1).astype(jnp.float32)) / weight_sum
    along_z = lead(jnp.sum(weights * lag_z, axis=0, keepdims=True)) / weight_sum
    along_x = lead(jnp.sum(weights * lag_x, axis=0, keepdims=True)) / weight_sum
    corrections = (along_y, along_z, along_x)

    grid_lane = lax.broadcasted_iota(jnp.int32, (8, LANES), 1)
    place = lax.broadcasted_iota(jnp.int32, (8, LANES), 0) * GZX + grid_lane
    target = mine[22:23].astype(jnp.int32)
    fields = [jnp.zeros((8, LANES), jnp.float32) for _ in range(3)]
    for s in range(3 * own):
        hit = place == target[:, s:s + 1]
        for comp in range(3):
            fields[comp] = jnp.where(
                hit, corrections[comp][:, SLOT * s:SLOT * s + 1], fields[comp])
    lane_z = grid_lane // GX
    lane_x = grid_lane % GX
    for comp in range(3):
        field = fields[comp]
        near = jnp.where(lane_z >= 1, pltpu.roll(field, GX, 1), 0.0)
        near = near + jnp.where(lane_z < GZX // GX - 1, pltpu.roll(field, LANES - GX, 1), 0.0)
        near = near + jnp.where(lane_x >= 1, pltpu.roll(field, 1, 1), 0.0)
        near = near + jnp.where(lane_x < GX - 1, pltpu.roll(field, LANES - 1, 1), 0.0)
        near = near[1:1 + tile_rows] + field[0:tile_rows] + field[2:2 + tile_rows]
        out_ref[:, comp, :] = 0.4 * field[1:1 + tile_rows] + 0.1 * near


def shards(first, second, windows, shifts):
    planes, deep, along = first.shape
    own = windows.shape[0]
    slots = 3 * own + 1
    count = lax.axis_size("span")
    pairs = [(i, i ^ 1) for i in range(count)]
    others = [(i, i + 1) for i in range(1, count - 1, 2)]
    others = others + [(b, a) for a, b in others]
    vmem = pl.BlockSpec(memory_space=pltpu.VMEM)

    def limit(mib):
        return pltpu.CompilerParams(vmem_limit_bytes=mib << 20)

    busy = pl.CostEstimate(flops=20 * 10**9, bytes_accessed=0, transcendentals=0)
    gap = pl.pallas_call(
        table_kernel,
        out_shape=jax.ShapeDtypeStruct((ROWS_A, 2 * LANES), jnp.int32),
        out_specs=vmem,
        compiler_params=limit(4),
        cost_estimate=pl.CostEstimate(flops=13 * 10**8, bytes_accessed=0, transcendentals=0),
        name="gap_table",
    )()
    message = jax.ShapeDtypeStruct((REACH * deep + PLAN_ROWS, along), second.dtype)
    tile, gap = lax.optimization_barrier((second, gap))
    low_planes, high_planes = tile[:REACH], tile[planes - REACH:]
    to_pair, to_other, plan = pl.pallas_call(
        send_kernel,
        out_shape=(message, message, jax.ShapeDtypeStruct((8, LANES), jnp.int32)),
        in_specs=[vmem] * 5,
        out_specs=(vmem,) * 3,
        compiler_params=limit(4),
        cost_estimate=busy,
        name="planes_to_send",
    )(windows[None], shifts, gap, low_planes, high_planes)
    from_other = lax.ppermute(to_other, "span", others)
    from_pair = lax.ppermute(to_pair, "span", pairs)
    mask_rows = 2 * (ROWS_A + ROWS_B + 16)
    frames_a = jax.ShapeDtypeStruct((2, 2, planes + 2 * PAD_A, deep, LANES), jnp.bfloat16)
    state = (
        jax.ShapeDtypeStruct((2, 2, planes + 2 * PAD_B, deep, LANES), jnp.bfloat16),
        jax.ShapeDtypeStruct((slots, mask_rows, LANES), jnp.bfloat16),
        jax.ShapeDtypeStruct((slots, 3 * ROWS_A + 16, 2 * LANES), jnp.float32),
        jax.ShapeDtypeStruct((slots, ROWS_A, LANES), jnp.float32),
        jax.ShapeDtypeStruct((slots, ROWS_B, LANES), jnp.float32),
    )
    scratch = [
        pltpu.SMEM((FIELDS, LANES), jnp.int32),
        pltpu.SMEM(((3 * own + 1) * (W // CHUNK) + PAIR,), jnp.int32),
    ]
    held = pl.pallas_call(
        inner_kernel,
        out_shape=(frames_a, *state),
        in_specs=[vmem] * 3,
        out_specs=(vmem,) * 6,
        scratch_shapes=[
            pltpu.VMEM((FIELDS, LANES), jnp.int32), *scratch, pltpu.SemaphoreType.DMA],
        compiler_params=limit(8),
        cost_estimate=busy,
        name="inner_sums",
    )(plan, first, second)
    sums, fields, *held = pl.pallas_call(
        outer_kernel,
        out_shape=(
            jax.ShapeDtypeStruct((24, LANES), jnp.float32),
            jax.ShapeDtypeStruct((FIELDS, LANES), jnp.int32), *state),
        in_specs=[vmem] * 10,
        out_specs=(vmem,) * 7,
        input_output_aliases={5 + i: 2 + i for i in range(5)},
        scratch_shapes=[
            *scratch, pltpu.SMEM((slots + CLOSE,), jnp.int32), pltpu.SemaphoreType.DMA],
        compiler_params=limit(8),
        name="outer_sums",
    )(plan, from_pair, from_other, gap, *held)
    other_sums = lax.ppermute(sums, "span", others)
    pair_sums = lax.ppermute(sums, "span", pairs)
    rest = pl.pallas_call(
        rest_kernel,
        out_shape=jax.ShapeDtypeStruct((24, LANES), jnp.float32),
        in_specs=[vmem] * 7,
        out_specs=vmem,
        scratch_shapes=[
            pltpu.SMEM((FIELDS, LANES), jnp.int32), pltpu.SMEM((slots + CLOSE,), jnp.int32),
            pltpu.SemaphoreType.DMA],
        compiler_params=limit(8),
        cost_estimate=busy,
        name="rest_of_sums",
    )(fields, gap, *held)
    field = pl.pallas_call(
        functools.partial(update_kernel, own),
        out_shape=jax.ShapeDtypeStruct((planes // STRIDE, 3, GZX), jnp.float32),
        in_specs=[vmem] * 4,
        out_specs=vmem,
        compiler_params=limit(4),
        name="smoothed_update",
    )(sums, rest, pair_sums, other_sums)
    return jnp.transpose(field, (1, 0, 2))


def solution(mesh):
    in_specs = (
        P(("grp", "span"), None, None),
        P(("grp", "span"), None, None),
        P(("grp", "span")),
        P(None, ("grp", "span")),
    )
    out_specs = P(None, ("grp", "span"), None)
    return jax.shard_map(shards, mesh=mesh, in_specs=in_specs, out_specs=out_specs, check_vma=False)
```

```python
import functools

import jax
import jax.numpy as jnp
from jax import lax
from jax.experimental import pallas as pl
from jax.experimental.pallas import tpu as pltpu
from jax.sharding import PartitionSpec as P

W = 48
STRIDE = 12
DYM = 3
GX = 16
GZX = 128
SHARP = 80.0
EPSILON = 1e-06

HALF = W // 2
BLOCK = W + 2
REACH = DYM + 1
LANES = 128
HOP = 64
CHUNK = 6
ROWS_A = 64
ROWS_B = 80
PAD_A = CHUNK
PAD_B = CHUNK + REACH
PIECES = 2
SPREAD = 32
PLAN_ROWS = 16
FIELDS = 24
PAIR = 8
REST = 4
CLOSE = 4
FAR = 4096


def table_kernel(gap_ref):
    row = lax.broadcasted_iota(jnp.int32, gap_ref.shape, 0)
    col = lax.broadcasted_iota(jnp.int32, gap_ref.shape, 1)
    lag = jnp.where(col >= ROWS_B, 1, 0) + jnp.where(col >= 2 * ROWS_B, 1, 0)
    gap_ref[...] = jnp.where(col < 3 * ROWS_B, col - lag * ROWS_B - row, FAR)


def send_kernel(win_ref, shift_ref, gap_ref, low_ref, high_ref, pair_ref, other_ref, plan_ref):
    reach, deep, along = low_ref.shape
    even = lax.axis_index("span") % 2 == 0
    node = win_ref[...]
    own = node.shape[1]
    plan_ref[...] = jnp.zeros(plan_ref.shape, jnp.int32)
    plan_ref[0:1, 0:own] = node >> 8
    plan_ref[1:2, 0:own] = node & 255
    plan_ref[2:5, 0:own] = shift_ref[...]
    plan = plan_ref[...].astype(jnp.float32).astype(jnp.bfloat16)
    for ref in (pair_ref, other_ref):
        ref[reach * deep:reach * deep + 8, 0:LANES] = plan

    def fill(to_low, to_high):
        for p in range(reach):
            to_low[p * deep:(p + 1) * deep, :] = low_ref[p]
            to_high[p * deep:(p + 1) * deep, :] = high_ref[p]

    @pl.when(even)
    def _():
        fill(other_ref, pair_ref)

    @pl.when(jnp.logical_not(even))
    def _():
        fill(pair_ref, other_ref)


def decode(plan, own, planes, deep, inner, table):
    device = lax.axis_index("span")
    last = lax.axis_size("span") - 1
    tile_rows = planes // STRIDE
    slot = lax.broadcasted_iota(jnp.int32, (1, LANES), 1)
    node = plan[0:1] * 256 + plan[1:2]
    dy, dz, dx = plan[2:3], plan[3:4], plan[4:5]
    row = (node >> (GZX.bit_length() - 1)) - device * tile_rows
    rest = node & (GZX - 1)
    cy = STRIDE * row + STRIDE // 2
    cz = STRIDE * (rest >> (GX.bit_length() - 1)) + STRIDE // 2
    cx = STRIDE * (rest & (GX - 1)) + STRIDE // 2
    start = jnp.maximum(cy - HALF, jnp.where(device == 0, -CHUNK, 0))
    stop = jnp.minimum(cy + HALF, jnp.where(device == last, planes + CHUNK, planes))
    mine = slot < own
    lower = (slot >= own) & (slot < 2 * own)
    upper = (slot >= 2 * own) & (slot < 3 * own)
    wanted = (
        mine | (lower & (row < 0) & (row >= -tile_rows))
        | (upper & (row >= tile_rows) & (row < 2 * tile_rows))
    )
    if inner:
        low = jnp.maximum(start, CHUNK)
        high = jnp.minimum(stop, planes - CHUNK)
        wanted = mine
    else:
        below = start < CHUNK
        low = jnp.where(mine & jnp.logical_not(below), planes - CHUNK, start)
        high = jnp.where(mine & below, CHUNK, stop)
    width = jnp.where(wanted, high - low, 0)
    count = sum([jnp.where(width > CHUNK * c, 1, 0) for c in range(W // CHUNK)])
    sx = cx + dx - HALF - 1
    sz = cz + dz - HALF - 1
    z_a = jnp.minimum(jnp.maximum(cz - HALF, 0) & -16, deep - ROWS_A)
    z_b = jnp.where(sz + BLOCK <= ROWS_B, 0, deep - ROWS_B)
    values = (
        jnp.where(cx + HALF <= LANES, 0, 1),
        z_a,
        jnp.where(sx + BLOCK <= LANES, 0, 1),
        z_b,
        dy,
        z_a + dz - z_b,
        (dx + LANES) & (LANES - 1),
        cz - HALF - z_a,
        start + dy - 1 + PAD_B,
        stop + dy + PAD_B,
        jnp.where(start == cy - HALF, 1, 0),
        jnp.where(stop == cy + HALF, 1, 0),
        low,
        count,
        cx - HALF,
        sx,
        sz - z_b,
        jnp.where((row == 0) | (row == tile_rows - 1), 1, 0),
    )
    for at, value in enumerate(values):
        table[at:at + 1, :] = jnp.where(slot < 3 * own, value, 0)
    return jnp.where(
        mine | (lower & (row == -1)) | (upper & (row == tile_rows)),
        (row + 1) * GZX + rest, -1)


def set_masks(masks, s, table):
    f_a, f_b = table[0, s], table[2, s]
    z_from, x_from = table[7, s], table[14, s]
    sx, zb_from = table[15, s], table[16, s]
    reach_x = sx + 1

    def in_x(rows, half, frame_at, low, high):
        lane = (lax.broadcasted_iota(jnp.int32, (rows, LANES), 1) + half * HOP) & (LANES - 1)
        x = lane + jnp.where(lane < HOP, LANES * frame_at, 0)
        return (x >= low) & (x < high)

    def in_z(rows, low, count):
        z = lax.broadcasted_iota(jnp.int32, (rows, LANES), 0)
        return (z >= low) & (z < low + count)

    row = lax.broadcasted_iota(jnp.int32, (16, LANES), 0)
    wide = row == 3
    low = jnp.where(wide, sx, reach_x + row - 1)
    high = low + jnp.where(wide, BLOCK, jnp.where(row < 3, W, 0))
    z_a = in_z(ROWS_A, z_from, W)
    z_b = in_z(ROWS_B, zb_from, BLOCK)
    at = 0
    for rows, frame_at, x_low, x_high, z in (
        (ROWS_A, f_a, x_from, x_from + W, z_a),
        (ROWS_B, f_b, sx, sx + BLOCK, z_b),
        (16, f_b, low, high, None),
    ):
        for half in range(2):
            inside = in_x(rows, half, frame_at, x_low, x_high)
            inside = inside if z is None else inside & z
            masks[s, at:at + rows] = jnp.where(inside, 1.0, 0.0).astype(jnp.bfloat16)
            at += rows


def set_units(units, total, s, low, planes, most):
    for c in range(most):
        units[total + c] = s + (low + planes * c + 64) * 256


def frame(v, fr, at):
    low = v[:, :LANES]
    high = jnp.concatenate([v[:, LANES:], v[:, HOP:LANES]], axis=1)
    fr[0, 0, at] = low
    fr[0, 1, at] = high
    fr[1, 0, at] = pltpu.roll(low, HOP, 1)
    fr[1, 1, at] = pltpu.roll(high, HOP, 1)


def run_units(half, total, units, table, spare, fr_a, fr_b, acc, sq_a, sq_b, masks):
    for at in range(REST - 1):
        units[total + at] = spare + 64 * 256
    ones = jnp.where(
        lax.broadcasted_iota(jnp.int32, (16, half * LANES), 0) == 0, 1.0, 0.0
    ).astype(jnp.bfloat16)

    def step(first, width):
        for h in range(width):
            code = units[first + h]
            s = code & 255
            y = (code >> 8) - 64
            y_two = y + half
            f_a = table[0, s]
            z_a = pl.multiple_of(table[1, s], 16)
            f_b = table[2, s]
            z_b = pl.multiple_of(table[3, s], 16)
            dy = table[4, s]
            dx = table[6, s]
            one_a = masks[s, 0:ROWS_A]
            two_a = masks[s, ROWS_A:2 * ROWS_A]
            at = 2 * ROWS_A
            one_b = masks[s, at:at + ROWS_B]
            two_b = masks[s, at + ROWS_B:at + 2 * ROWS_B]
            at += 2 * ROWS_B
            rows = masks[s, at:at + 16] + masks[s, at + 16:at + 32]
            a = [
                fr_a[0, f_a, y + PAD_A + p, pl.ds(z_a, ROWS_A), :] * one_a
                + fr_a[1, f_a, y_two + PAD_A + p, pl.ds(z_a, ROWS_A), :] * two_a
                for p in range(half)
            ]
            b = [
                fr_b[0, f_b, y + dy - 1 + PAD_B + p, pl.ds(z_b, ROWS_B), :] * one_b
                + fr_b[1, f_b, y_two + dy - 1 + PAD_B + p, pl.ds(z_b, ROWS_B), :] * two_b
                for p in range(half + 2)
            ]
            left = [
                jnp.concatenate(
                    [pltpu.roll(v, (dx + lag - 1 + LANES) & (LANES - 1), 1) for v in a], axis=1)
                for lag in range(3)
            ]
            left.append(jnp.concatenate([rows] * half, axis=1))
            left = jnp.concatenate(left, axis=0)
            right = [jnp.concatenate(b[lag:lag + half], axis=1) for lag in range(3)]
            right = jnp.concatenate(right + [ones], axis=0)
            acc[s] += lax.dot_general(
                left, right, (((1,), (1,)), ((), ())), preferred_element_type=jnp.float32)
            wide = [v.astype(jnp.float32) for v in a]
            sq_a[s] += sum([v * v for v in wide])
            wide = [v.astype(jnp.float32) for v in b[1:-1]]
            sq_b[s] += sum([v * v for v in wide])

    def wide_step(t, carry):
        step(PAIR * t, PAIR)
        return carry

    full = (total + REST - 1) // PAIR
    lax.fori_loop(0, full, wide_step, 0)

    @pl.when(total > PAIR * full)
    def _():
        step(PAIR * full, REST)


def inner_kernel(
    plan_ref, first_ref, second_ref, fr_a, fr_b, masks, acc, sq_a, sq_b,
    table_v, table, units, sem_t,
):
    planes, deep, along = first_ref.shape
    own = (acc.shape[0] - 1) // 3
    device = lax.axis_index("span")
    last = lax.axis_size("span") - 1
    piece = planes // PIECES
    decode(plan_ref[...], own, planes, deep, True, table_v)
    to_scalar = pltpu.make_async_copy(table_v, table, sem_t)
    to_scalar.start()
    for ref, fr, pad in ((first_ref, fr_a, PAD_A), (second_ref, fr_b, PAD_B)):
        def body(i, carry, ref=ref, fr=fr, pad=pad):
            for p in range(piece):
                at = i * piece + p
                frame(ref[at], fr, at + pad)
            return carry

        lax.fori_loop(0, PIECES, body, 0)

    @pl.when((device == 0) | (device == last))
    def _():
        zero = jnp.zeros((2, 2, CHUNK, deep, LANES), jnp.bfloat16)
        fr_a[:, :, 0:PAD_A] = zero
        fr_a[:, :, PAD_A + planes:] = zero
        fr_b[:, :, 0:CHUNK] = zero
        fr_b[:, :, PAD_B + planes + REACH:] = zero

    to_scalar.wait()

    def prepare(s, total):
        set_masks(masks, s, table)
        for ref in (acc, sq_a, sq_b):
            ref[s] = jnp.zeros(ref.shape[1:], jnp.float32)
        set_units(units, total, s, table[12, s], 2 * CHUNK, W // CHUNK // 2)
        return total + (table[13, s] >> 1)

    total = lax.fori_loop(0, own, prepare, 0)
    run_units(CHUNK, total, units, table, 3 * own, fr_a, fr_b, acc, sq_a, sq_b, masks)


def finish_slots(alive, active, table, out_ref, gap_base, fr_b, masks, acc, sq_a, sq_b):
    cols = 2 * LANES
    col_one = lax.broadcasted_iota(jnp.int32, (1, cols), 1)
    lag_one = jnp.where(col_one >= ROWS_B, 1, 0) + jnp.where(col_one >= 2 * ROWS_B, 1, 0)
    lag_one = lag_one + jnp.where(col_one >= 3 * ROWS_B, 1, 0)
    z_one = col_one - lag_one * ROWS_B
    lag_18 = jnp.broadcast_to(lag_one, (18, cols))
    lane_18 = lax.broadcasted_iota(jnp.int32, (18, LANES), 1)
    lane_4 = lax.broadcasted_iota(jnp.int32, (4, LANES), 1)
    slant = lax.broadcasted_iota(jnp.int32, (8, cols), 1)
    slant = slant - lax.broadcasted_iota(jnp.int32, (8, cols), 0)
    mean_lane = lax.broadcasted_iota(jnp.int32, (1, LANES), 1) == 3 * ROWS_B - LANES

    def finish(t, carry):
        for h in range(CLOSE):
            s = active[CLOSE * t + h]
            f_b = table[2, s]
            z_b = pl.multiple_of(table[3, s], 16)
            offset = table[5, s]
            low_z = table[16, s] + 1
            band = (gap_base[...] >= offset - 1) & (gap_base[...] <= offset + 1)
            tops = [None] * 9
            lows = []
            for lag_x in range(3):
                part = jnp.where(band, acc[s, lag_x * ROWS_A:(lag_x + 1) * ROWS_A, :], 0.0)
                part = sum([part[8 * i:8 * i + 8] for i in range(ROWS_A // 8)])
                for lag_z in range(3):
                    hit = ((slant - (offset + lag_z - 1)) & 7) == 0
                    tops[3 * lag_z + lag_x] = jnp.sum(
                        jnp.where(hit, part, 0.0), axis=0, keepdims=True)
            for lag_z in range(3):
                low = low_z + lag_z - 1
                inside = (z_one >= low) & (z_one < low + W)
                lows.append(jnp.where(inside, acc[s, 3 * ROWS_A:3 * ROWS_A + 3, :], 0.0))
            stack = jnp.concatenate(tops + lows, axis=0)

            at = 2 * ROWS_A
            mask = masks[s, at:at + ROWS_B].astype(jnp.float32)
            ends = [
                fr_b[0, f_b, table[8 + i, s], pl.ds(z_b, ROWS_B), :].astype(jnp.float32)
                * (mask * table[10 + i, s].astype(jnp.float32))
                for i in range(2)
            ]
            row_b = jnp.where(
                lag_one == 1, acc[s, 3 * ROWS_A + 3:3 * ROWS_A + 4, :], 0.0)
            row_a = jnp.sum(acc[s, ROWS_A:2 * ROWS_A, LANES:], axis=0, keepdims=True)
            sums = [
                jnp.where(mean_lane, row_a, 0.0),
                jnp.sum(sq_a[s], axis=0, keepdims=True),
                jnp.sum(ends[0] + ends[1], axis=0, keepdims=True)
                + row_b[:, :LANES] + row_b[:, LANES:],
                jnp.sum(
                    sq_b[s] + (ends[0] * ends[0] + ends[1] * ends[1]), axis=0, keepdims=True),
            ]
            sums = jnp.sum(jnp.concatenate(sums, axis=0), axis=1, keepdims=True)
            total_18 = jnp.zeros((18, LANES), jnp.float32)
            for lag_y in range(3):
                part = jnp.sum(jnp.where(lag_18 == lag_y, stack, 0.0), axis=1, keepdims=True)
                total_18 = total_18 + jnp.where(lane_18 == s + SPREAD * lag_y, part, 0.0)
            out_ref[0:18] += total_18
            out_ref[18:22] += jnp.where(lane_4 == s, sums, 0.0)
        return carry

    lax.fori_loop(0, (alive + CLOSE - 1) // CLOSE, finish, 0)


def outer_kernel(
    plan_ref, pair_ref, other_ref, gap_base, fr_a, fr_b_in, masks_in, acc_in, sq_a_in, sq_b_in,
    out_ref, table_v, fr_b, masks, acc, sq_a, sq_b, table, units, active, sem_t,
):
    deep = fr_a.shape[3]
    planes = fr_a.shape[2] - 2 * PAD_A
    own = (acc.shape[0] - 1) // 3
    even = lax.axis_index("span") % 2 == 0
    base = REACH * deep
    from_pair, from_other = [
        ref[base:base + 8, 0:LANES].astype(jnp.float32).astype(jnp.int32)
        for ref in (pair_ref, other_ref)
    ]
    below = jnp.where(even, from_other, from_pair)
    above = jnp.where(even, from_pair, from_other)
    plan = plan_ref[...] + pltpu.roll(below, own, 1) + pltpu.roll(above, 2 * own, 1)
    target = decode(plan, own, planes, deep, False, table_v)
    to_scalar = pltpu.make_async_copy(table_v, table, sem_t)
    to_scalar.start()
    out_ref[...] = jnp.zeros(out_ref.shape, jnp.float32)
    out_ref[22:23] = target.astype(jnp.float32)

    low_at, high_at = CHUNK, PAD_B + planes
    pair_at = jnp.where(even, high_at, low_at)
    other_at = jnp.where(even, low_at, high_at)
    for p in range(REACH):
        frame(pair_ref[p * deep:(p + 1) * deep, :], fr_b, pair_at + p)
        frame(other_ref[p * deep:(p + 1) * deep, :], fr_b, other_at + p)
    to_scalar.wait()

    def prepare_own(s, carry):
        total, alive = carry
        active[alive] = s
        set_units(units, total, s, table[12, s], CHUNK, 2)
        return total + table[13, s], alive + table[17, s]

    carry = lax.fori_loop(0, own, prepare_own, (0, 0))

    def prepare(s, carry):
        total, alive = carry
        count = table[13, s]

        @pl.when(count > 0)
        def _():
            set_masks(masks, s, table)
            for ref in (acc, sq_a, sq_b):
                ref[s] = jnp.zeros(ref.shape[1:], jnp.float32)
            active[alive] = s
            set_units(units, total, s, table[12, s], CHUNK, W // CHUNK)

        return total + count, alive + jnp.where(count > 0, 1, 0)

    total, alive = lax.fori_loop(own, 3 * own, prepare, carry)
    spare = 3 * own
    for at in range(CLOSE - 1):
        active[alive + at] = spare
    run_units(CHUNK // 2, total, units, table, spare, fr_a, fr_b, acc, sq_a, sq_b, masks)
    finish_slots(alive, active, table, out_ref, gap_base, fr_b, masks, acc, sq_a, sq_b)


def rest_kernel(
    table_v, gap_base, fr_b, masks, acc, sq_a, sq_b, out_ref, table, active, sem_t,
):
    own = (acc.shape[0] - 1) // 3
    to_scalar = pltpu.make_async_copy(table_v, table, sem_t)
    to_scalar.start()
    out_ref[...] = jnp.zeros(out_ref.shape, jnp.float32)
    to_scalar.wait()

    def listed(s, alive):
        active[alive] = s
        return alive + 1 - table[17, s]

    alive = lax.fori_loop(0, own, listed, 0)
    for at in range(CLOSE - 1):
        active[alive + at] = 3 * own
    finish_slots(alive, active, table, out_ref, gap_base, fr_b, masks, acc, sq_a, sq_b)


def update_kernel(own, mine_ref, rest_ref, pair_ref, other_ref, out_ref):
    tile_rows = out_ref.shape[0]
    even = lax.axis_index("span") % 2 == 0
    mine = mine_ref[...] + rest_ref[...]
    pair = pair_ref[...]
    other = other_ref[...]
    below = jnp.where(even, other, pair)
    above = jnp.where(even, pair, other)
    lane = lax.broadcasted_iota(jnp.int32, mine.shape, 1)
    slot = lane & (SPREAD - 1)
    total = mine + jnp.where(
        slot < own,
        pltpu.roll(below, LANES - 2 * own, 1) + pltpu.roll(above, LANES - own, 1),
        jnp.where(
            slot < 2 * own, pltpu.roll(below, own, 1),
            jnp.where(slot < 3 * own, pltpu.roll(above, 2 * own, 1), 0.0)))

    def lead(v):
        return v + pltpu.roll(v, LANES - SPREAD, 1) + pltpu.roll(v, LANES - 2 * SPREAD, 1)

    def spread(v):
        v = jnp.where(lane[0:v.shape[0]] < SPREAD, v, 0.0)
        return v + pltpu.roll(v, SPREAD, 1) + pltpu.roll(v, 2 * SPREAD, 1)

    stats = spread(total[18:22])
    voxels = float(W) ** 3
    block_voxels = float(BLOCK) ** 3
    mean_a = stats[0:1] / voxels
    energy_a = jnp.maximum(stats[1:2] / voxels - mean_a * mean_a, 0.0)
    mean_b = stats[2:3] / block_voxels
    energy_b = jnp.maximum(stats[3:4] / block_voxels - mean_b * mean_b, 0.0)
    normaliser = voxels * jnp.sqrt((energy_a + EPSILON) * (energy_b + EPSILON))
    scaled = SHARP * ((total[0:9] - mean_a * total[9:18]) / normaliser)
    used = lane[0:9] < 3 * SPREAD
    scaled = jnp.where(used, scaled, -1e30)
    top = jnp.max(scaled, axis=0, keepdims=True)
    top = jnp.maximum(top, jnp.maximum(
        pltpu.roll(top, LANES - SPREAD, 1), pltpu.roll(top, LANES - 2 * SPREAD, 1)))
    weights = jnp.where(used, jnp.exp(scaled - spread(top)), 0.0)
    lag_row = lax.broadcasted_iota(jnp.int32, weights.shape, 0)
    lag_z = jnp.where(lag_row >= 6, 1.0, jnp.where(lag_row >= 3, 0.0, -1.0))
    lag_x = jnp.where(
        (lag_row == 0) | (lag_row == 3) | (lag_row == 6), -1.0,
        jnp.where((lag_row == 2) | (lag_row == 5) | (lag_row == 8), 1.0, 0.0))
    lag_y = jnp.where(lane[0:1] >= 2 * SPREAD, 1.0, jnp.where(lane[0:1] >= SPREAD, 0.0, -1.0))
    column = jnp.sum(weights, axis=0, keepdims=True)
    moments = lead(jnp.concatenate([
        column * lag_y,
        jnp.sum(weights * lag_z, axis=0, keepdims=True),
        jnp.sum(weights * lag_x, axis=0, keepdims=True),
        column,
        jnp.zeros((4, LANES), jnp.float32),
    ], axis=0))
    found = jnp.where(lane[0:8] < 3 * own, moments / moments[3:4], 0.0)
    high = found.astype(jnp.bfloat16).astype(jnp.float32)
    left = found - high
    middle = left.astype(jnp.bfloat16).astype(jnp.float32)
    parts = jnp.concatenate(
        [high, middle, left - middle, jnp.zeros((8, LANES), jnp.float32)], axis=0
    ).astype(jnp.bfloat16)
    place = lax.broadcasted_iota(jnp.int32, ((tile_rows + 2) * GZX, LANES), 0)
    node = jnp.where(place == mine[22:23].astype(jnp.int32), 1.0, 0.0).astype(jnp.bfloat16)
    field = lax.dot_general(
        parts, node, (((1,), (1,)), ((), ())), preferred_element_type=jnp.float32)
    field = field[0:8] + field[8:16] + field[16:24]
    lane_x = lane[0:8] & (GX - 1)
    for row in range(tile_rows):
        before, centre, after = [
            field[:, (row + i) * GZX:(row + i + 1) * GZX] for i in range(3)]
        near = before + after
        near = near + jnp.where(lane[0:8] >= GX, pltpu.roll(centre, GX, 1), 0.0)
        near = near + jnp.where(lane[0:8] < GZX - GX, pltpu.roll(centre, LANES - GX, 1), 0.0)
        near = near + jnp.where(lane_x >= 1, pltpu.roll(centre, 1, 1), 0.0)
        near = near + jnp.where(lane_x < GX - 1, pltpu.roll(centre, LANES - 1, 1), 0.0)
        out_ref[row] = (0.4 * centre + 0.1 * near)[0:3]


def shards(first, second, windows, shifts):
    planes, deep, along = first.shape
    own = windows.shape[0]
    slots = 3 * own + 1
    count = lax.axis_size("span")
    pairs = [(i, i ^ 1) for i in range(count)]
    others = [(i, i + 1) for i in range(1, count - 1, 2)]
    others = others + [(b, a) for a, b in others]
    vmem = pl.BlockSpec(memory_space=pltpu.VMEM)

    def limit(mib):
        return pltpu.CompilerParams(vmem_limit_bytes=mib << 20)

    busy = pl.CostEstimate(flops=20 * 10**9, bytes_accessed=0, transcendentals=0)
    gap = pl.pallas_call(
        table_kernel,
        out_shape=jax.ShapeDtypeStruct((ROWS_A, 2 * LANES), jnp.int32),
        out_specs=vmem,
        compiler_params=limit(4),
        cost_estimate=pl.CostEstimate(flops=13 * 10**8, bytes_accessed=0, transcendentals=0),
        name="gap_table",
    )()
    message = jax.ShapeDtypeStruct((REACH * deep + PLAN_ROWS, along), second.dtype)
    tile, gap = lax.optimization_barrier((second, gap))
    low_planes, high_planes = tile[:REACH], tile[planes - REACH:]
    to_pair, to_other, plan = pl.pallas_call(
        send_kernel,
        out_shape=(message, message, jax.ShapeDtypeStruct((8, LANES), jnp.int32)),
        in_specs=[vmem] * 5,
        out_specs=(vmem,) * 3,
        compiler_params=limit(4),
        cost_estimate=busy,
        name="planes_to_send",
    )(windows[None], shifts, gap, low_planes, high_planes)
    from_other = lax.ppermute(to_other, "span", others)
    from_pair = lax.ppermute(to_pair, "span", pairs)
    mask_rows = 2 * (ROWS_A + ROWS_B + 16)
    frames_a = jax.ShapeDtypeStruct((2, 2, planes + 2 * PAD_A, deep, LANES), jnp.bfloat16)
    state = (
        jax.ShapeDtypeStruct((2, 2, planes + 2 * PAD_B, deep, LANES), jnp.bfloat16),
        jax.ShapeDtypeStruct((slots, mask_rows, LANES), jnp.bfloat16),
        jax.ShapeDtypeStruct((slots, 3 * ROWS_A + 16, 2 * LANES), jnp.float32),
        jax.ShapeDtypeStruct((slots, ROWS_A, LANES), jnp.float32),
        jax.ShapeDtypeStruct((slots, ROWS_B, LANES), jnp.float32),
    )
    scratch = [
        pltpu.SMEM((FIELDS, LANES), jnp.int32),
        pltpu.SMEM(((3 * own + 1) * (W // CHUNK) + PAIR,), jnp.int32),
    ]
    held = pl.pallas_call(
        inner_kernel,
        out_shape=(frames_a, *state),
        in_specs=[vmem] * 3,
        out_specs=(vmem,) * 6,
        scratch_shapes=[
            pltpu.VMEM((FIELDS, LANES), jnp.int32), *scratch, pltpu.SemaphoreType.DMA],
        compiler_params=limit(8),
        cost_estimate=busy,
        name="inner_sums",
    )(plan, first, second)
    sums, fields, *held = pl.pallas_call(
        outer_kernel,
        out_shape=(
            jax.ShapeDtypeStruct((24, LANES), jnp.float32),
            jax.ShapeDtypeStruct((FIELDS, LANES), jnp.int32), *state),
        in_specs=[vmem] * 10,
        out_specs=(vmem,) * 7,
        input_output_aliases={5 + i: 2 + i for i in range(5)},
        scratch_shapes=[
            *scratch, pltpu.SMEM((slots + CLOSE,), jnp.int32), pltpu.SemaphoreType.DMA],
        compiler_params=limit(8),
        name="outer_sums",
    )(plan, from_pair, from_other, gap, *held)
    other_sums = lax.ppermute(sums, "span", others)
    pair_sums = lax.ppermute(sums, "span", pairs)
    rest = pl.pallas_call(
        rest_kernel,
        out_shape=jax.ShapeDtypeStruct((24, LANES), jnp.float32),
        in_specs=[vmem] * 7,
        out_specs=vmem,
        scratch_shapes=[
            pltpu.SMEM((FIELDS, LANES), jnp.int32), pltpu.SMEM((slots + CLOSE,), jnp.int32),
            pltpu.SemaphoreType.DMA],
        compiler_params=limit(8),
        cost_estimate=busy,
        name="rest_of_sums",
    )(fields, gap, *held)
    field = pl.pallas_call(
        functools.partial(update_kernel, own),
        out_shape=jax.ShapeDtypeStruct((planes // STRIDE, 3, GZX), jnp.float32),
        in_specs=[vmem] * 4,
        out_specs=vmem,
        compiler_params=limit(4),
        name="smoothed_update",
    )(sums, rest, pair_sums, other_sums)
    return jnp.transpose(field, (1, 0, 2))


def solution(mesh):
    in_specs = (
        P(("grp", "span"), None, None),
        P(("grp", "span"), None, None),
        P(("grp", "span")),
        P(None, ("grp", "span")),
    )
    out_specs = P(None, ("grp", "span"), None)
    return jax.shard_map(shards, mesh=mesh, in_specs=in_specs, out_specs=out_specs, check_vma=False)
```

```python
import functools

import jax
import jax.numpy as jnp
from jax import lax
from jax.experimental import pallas as pl
from jax.experimental.pallas import tpu as pltpu
from jax.sharding import PartitionSpec as P

W = 48
STRIDE = 12
DYM = 3
GX = 16
GZX = 128
SHARP = 80.0
EPSILON = 1e-06

HALF = W // 2
BLOCK = W + 2
REACH = DYM + 1
LANES = 128
HOP = 64
CHUNK = 6
ROWS_A = 64
ROWS_B = 80
PAD_A = CHUNK
PAD_B = CHUNK + REACH
PIECES = 2
SPREAD = 32
PLAN_ROWS = 16
FIELDS = 24
PAIR = 8
REST = 4
CLOSE = 4
FAR = 4096


def table_kernel(gap_ref):
    row = lax.broadcasted_iota(jnp.int32, gap_ref.shape, 0)
    col = lax.broadcasted_iota(jnp.int32, gap_ref.shape, 1)
    lag = jnp.where(col >= ROWS_B, 1, 0) + jnp.where(col >= 2 * ROWS_B, 1, 0)
    gap_ref[...] = jnp.where(col < 3 * ROWS_B, col - lag * ROWS_B - row, FAR)


def send_kernel(win_ref, shift_ref, gap_ref, low_ref, high_ref, pair_ref, other_ref, plan_ref):
    reach, deep, along = low_ref.shape
    even = lax.axis_index("span") % 2 == 0
    node = win_ref[...]
    own = node.shape[1]
    plan_ref[...] = jnp.zeros(plan_ref.shape, jnp.int32)
    plan_ref[0:1, 0:own] = node >> 8
    plan_ref[1:2, 0:own] = node & 255
    plan_ref[2:5, 0:own] = shift_ref[...]
    plan = plan_ref[...].astype(jnp.float32).astype(jnp.bfloat16)
    for ref in (pair_ref, other_ref):
        ref[reach * deep:reach * deep + 8, 0:LANES] = plan

    def fill(to_low, to_high):
        for p in range(reach):
            to_low[p * deep:(p + 1) * deep, :] = low_ref[p]
            to_high[p * deep:(p + 1) * deep, :] = high_ref[p]

    @pl.when(even)
    def _():
        fill(other_ref, pair_ref)

    @pl.when(jnp.logical_not(even))
    def _():
        fill(pair_ref, other_ref)


def decode(plan, own, planes, deep, inner, table):
    device = lax.axis_index("span")
    last = lax.axis_size("span") - 1
    tile_rows = planes // STRIDE
    slot = lax.broadcasted_iota(jnp.int32, (1, LANES), 1)
    node = plan[0:1] * 256 + plan[1:2]
    dy, dz, dx = plan[2:3], plan[3:4], plan[4:5]
    row = (node >> (GZX.bit_length() - 1)) - device * tile_rows
    rest = node & (GZX - 1)
    cy = STRIDE * row + STRIDE // 2
    cz = STRIDE * (rest >> (GX.bit_length() - 1)) + STRIDE // 2
    cx = STRIDE * (rest & (GX - 1)) + STRIDE // 2
    start = jnp.maximum(cy - HALF, jnp.where(device == 0, -CHUNK, 0))
    stop = jnp.minimum(cy + HALF, jnp.where(device == last, planes + CHUNK, planes))
    mine = slot < own
    lower = (slot >= own) & (slot < 2 * own)
    upper = (slot >= 2 * own) & (slot < 3 * own)
    wanted = (
        mine | (lower & (row < 0) & (row >= -tile_rows))
        | (upper & (row >= tile_rows) & (row < 2 * tile_rows))
    )
    if inner:
        low = jnp.maximum(start, CHUNK)
        high = jnp.minimum(stop, planes - CHUNK)
        wanted = mine
    else:
        below = start < CHUNK
        low = jnp.where(mine & jnp.logical_not(below), planes - CHUNK, start)
        high = jnp.where(mine & below, CHUNK, stop)
    width = jnp.where(wanted, high - low, 0)
    count = sum([jnp.where(width > CHUNK * c, 1, 0) for c in range(W // CHUNK)])
    sx = cx + dx - HALF - 1
    sz = cz + dz - HALF - 1
    z_a = jnp.minimum(jnp.maximum(cz - HALF, 0) & -16, deep - ROWS_A)
    z_b = jnp.where(sz + BLOCK <= ROWS_B, 0, deep - ROWS_B)
    values = (
        jnp.where(cx + HALF <= LANES, 0, 1),
        z_a,
        jnp.where(sx + BLOCK <= LANES, 0, 1),
        z_b,
        dy,
        z_a + dz - z_b,
        (dx + LANES) & (LANES - 1),
        cz - HALF - z_a,
        start + dy - 1 + PAD_B,
        stop + dy + PAD_B,
        jnp.where(start == cy - HALF, 1, 0),
        jnp.where(stop == cy + HALF, 1, 0),
        low,
        count,
        cx - HALF,
        sx,
        sz - z_b,
        jnp.where((row == 0) | (row == tile_rows - 1), 1, 0),
    )
    for at, value in enumerate(values):
        table[at:at + 1, :] = jnp.where(slot < 3 * own, value, 0)
    return jnp.where(
        mine | (lower & (row == -1)) | (upper & (row == tile_rows)),
        (row + 1) * GZX + rest, -1)


def set_masks(masks, s, table):
    f_a, f_b = table[0, s], table[2, s]
    z_from, x_from = table[7, s], table[14, s]
    sx, zb_from = table[15, s], table[16, s]
    reach_x = sx + 1

    def in_x(rows, half, frame_at, low, high):
        lane = (lax.broadcasted_iota(jnp.int32, (rows, LANES), 1) + half * HOP) & (LANES - 1)
        x = lane + jnp.where(lane < HOP, LANES * frame_at, 0)
        return (x >= low) & (x < high)

    def in_z(rows, low, count):
        z = lax.broadcasted_iota(jnp.int32, (rows, LANES), 0)
        return (z >= low) & (z < low + count)

    row = lax.broadcasted_iota(jnp.int32, (16, LANES), 0)
    wide = row == 3
    low = jnp.where(wide, sx, reach_x + row - 1)
    high = low + jnp.where(wide, BLOCK, jnp.where(row < 3, W, 0))
    z_a = in_z(ROWS_A, z_from, W)
    z_b = in_z(ROWS_B, zb_from, BLOCK)
    at = 0
    for rows, frame_at, x_low, x_high, z in (
        (ROWS_A, f_a, x_from, x_from + W, z_a),
        (ROWS_B, f_b, sx, sx + BLOCK, z_b),
        (16, f_b, low, high, None),
    ):
        for half in range(2):
            inside = in_x(rows, half, frame_at, x_low, x_high)
            inside = inside if z is None else inside & z
            masks[s, at:at + rows] = jnp.where(inside, 1.0, 0.0).astype(jnp.bfloat16)
            at += rows


def set_units(units, total, s, low, planes, most):
    for c in range(most):
        units[total + c] = s + (low + planes * c + 64) * 256


def frame(v, fr, at):
    low = v[:, :LANES]
    high = jnp.concatenate([v[:, LANES:], v[:, HOP:LANES]], axis=1)
    fr[0, 0, at] = low
    fr[0, 1, at] = high
    fr[1, 0, at] = pltpu.roll(low, HOP, 1)
    fr[1, 1, at] = pltpu.roll(high, HOP, 1)


def run_units(half, total, units, table, spare, fr_a, fr_b, acc, sq_a, sq_b, masks):
    for at in range(REST - 1):
        units[total + at] = spare + 64 * 256
    ones = jnp.where(
        lax.broadcasted_iota(jnp.int32, (16, half * LANES), 0) == 0, 1.0, 0.0
    ).astype(jnp.bfloat16)

    def step(first, width):
        for h in range(width):
            code = units[first + h]
            s = code & 255
            y = (code >> 8) - 64
            y_two = y + half
            f_a = table[0, s]
            z_a = pl.multiple_of(table[1, s], 16)
            f_b = table[2, s]
            z_b = pl.multiple_of(table[3, s], 16)
            dy = table[4, s]
            dx = table[6, s]
            one_a = masks[s, 0:ROWS_A]
            two_a = masks[s, ROWS_A:2 * ROWS_A]
            at = 2 * ROWS_A
            one_b = masks[s, at:at + ROWS_B]
            two_b = masks[s, at + ROWS_B:at + 2 * ROWS_B]
            at += 2 * ROWS_B
            rows = masks[s, at:at + 16] + masks[s, at + 16:at + 32]
            a = [
                fr_a[0, f_a, y + PAD_A + p, pl.ds(z_a, ROWS_A), :] * one_a
                + fr_a[1, f_a, y_two + PAD_A + p, pl.ds(z_a, ROWS_A), :] * two_a
                for p in range(half)
            ]
            b = [
                fr_b[0, f_b, y + dy - 1 + PAD_B + p, pl.ds(z_b, ROWS_B), :] * one_b
                + fr_b[1, f_b, y_two + dy - 1 + PAD_B + p, pl.ds(z_b, ROWS_B), :] * two_b
                for p in range(half + 2)
            ]
            left = [
                jnp.concatenate(
                    [pltpu.roll(v, (dx + lag - 1 + LANES) & (LANES - 1), 1) for v in a], axis=1)
                for lag in range(3)
            ]
            left.append(jnp.concatenate([rows] * half, axis=1))
            left = jnp.concatenate(left, axis=0)
            right = [jnp.concatenate(b[lag:lag + half], axis=1) for lag in range(3)]
            right = jnp.concatenate(right + [ones], axis=0)
            acc[s] += lax.dot_general(
                left, right, (((1,), (1,)), ((), ())), preferred_element_type=jnp.float32)
            wide = [v.astype(jnp.float32) for v in a]
            sq_a[s] += sum([v * v for v in wide])
            wide = [v.astype(jnp.float32) for v in b[1:-1]]
            sq_b[s] += sum([v * v for v in wide])

    def wide_step(t, carry):
        step(PAIR * t, PAIR)
        return carry

    full = (total + REST - 1) // PAIR
    lax.fori_loop(0, full, wide_step, 0)

    @pl.when(total > PAIR * full)
    def _():
        step(PAIR * full, REST)


def inner_kernel(
    plan_ref, first_ref, second_ref, fr_a, fr_b, masks, acc, sq_a, sq_b,
    table_v, table, units, sem_t,
):
    planes, deep, along = first_ref.shape
    own = (acc.shape[0] - 1) // 3
    device = lax.axis_index("span")
    last = lax.axis_size("span") - 1
    piece = planes // PIECES
    decode(plan_ref[...], own, planes, deep, True, table_v)
    to_scalar = pltpu.make_async_copy(table_v, table, sem_t)
    to_scalar.start()
    for ref, fr, pad in ((first_ref, fr_a, PAD_A), (second_ref, fr_b, PAD_B)):
        def body(i, carry, ref=ref, fr=fr, pad=pad):
            for p in range(piece):
                at = i * piece + p
                frame(ref[at], fr, at + pad)
            return carry

        lax.fori_loop(0, PIECES, body, 0)

    @pl.when((device == 0) | (device == last))
    def _():
        zero = jnp.zeros((2, 2, CHUNK, deep, LANES), jnp.bfloat16)
        fr_a[:, :, 0:PAD_A] = zero
        fr_a[:, :, PAD_A + planes:] = zero
        fr_b[:, :, 0:CHUNK] = zero
        fr_b[:, :, PAD_B + planes + REACH:] = zero

    to_scalar.wait()

    def prepare(s, total):
        set_masks(masks, s, table)
        for ref in (acc, sq_a, sq_b):
            ref[s] = jnp.zeros(ref.shape[1:], jnp.float32)
        set_units(units, total, s, table[12, s], 2 * CHUNK, W // CHUNK // 2)
        return total + (table[13, s] >> 1)

    total = lax.fori_loop(0, own, prepare, 0)
    run_units(CHUNK, total, units, table, 3 * own, fr_a, fr_b, acc, sq_a, sq_b, masks)


def finish_slots(alive, active, table, out_ref, gap_base, fr_b, masks, acc, sq_a, sq_b):
    cols = 2 * LANES
    col_one = lax.broadcasted_iota(jnp.int32, (1, cols), 1)
    lag_one = jnp.where(col_one >= ROWS_B, 1, 0) + jnp.where(col_one >= 2 * ROWS_B, 1, 0)
    lag_one = lag_one + jnp.where(col_one >= 3 * ROWS_B, 1, 0)
    z_one = col_one - lag_one * ROWS_B
    lag_18 = jnp.broadcast_to(lag_one, (18, cols))
    lane_18 = lax.broadcasted_iota(jnp.int32, (18, LANES), 1)
    lane_4 = lax.broadcasted_iota(jnp.int32, (4, LANES), 1)
    slant = lax.broadcasted_iota(jnp.int32, (8, cols), 1)
    slant = slant - lax.broadcasted_iota(jnp.int32, (8, cols), 0)
    mean_lane = lax.broadcasted_iota(jnp.int32, (1, LANES), 1) == 3 * ROWS_B - LANES

    def finish(t, carry):
        for h in range(CLOSE):
            s = active[CLOSE * t + h]
            f_b = table[2, s]
            z_b = pl.multiple_of(table[3, s], 16)
            offset = table[5, s]
            low_z = table[16, s] + 1
            band = (gap_base[...] >= offset - 1) & (gap_base[...] <= offset + 1)
            tops = [None] * 9
            lows = []
            for lag_x in range(3):
                part = jnp.where(band, acc[s, lag_x * ROWS_A:(lag_x + 1) * ROWS_A, :], 0.0)
                part = sum([part[8 * i:8 * i + 8] for i in range(ROWS_A // 8)])
                for lag_z in range(3):
                    hit = ((slant - (offset + lag_z - 1)) & 7) == 0
                    tops[3 * lag_z + lag_x] = jnp.sum(
                        jnp.where(hit, part, 0.0), axis=0, keepdims=True)
            for lag_z in range(3):
                low = low_z + lag_z - 1
                inside = (z_one >= low) & (z_one < low + W)
                lows.append(jnp.where(inside, acc[s, 3 * ROWS_A:3 * ROWS_A + 3, :], 0.0))
            stack = jnp.concatenate(tops + lows, axis=0)

            at = 2 * ROWS_A
            mask = masks[s, at:at + ROWS_B].astype(jnp.float32)
            ends = [
                fr_b[0, f_b, table[8 + i, s], pl.ds(z_b, ROWS_B), :].astype(jnp.float32)
                * (mask * table[10 + i, s].astype(jnp.float32))
                for i in range(2)
            ]
            row_b = jnp.where(
                lag_one == 1, acc[s, 3 * ROWS_A + 3:3 * ROWS_A + 4, :], 0.0)
            row_a = jnp.sum(acc[s, ROWS_A:2 * ROWS_A, LANES:], axis=0, keepdims=True)
            sums = [
                jnp.where(mean_lane, row_a, 0.0),
                jnp.sum(sq_a[s], axis=0, keepdims=True),
                jnp.sum(ends[0] + ends[1], axis=0, keepdims=True)
                + row_b[:, :LANES] + row_b[:, LANES:],
                jnp.sum(
                    sq_b[s] + (ends[0] * ends[0] + ends[1] * ends[1]), axis=0, keepdims=True),
            ]
            sums = jnp.sum(jnp.concatenate(sums, axis=0), axis=1, keepdims=True)
            total_18 = jnp.zeros((18, LANES), jnp.float32)
            for lag_y in range(3):
                part = jnp.sum(jnp.where(lag_18 == lag_y, stack, 0.0), axis=1, keepdims=True)
                total_18 = total_18 + jnp.where(lane_18 == s + SPREAD * lag_y, part, 0.0)
            out_ref[0:18] += total_18
            out_ref[18:22] += jnp.where(lane_4 == s, sums, 0.0)
        return carry

    lax.fori_loop(0, (alive + CLOSE - 1) // CLOSE, finish, 0)


def outer_kernel(
    plan_ref, pair_ref, other_ref, gap_base, fr_a, fr_b_in, masks_in, acc_in, sq_a_in, sq_b_in,
    out_ref, table_v, fr_b, masks, acc, sq_a, sq_b, table, units, active, sem_t,
):
    deep = fr_a.shape[3]
    planes = fr_a.shape[2] - 2 * PAD_A
    own = (acc.shape[0] - 1) // 3
    even = lax.axis_index("span") % 2 == 0
    base = REACH * deep
    from_pair, from_other = [
        ref[base:base + 8, 0:LANES].astype(jnp.float32).astype(jnp.int32)
        for ref in (pair_ref, other_ref)
    ]
    below = jnp.where(even, from_other, from_pair)
    above = jnp.where(even, from_pair, from_other)
    plan = plan_ref[...] + pltpu.roll(below, own, 1) + pltpu.roll(above, 2 * own, 1)
    target = decode(plan, own, planes, deep, False, table_v)
    to_scalar = pltpu.make_async_copy(table_v, table, sem_t)
    to_scalar.start()
    out_ref[...] = jnp.zeros(out_ref.shape, jnp.float32)
    out_ref[22:23] = target.astype(jnp.float32)

    low_at, high_at = CHUNK, PAD_B + planes
    pair_at = jnp.where(even, high_at, low_at)
    other_at = jnp.where(even, low_at, high_at)
    for p in range(REACH):
        frame(pair_ref[p * deep:(p + 1) * deep, :], fr_b, pair_at + p)
        frame(other_ref[p * deep:(p + 1) * deep, :], fr_b, other_at + p)
    to_scalar.wait()

    def prepare_own(s, carry):
        total, alive = carry
        active[alive] = s
        set_units(units, total, s, table[12, s], CHUNK, 2)
        return total + table[13, s] * table[17, s], alive + table[17, s]

    carry = lax.fori_loop(0, own, prepare_own, (0, 0))

    def prepare(s, carry):
        total, alive = carry
        count = table[13, s]

        @pl.when(count > 0)
        def _():
            set_masks(masks, s, table)
            for ref in (acc, sq_a, sq_b):
                ref[s] = jnp.zeros(ref.shape[1:], jnp.float32)
            active[alive] = s
            set_units(units, total, s, table[12, s], CHUNK, W // CHUNK)

        return total + count, alive + jnp.where(count > 0, 1, 0)

    total, alive = lax.fori_loop(own, 3 * own, prepare, carry)
    spare = 3 * own
    for at in range(CLOSE - 1):
        active[alive + at] = spare
    run_units(CHUNK // 2, total, units, table, spare, fr_a, fr_b, acc, sq_a, sq_b, masks)
    finish_slots(alive, active, table, out_ref, gap_base, fr_b, masks, acc, sq_a, sq_b)


def rest_kernel(
    table_v, gap_base, fr_a, fr_b, masks, acc_in, sq_a_in, sq_b_in,
    out_ref, acc, sq_a, sq_b, table, units, active, sem_t,
):
    own = (acc.shape[0] - 1) // 3
    to_scalar = pltpu.make_async_copy(table_v, table, sem_t)
    to_scalar.start()
    out_ref[...] = jnp.zeros(out_ref.shape, jnp.float32)
    to_scalar.wait()

    def listed(s, carry):
        total, alive = carry
        active[alive] = s
        set_units(units, total, s, table[12, s], CHUNK, 2)
        other = 1 - table[17, s]
        return total + table[13, s] * other, alive + other

    total, alive = lax.fori_loop(0, own, listed, (0, 0))
    spare = 3 * own
    for at in range(CLOSE - 1):
        active[alive + at] = spare
    run_units(CHUNK // 2, total, units, table, spare, fr_a, fr_b, acc, sq_a, sq_b, masks)
    finish_slots(alive, active, table, out_ref, gap_base, fr_b, masks, acc, sq_a, sq_b)


def update_kernel(own, mine_ref, rest_ref, pair_ref, other_ref, out_ref):
    tile_rows = out_ref.shape[0]
    even = lax.axis_index("span") % 2 == 0
    mine = mine_ref[...] + rest_ref[...]
    pair = pair_ref[...]
    other = other_ref[...]
    below = jnp.where(even, other, pair)
    above = jnp.where(even, pair, other)
    lane = lax.broadcasted_iota(jnp.int32, mine.shape, 1)
    slot = lane & (SPREAD - 1)
    total = mine + jnp.where(
        slot < own,
        pltpu.roll(below, LANES - 2 * own, 1) + pltpu.roll(above, LANES - own, 1),
        jnp.where(
            slot < 2 * own, pltpu.roll(below, own, 1),
            jnp.where(slot < 3 * own, pltpu.roll(above, 2 * own, 1), 0.0)))

    def lead(v):
        return v + pltpu.roll(v, LANES - SPREAD, 1) + pltpu.roll(v, LANES - 2 * SPREAD, 1)

    def spread(v):
        v = jnp.where(lane[0:v.shape[0]] < SPREAD, v, 0.0)
        return v + pltpu.roll(v, SPREAD, 1) + pltpu.roll(v, 2 * SPREAD, 1)

    stats = spread(total[18:22])
    voxels = float(W) ** 3
    block_voxels = float(BLOCK) ** 3
    mean_a = stats[0:1] / voxels
    energy_a = jnp.maximum(stats[1:2] / voxels - mean_a * mean_a, 0.0)
    mean_b = stats[2:3] / block_voxels
    energy_b = jnp.maximum(stats[3:4] / block_voxels - mean_b * mean_b, 0.0)
    normaliser = voxels * jnp.sqrt((energy_a + EPSILON) * (energy_b + EPSILON))
    scaled = SHARP * ((total[0:9] - mean_a * total[9:18]) / normaliser)
    used = lane[0:9] < 3 * SPREAD
    scaled = jnp.where(used, scaled, -1e30)
    top = jnp.max(scaled, axis=0, keepdims=True)
    top = jnp.maximum(top, jnp.maximum(
        pltpu.roll(top, LANES - SPREAD, 1), pltpu.roll(top, LANES - 2 * SPREAD, 1)))
    weights = jnp.where(used, jnp.exp(scaled - spread(top)), 0.0)
    lag_row = lax.broadcasted_iota(jnp.int32, weights.shape, 0)
    lag_z = jnp.where(lag_row >= 6, 1.0, jnp.where(lag_row >= 3, 0.0, -1.0))
    lag_x = jnp.where(
        (lag_row == 0) | (lag_row == 3) | (lag_row == 6), -1.0,
        jnp.where((lag_row == 2) | (lag_row == 5) | (lag_row == 8), 1.0, 0.0))
    lag_y = jnp.where(lane[0:1] >= 2 * SPREAD, 1.0, jnp.where(lane[0:1] >= SPREAD, 0.0, -1.0))
    column = jnp.sum(weights, axis=0, keepdims=True)
    moments = lead(jnp.concatenate([
        column * lag_y,
        jnp.sum(weights * lag_z, axis=0, keepdims=True),
        jnp.sum(weights * lag_x, axis=0, keepdims=True),
        column,
        jnp.zeros((4, LANES), jnp.float32),
    ], axis=0))
    found = jnp.where(lane[0:8] < 3 * own, moments / moments[3:4], 0.0)
    high = found.astype(jnp.bfloat16).astype(jnp.float32)
    left = found - high
    middle = left.astype(jnp.bfloat16).astype(jnp.float32)
    parts = jnp.concatenate(
        [high, middle, left - middle, jnp.zeros((8, LANES), jnp.float32)], axis=0
    ).astype(jnp.bfloat16)
    place = lax.broadcasted_iota(jnp.int32, ((tile_rows + 2) * GZX, LANES), 0)
    node = jnp.where(place == mine[22:23].astype(jnp.int32), 1.0, 0.0).astype(jnp.bfloat16)
    field = lax.dot_general(
        parts, node, (((1,), (1,)), ((), ())), preferred_element_type=jnp.float32)
    field = field[0:8] + field[8:16] + field[16:24]
    lane_x = lane[0:8] & (GX - 1)
    for row in range(tile_rows):
        before, centre, after = [
            field[:, (row + i) * GZX:(row + i + 1) * GZX] for i in range(3)]
        near = before + after
        near = near + jnp.where(lane[0:8] >= GX, pltpu.roll(centre, GX, 1), 0.0)
        near = near + jnp.where(lane[0:8] < GZX - GX, pltpu.roll(centre, LANES - GX, 1), 0.0)
        near = near + jnp.where(lane_x >= 1, pltpu.roll(centre, 1, 1), 0.0)
        near = near + jnp.where(lane_x < GX - 1, pltpu.roll(centre, LANES - 1, 1), 0.0)
        out_ref[row] = (0.4 * centre + 0.1 * near)[0:3]


def shards(first, second, windows, shifts):
    planes, deep, along = first.shape
    own = windows.shape[0]
    slots = 3 * own + 1
    count = lax.axis_size("span")
    pairs = [(i, i ^ 1) for i in range(count)]
    others = [(i, i + 1) for i in range(1, count - 1, 2)]
    others = others + [(b, a) for a, b in others]
    vmem = pl.BlockSpec(memory_space=pltpu.VMEM)

    def limit(mib):
        return pltpu.CompilerParams(vmem_limit_bytes=mib << 20)

    busy = pl.CostEstimate(flops=20 * 10**9, bytes_accessed=0, transcendentals=0)
    gap = pl.pallas_call(
        table_kernel,
        out_shape=jax.ShapeDtypeStruct((ROWS_A, 2 * LANES), jnp.int32),
        out_specs=vmem,
        compiler_params=limit(4),
        cost_estimate=pl.CostEstimate(flops=13 * 10**8, bytes_accessed=0, transcendentals=0),
        name="gap_table",
    )()
    message = jax.ShapeDtypeStruct((REACH * deep + PLAN_ROWS, along), second.dtype)
    tile, gap = lax.optimization_barrier((second, gap))
    low_planes, high_planes = tile[:REACH], tile[planes - REACH:]
    to_pair, to_other, plan = pl.pallas_call(
        send_kernel,
        out_shape=(message, message, jax.ShapeDtypeStruct((8, LANES), jnp.int32)),
        in_specs=[vmem] * 5,
        out_specs=(vmem,) * 3,
        compiler_params=limit(4),
        cost_estimate=busy,
        name="planes_to_send",
    )(windows[None], shifts, gap, low_planes, high_planes)
    from_other = lax.ppermute(to_other, "span", others)
    from_pair = lax.ppermute(to_pair, "span", pairs)
    mask_rows = 2 * (ROWS_A + ROWS_B + 16)
    frames_a = jax.ShapeDtypeStruct((2, 2, planes + 2 * PAD_A, deep, LANES), jnp.bfloat16)
    state = (
        jax.ShapeDtypeStruct((2, 2, planes + 2 * PAD_B, deep, LANES), jnp.bfloat16),
        jax.ShapeDtypeStruct((slots, mask_rows, LANES), jnp.bfloat16),
        jax.ShapeDtypeStruct((slots, 3 * ROWS_A + 16, 2 * LANES), jnp.float32),
        jax.ShapeDtypeStruct((slots, ROWS_A, LANES), jnp.float32),
        jax.ShapeDtypeStruct((slots, ROWS_B, LANES), jnp.float32),
    )
    scratch = [
        pltpu.SMEM((FIELDS, LANES), jnp.int32),
        pltpu.SMEM(((3 * own + 1) * (W // CHUNK) + PAIR,), jnp.int32),
    ]
    fr_a, *held = pl.pallas_call(
        inner_kernel,
        out_shape=(frames_a, *state),
        in_specs=[vmem] * 3,
        out_specs=(vmem,) * 6,
        scratch_shapes=[
            pltpu.VMEM((FIELDS, LANES), jnp.int32), *scratch, pltpu.SemaphoreType.DMA],
        compiler_params=limit(8),
        cost_estimate=busy,
        name="inner_sums",
    )(plan, first, second)
    sums, fields, *held = pl.pallas_call(
        outer_kernel,
        out_shape=(
            jax.ShapeDtypeStruct((24, LANES), jnp.float32),
            jax.ShapeDtypeStruct((FIELDS, LANES), jnp.int32), *state),
        in_specs=[vmem] * 10,
        out_specs=(vmem,) * 7,
        input_output_aliases={5 + i: 2 + i for i in range(5)},
        scratch_shapes=[
            *scratch, pltpu.SMEM((slots + CLOSE,), jnp.int32), pltpu.SemaphoreType.DMA],
        compiler_params=limit(8),
        name="outer_sums",
    )(plan, from_pair, from_other, gap, fr_a, *held)
    other_sums = lax.ppermute(sums, "span", others)
    pair_sums = lax.ppermute(sums, "span", pairs)
    rest, *_ = pl.pallas_call(
        rest_kernel,
        out_shape=(jax.ShapeDtypeStruct((24, LANES), jnp.float32), *state[2:]),
        in_specs=[vmem] * 8,
        out_specs=(vmem,) * 4,
        input_output_aliases={5 + i: 1 + i for i in range(3)},
        scratch_shapes=[
            *scratch, pltpu.SMEM((slots + CLOSE,), jnp.int32), pltpu.SemaphoreType.DMA],
        compiler_params=limit(8),
        cost_estimate=busy,
        name="rest_of_sums",
    )(fields, gap, fr_a, *held)
    field = pl.pallas_call(
        functools.partial(update_kernel, own),
        out_shape=jax.ShapeDtypeStruct((planes // STRIDE, 3, GZX), jnp.float32),
        in_specs=[vmem] * 4,
        out_specs=vmem,
        compiler_params=limit(4),
        name="smoothed_update",
    )(sums, rest, pair_sums, other_sums)
    return jnp.transpose(field, (1, 0, 2))


def solution(mesh):
    in_specs = (
        P(("grp", "span"), None, None),
        P(("grp", "span"), None, None),
        P(("grp", "span")),
        P(None, ("grp", "span")),
    )
    out_specs = P(None, ("grp", "span"), None)
    return jax.shard_map(shards, mesh=mesh, in_specs=in_specs, out_specs=out_specs, check_vma=False)
```

```python
import functools

import jax
import jax.numpy as jnp
from jax import lax
from jax.experimental import pallas as pl
from jax.experimental.pallas import tpu as pltpu
from jax.sharding import PartitionSpec as P

W = 48
STRIDE = 12
DYM = 3
GX = 16
GZX = 128
SHARP = 80.0
EPSILON = 1e-06

HALF = W // 2
BLOCK = W + 2
REACH = DYM + 1
LANES = 128
HOP = 64
CHUNK = 6
ROWS_A = 64
ROWS_B = 80
PAD_A = CHUNK
PAD_B = CHUNK + REACH
PIECES = 2
SPREAD = 32
PLAN_ROWS = 16
FIELDS = 24
PAIR = 8
REST = 4
CLOSE = 4
CLOSE_REST = 3
FAR = 4096


def table_kernel(gap_ref):
    row = lax.broadcasted_iota(jnp.int32, gap_ref.shape, 0)
    col = lax.broadcasted_iota(jnp.int32, gap_ref.shape, 1)
    lag = jnp.where(col >= ROWS_B, 1, 0) + jnp.where(col >= 2 * ROWS_B, 1, 0)
    gap_ref[...] = jnp.where(col < 3 * ROWS_B, col - lag * ROWS_B - row, FAR)


def send_kernel(win_ref, shift_ref, gap_ref, low_ref, high_ref, pair_ref, other_ref, plan_ref):
    reach, deep, along = low_ref.shape
    even = lax.axis_index("span") % 2 == 0
    node = win_ref[...]
    own = node.shape[1]
    plan_ref[...] = jnp.zeros(plan_ref.shape, jnp.int32)
    plan_ref[0:1, 0:own] = node >> 8
    plan_ref[1:2, 0:own] = node & 255
    plan_ref[2:5, 0:own] = shift_ref[...]
    plan = plan_ref[...].astype(jnp.float32).astype(jnp.bfloat16)
    for ref in (pair_ref, other_ref):
        ref[reach * deep:reach * deep + 8, 0:LANES] = plan

    def fill(to_low, to_high):
        for p in range(reach):
            to_low[p * deep:(p + 1) * deep, :] = low_ref[p]
            to_high[p * deep:(p + 1) * deep, :] = high_ref[p]

    @pl.when(even)
    def _():
        fill(other_ref, pair_ref)

    @pl.when(jnp.logical_not(even))
    def _():
        fill(pair_ref, other_ref)


def decode(plan, own, planes, deep, inner, table):
    device = lax.axis_index("span")
    last = lax.axis_size("span") - 1
    tile_rows = planes // STRIDE
    slot = lax.broadcasted_iota(jnp.int32, (1, LANES), 1)
    node = plan[0:1] * 256 + plan[1:2]
    dy, dz, dx = plan[2:3], plan[3:4], plan[4:5]
    row = (node >> (GZX.bit_length() - 1)) - device * tile_rows
    rest = node & (GZX - 1)
    cy = STRIDE * row + STRIDE // 2
    cz = STRIDE * (rest >> (GX.bit_length() - 1)) + STRIDE // 2
    cx = STRIDE * (rest & (GX - 1)) + STRIDE // 2
    start = jnp.maximum(cy - HALF, jnp.where(device == 0, -CHUNK, 0))
    stop = jnp.minimum(cy + HALF, jnp.where(device == last, planes + CHUNK, planes))
    mine = slot < own
    lower = (slot >= own) & (slot < 2 * own)
    upper = (slot >= 2 * own) & (slot < 3 * own)
    wanted = (
        mine | (lower & (row < 0) & (row >= -tile_rows))
        | (upper & (row >= tile_rows) & (row < 2 * tile_rows))
    )
    if inner:
        low = jnp.maximum(start, CHUNK)
        high = jnp.minimum(stop, planes - CHUNK)
        wanted = mine
    else:
        below = start < CHUNK
        low = jnp.where(mine & jnp.logical_not(below), planes - CHUNK, start)
        high = jnp.where(mine & below, CHUNK, stop)
    width = jnp.where(wanted, high - low, 0)
    count = sum([jnp.where(width > CHUNK * c, 1, 0) for c in range(W // CHUNK)])
    sx = cx + dx - HALF - 1
    sz = cz + dz - HALF - 1
    z_a = jnp.minimum(jnp.maximum(cz - HALF, 0) & -16, deep - ROWS_A)
    z_b = jnp.where(sz + BLOCK <= ROWS_B, 0, deep - ROWS_B)
    values = (
        jnp.where(cx + HALF <= LANES, 0, 1),
        z_a,
        jnp.where(sx + BLOCK <= LANES, 0, 1),
        z_b,
        dy,
        z_a + dz - z_b,
        (dx + LANES) & (LANES - 1),
        cz - HALF - z_a,
        start + dy - 1 + PAD_B,
        stop + dy + PAD_B,
        jnp.where(start == cy - HALF, 1, 0),
        jnp.where(stop == cy + HALF, 1, 0),
        low,
        count,
        cx - HALF,
        sx,
        sz - z_b,
        jnp.where((row == 0) | (row == tile_rows - 1), 1, 0),
    )
    for at, value in enumerate(values):
        table[at:at + 1, :] = jnp.where(slot < 3 * own, value, 0)
    return jnp.where(
        mine | (lower & (row == -1)) | (upper & (row == tile_rows)),
        (row + 1) * GZX + rest, -1)


def set_masks(masks, s, table):
    f_a, f_b = table[0, s], table[2, s]
    z_from, x_from = table[7, s], table[14, s]
    sx, zb_from = table[15, s], table[16, s]
    reach_x = sx + 1

    def in_x(rows, half, frame_at, low, high):
        lane = (lax.broadcasted_iota(jnp.int32, (rows, LANES), 1) + half * HOP) & (LANES - 1)
        x = lane + jnp.where(lane < HOP, LANES * frame_at, 0)
        return (x >= low) & (x < high)

    def in_z(rows, low, count):
        z = lax.broadcasted_iota(jnp.int32, (rows, LANES), 0)
        return (z >= low) & (z < low + count)

    row = lax.broadcasted_iota(jnp.int32, (16, LANES), 0)
    wide = row == 3
    low = jnp.where(wide, sx, reach_x + row - 1)
    high = low + jnp.where(wide, BLOCK, jnp.where(row < 3, W, 0))
    z_a = in_z(ROWS_A, z_from, W)
    z_b = in_z(ROWS_B, zb_from, BLOCK)
    at = 0
    for rows, frame_at, x_low, x_high, z in (
        (ROWS_A, f_a, x_from, x_from + W, z_a),
        (ROWS_B, f_b, sx, sx + BLOCK, z_b),
        (16, f_b, low, high, None),
    ):
        for half in range(2):
            inside = in_x(rows, half, frame_at, x_low, x_high)
            inside = inside if z is None else inside & z
            masks[s, at:at + rows] = jnp.where(inside, 1.0, 0.0).astype(jnp.bfloat16)
            at += rows


def set_units(units, total, s, low, planes, most):
    for c in range(most):
        units[total + c] = s + (low + planes * c + 64) * 256


def frame(v, fr, at):
    low = v[:, :LANES]
    high = jnp.concatenate([v[:, LANES:], v[:, HOP:LANES]], axis=1)
    fr[0, 0, at] = low
    fr[0, 1, at] = high
    fr[1, 0, at] = pltpu.roll(low, HOP, 1)
    fr[1, 1, at] = pltpu.roll(high, HOP, 1)


def run_units(half, total, units, table, spare, fr_a, fr_b, acc, sq_a, sq_b, masks):
    for at in range(REST - 1):
        units[total + at] = spare + 64 * 256
    ones = jnp.where(
        lax.broadcasted_iota(jnp.int32, (16, half * LANES), 0) == 0, 1.0, 0.0
    ).astype(jnp.bfloat16)

    def step(first, width):
        for h in range(width):
            code = units[first + h]
            s = code & 255
            y = (code >> 8) - 64
            y_two = y + half
            f_a = table[0, s]
            z_a = pl.multiple_of(table[1, s], 16)
            f_b = table[2, s]
            z_b = pl.multiple_of(table[3, s], 16)
            dy = table[4, s]
            dx = table[6, s]
            one_a = masks[s, 0:ROWS_A]
            two_a = masks[s, ROWS_A:2 * ROWS_A]
            at = 2 * ROWS_A
            one_b = masks[s, at:at + ROWS_B]
            two_b = masks[s, at + ROWS_B:at + 2 * ROWS_B]
            at += 2 * ROWS_B
            rows = masks[s, at:at + 16] + masks[s, at + 16:at + 32]
            a = [
                fr_a[0, f_a, y + PAD_A + p, pl.ds(z_a, ROWS_A), :] * one_a
                + fr_a[1, f_a, y_two + PAD_A + p, pl.ds(z_a, ROWS_A), :] * two_a
                for p in range(half)
            ]
            b = [
                fr_b[0, f_b, y + dy - 1 + PAD_B + p, pl.ds(z_b, ROWS_B), :] * one_b
                + fr_b[1, f_b, y_two + dy - 1 + PAD_B + p, pl.ds(z_b, ROWS_B), :] * two_b
                for p in range(half + 2)
            ]
            left = [
                jnp.concatenate(
                    [pltpu.roll(v, (dx + lag - 1 + LANES) & (LANES - 1), 1) for v in a], axis=1)
                for lag in range(3)
            ]
            left.append(jnp.concatenate([rows] * half, axis=1))
            left = jnp.concatenate(left, axis=0)
            right = [jnp.concatenate(b[lag:lag + half], axis=1) for lag in range(3)]
            right = jnp.concatenate(right + [ones], axis=0)
            acc[s] += lax.dot_general(
                left, right, (((1,), (1,)), ((), ())), preferred_element_type=jnp.float32)
            wide = [v.astype(jnp.float32) for v in a]
            sq_a[s] += sum([v * v for v in wide])
            wide = [v.astype(jnp.float32) for v in b[1:-1]]
            sq_b[s] += sum([v * v for v in wide])

    def wide_step(t, carry):
        step(PAIR * t, PAIR)
        return carry

    full = (total + REST - 1) // PAIR
    lax.fori_loop(0, full, wide_step, 0)

    @pl.when(total > PAIR * full)
    def _():
        step(PAIR * full, REST)


def inner_kernel(
    plan_ref, first_ref, second_ref, fr_a, fr_b, masks, acc, sq_a, sq_b,
    table_v, table, units, sem_t,
):
    planes, deep, along = first_ref.shape
    own = (acc.shape[0] - 1) // 3
    device = lax.axis_index("span")
    last = lax.axis_size("span") - 1
    piece = planes // PIECES
    decode(plan_ref[...], own, planes, deep, True, table_v)
    to_scalar = pltpu.make_async_copy(table_v, table, sem_t)
    to_scalar.start()
    for ref, fr, pad in ((first_ref, fr_a, PAD_A), (second_ref, fr_b, PAD_B)):
        def body(i, carry, ref=ref, fr=fr, pad=pad):
            for p in range(piece):
                at = i * piece + p
                frame(ref[at], fr, at + pad)
            return carry

        lax.fori_loop(0, PIECES, body, 0)

    @pl.when((device == 0) | (device == last))
    def _():
        zero = jnp.zeros((2, 2, CHUNK, deep, LANES), jnp.bfloat16)
        fr_a[:, :, 0:PAD_A] = zero
        fr_a[:, :, PAD_A + planes:] = zero
        fr_b[:, :, 0:CHUNK] = zero
        fr_b[:, :, PAD_B + planes + REACH:] = zero

    to_scalar.wait()

    def prepare(s, total):
        set_masks(masks, s, table)
        for ref in (acc, sq_a, sq_b):
            ref[s] = jnp.zeros(ref.shape[1:], jnp.float32)
        set_units(units, total, s, table[12, s], 2 * CHUNK, W // CHUNK // 2)
        return total + (table[13, s] >> 1)

    total = lax.fori_loop(0, own, prepare, 0)
    run_units(CHUNK, total, units, table, 3 * own, fr_a, fr_b, acc, sq_a, sq_b, masks)


def finish_slots(width, alive, active, table, out_ref, gap_base, fr_b, masks, acc, sq_a, sq_b):
    cols = 2 * LANES
    col_one = lax.broadcasted_iota(jnp.int32, (1, cols), 1)
    lag_one = jnp.where(col_one >= ROWS_B, 1, 0) + jnp.where(col_one >= 2 * ROWS_B, 1, 0)
    lag_one = lag_one + jnp.where(col_one >= 3 * ROWS_B, 1, 0)
    z_one = col_one - lag_one * ROWS_B
    lag_18 = jnp.broadcast_to(lag_one, (18, cols))
    lane_18 = lax.broadcasted_iota(jnp.int32, (18, LANES), 1)
    lane_4 = lax.broadcasted_iota(jnp.int32, (4, LANES), 1)
    slant = lax.broadcasted_iota(jnp.int32, (8, cols), 1)
    slant = slant - lax.broadcasted_iota(jnp.int32, (8, cols), 0)
    mean_lane = lax.broadcasted_iota(jnp.int32, (1, LANES), 1) == 3 * ROWS_B - LANES

    def finish(t, carry):
        for h in range(width):
            s = active[width * t + h]
            f_b = table[2, s]
            z_b = pl.multiple_of(table[3, s], 16)
            offset = table[5, s]
            low_z = table[16, s] + 1
            band = (gap_base[...] >= offset - 1) & (gap_base[...] <= offset + 1)
            tops = [None] * 9
            lows = []
            for lag_x in range(3):
                part = jnp.where(band, acc[s, lag_x * ROWS_A:(lag_x + 1) * ROWS_A, :], 0.0)
                part = sum([part[8 * i:8 * i + 8] for i in range(ROWS_A // 8)])
                for lag_z in range(3):
                    hit = ((slant - (offset + lag_z - 1)) & 7) == 0
                    tops[3 * lag_z + lag_x] = jnp.sum(
                        jnp.where(hit, part, 0.0), axis=0, keepdims=True)
            for lag_z in range(3):
                low = low_z + lag_z - 1
                inside = (z_one >= low) & (z_one < low + W)
                lows.append(jnp.where(inside, acc[s, 3 * ROWS_A:3 * ROWS_A + 3, :], 0.0))
            stack = jnp.concatenate(tops + lows, axis=0)

            at = 2 * ROWS_A
            mask = masks[s, at:at + ROWS_B].astype(jnp.float32)
            ends = [
                fr_b[0, f_b, table[8 + i, s], pl.ds(z_b, ROWS_B), :].astype(jnp.float32)
                * (mask * table[10 + i, s].astype(jnp.float32))
                for i in range(2)
            ]
            row_b = jnp.where(
                lag_one == 1, acc[s, 3 * ROWS_A + 3:3 * ROWS_A + 4, :], 0.0)
            row_a = jnp.sum(acc[s, ROWS_A:2 * ROWS_A, LANES:], axis=0, keepdims=True)
            sums = [
                jnp.where(mean_lane, row_a, 0.0),
                jnp.sum(sq_a[s], axis=0, keepdims=True),
                jnp.sum(ends[0] + ends[1], axis=0, keepdims=True)
                + row_b[:, :LANES] + row_b[:, LANES:],
                jnp.sum(
                    sq_b[s] + (ends[0] * ends[0] + ends[1] * ends[1]), axis=0, keepdims=True),
            ]
            sums = jnp.sum(jnp.concatenate(sums, axis=0), axis=1, keepdims=True)
            total_18 = jnp.zeros((18, LANES), jnp.float32)
            for lag_y in range(3):
                part = jnp.sum(jnp.where(lag_18 == lag_y, stack, 0.0), axis=1, keepdims=True)
                total_18 = total_18 + jnp.where(lane_18 == s + SPREAD * lag_y, part, 0.0)
            out_ref[0:18] += total_18
            out_ref[18:22] += jnp.where(lane_4 == s, sums, 0.0)
        return carry

    lax.fori_loop(0, (alive + width - 1) // width, finish, 0)


def outer_kernel(
    plan_ref, pair_ref, other_ref, gap_base, fr_a, fr_b_in, masks_in, acc_in, sq_a_in, sq_b_in,
    out_ref, table_v, fr_b, masks, acc, sq_a, sq_b, table, units, active, sem_t,
):
    deep = fr_a.shape[3]
    planes = fr_a.shape[2] - 2 * PAD_A
    own = (acc.shape[0] - 1) // 3
    even = lax.axis_index("span") % 2 == 0
    base = REACH * deep
    from_pair, from_other = [
        ref[base:base + 8, 0:LANES].astype(jnp.float32).astype(jnp.int32)
        for ref in (pair_ref, other_ref)
    ]
    below = jnp.where(even, from_other, from_pair)
    above = jnp.where(even, from_pair, from_other)
    plan = plan_ref[...] + pltpu.roll(below, own, 1) + pltpu.roll(above, 2 * own, 1)
    target = decode(plan, own, planes, deep, False, table_v)
    to_scalar = pltpu.make_async_copy(table_v, table, sem_t)
    to_scalar.start()
    out_ref[...] = jnp.zeros(out_ref.shape, jnp.float32)
    out_ref[22:23] = target.astype(jnp.float32)

    low_at, high_at = CHUNK, PAD_B + planes
    pair_at = jnp.where(even, high_at, low_at)
    other_at = jnp.where(even, low_at, high_at)
    for p in range(REACH):
        frame(pair_ref[p * deep:(p + 1) * deep, :], fr_b, pair_at + p)
        frame(other_ref[p * deep:(p + 1) * deep, :], fr_b, other_at + p)
    to_scalar.wait()

    def prepare_own(s, carry):
        total, alive = carry
        active[alive] = s
        set_units(units, total, s, table[12, s], CHUNK, 2)
        return total + table[13, s] * table[17, s], alive + table[17, s]

    carry = lax.fori_loop(0, own, prepare_own, (0, 0))

    def prepare(s, carry):
        total, alive = carry
        count = table[13, s]

        @pl.when(count > 0)
        def _():
            set_masks(masks, s, table)
            for ref in (acc, sq_a, sq_b):
                ref[s] = jnp.zeros(ref.shape[1:], jnp.float32)
            active[alive] = s
            set_units(units, total, s, table[12, s], CHUNK, W // CHUNK)

        return total + count, alive + jnp.where(count > 0, 1, 0)

    total, alive = lax.fori_loop(own, 3 * own, prepare, carry)
    spare = 3 * own
    for at in range(CLOSE - 1):
        active[alive + at] = spare
    run_units(CHUNK // 2, total, units, table, spare, fr_a, fr_b, acc, sq_a, sq_b, masks)
    finish_slots(CLOSE, alive, active, table, out_ref, gap_base, fr_b, masks, acc, sq_a, sq_b)


def rest_kernel(
    table_v, gap_base, fr_a, fr_b, masks, acc_in, sq_a_in, sq_b_in,
    out_ref, acc, sq_a, sq_b, table, units, active, sem_t,
):
    own = (acc.shape[0] - 1) // 3
    to_scalar = pltpu.make_async_copy(table_v, table, sem_t)
    to_scalar.start()
    out_ref[...] = jnp.zeros(out_ref.shape, jnp.float32)
    to_scalar.wait()

    def listed(s, carry):
        total, alive = carry
        active[alive] = s
        set_units(units, total, s, table[12, s], CHUNK, 2)
        other = 1 - table[17, s]
        return total + table[13, s] * other, alive + other

    total, alive = lax.fori_loop(0, own, listed, (0, 0))
    spare = 3 * own
    for at in range(CLOSE - 1):
        active[alive + at] = spare
    run_units(CHUNK // 2, total, units, table, spare, fr_a, fr_b, acc, sq_a, sq_b, masks)
    finish_slots(CLOSE_REST, alive, active, table, out_ref, gap_base, fr_b, masks, acc, sq_a, sq_b)


def update_kernel(own, mine_ref, rest_ref, pair_ref, other_ref, out_ref):
    tile_rows = out_ref.shape[0]
    even = lax.axis_index("span") % 2 == 0
    mine = mine_ref[...] + rest_ref[...]
    pair = pair_ref[...]
    other = other_ref[...]
    below = jnp.where(even, other, pair)
    above = jnp.where(even, pair, other)
    lane = lax.broadcasted_iota(jnp.int32, mine.shape, 1)
    slot = lane & (SPREAD - 1)
    total = mine + jnp.where(
        slot < own,
        pltpu.roll(below, LANES - 2 * own, 1) + pltpu.roll(above, LANES - own, 1),
        jnp.where(
            slot < 2 * own, pltpu.roll(below, own, 1),
            jnp.where(slot < 3 * own, pltpu.roll(above, 2 * own, 1), 0.0)))

    def lead(v):
        return v + pltpu.roll(v, LANES - SPREAD, 1) + pltpu.roll(v, LANES - 2 * SPREAD, 1)

    def spread(v):
        v = jnp.where(lane[0:v.shape[0]] < SPREAD, v, 0.0)
        return v + pltpu.roll(v, SPREAD, 1) + pltpu.roll(v, 2 * SPREAD, 1)

    stats = spread(total[18:22])
    voxels = float(W) ** 3
    block_voxels = float(BLOCK) ** 3
    mean_a = stats[0:1] / voxels
    energy_a = jnp.maximum(stats[1:2] / voxels - mean_a * mean_a, 0.0)
    mean_b = stats[2:3] / block_voxels
    energy_b = jnp.maximum(stats[3:4] / block_voxels - mean_b * mean_b, 0.0)
    normaliser = voxels * jnp.sqrt((energy_a + EPSILON) * (energy_b + EPSILON))
    scaled = SHARP * ((total[0:9] - mean_a * total[9:18]) / normaliser)
    used = lane[0:9] < 3 * SPREAD
    scaled = jnp.where(used, scaled, -1e30)
    top = jnp.max(scaled, axis=0, keepdims=True)
    top = jnp.maximum(top, jnp.maximum(
        pltpu.roll(top, LANES - SPREAD, 1), pltpu.roll(top, LANES - 2 * SPREAD, 1)))
    weights = jnp.where(used, jnp.exp(scaled - spread(top)), 0.0)
    lag_row = lax.broadcasted_iota(jnp.int32, weights.shape, 0)
    lag_z = jnp.where(lag_row >= 6, 1.0, jnp.where(lag_row >= 3, 0.0, -1.0))
    lag_x = jnp.where(
        (lag_row == 0) | (lag_row == 3) | (lag_row == 6), -1.0,
        jnp.where((lag_row == 2) | (lag_row == 5) | (lag_row == 8), 1.0, 0.0))
    lag_y = jnp.where(lane[0:1] >= 2 * SPREAD, 1.0, jnp.where(lane[0:1] >= SPREAD, 0.0, -1.0))
    column = jnp.sum(weights, axis=0, keepdims=True)
    moments = lead(jnp.concatenate([
        column * lag_y,
        jnp.sum(weights * lag_z, axis=0, keepdims=True),
        jnp.sum(weights * lag_x, axis=0, keepdims=True),
        column,
        jnp.zeros((4, LANES), jnp.float32),
    ], axis=0))
    found = jnp.where(lane[0:8] < 3 * own, moments / moments[3:4], 0.0)
    high = found.astype(jnp.bfloat16).astype(jnp.float32)
    left = found - high
    middle = left.astype(jnp.bfloat16).astype(jnp.float32)
    parts = jnp.concatenate(
        [high, middle, left - middle, jnp.zeros((8, LANES), jnp.float32)], axis=0
    ).astype(jnp.bfloat16)
    place = lax.broadcasted_iota(jnp.int32, ((tile_rows + 2) * GZX, LANES), 0)
    node = jnp.where(place == mine[22:23].astype(jnp.int32), 1.0, 0.0).astype(jnp.bfloat16)
    field = lax.dot_general(
        parts, node, (((1,), (1,)), ((), ())), preferred_element_type=jnp.float32)
    field = field[0:8] + field[8:16] + field[16:24]
    lane_x = lane[0:8] & (GX - 1)
    for row in range(tile_rows):
        before, centre, after = [
            field[:, (row + i) * GZX:(row + i + 1) * GZX] for i in range(3)]
        near = before + after
        near = near + jnp.where(lane[0:8] >= GX, pltpu.roll(centre, GX, 1), 0.0)
        near = near + jnp.where(lane[0:8] < GZX - GX, pltpu.roll(centre, LANES - GX, 1), 0.0)
        near = near + jnp.where(lane_x >= 1, pltpu.roll(centre, 1, 1), 0.0)
        near = near + jnp.where(lane_x < GX - 1, pltpu.roll(centre, LANES - 1, 1), 0.0)
        out_ref[row] = (0.4 * centre + 0.1 * near)[0:3]


def shards(first, second, windows, shifts):
    planes, deep, along = first.shape
    own = windows.shape[0]
    slots = 3 * own + 1
    count = lax.axis_size("span")
    pairs = [(i, i ^ 1) for i in range(count)]
    others = [(i, i + 1) for i in range(1, count - 1, 2)]
    others = others + [(b, a) for a, b in others]
    vmem = pl.BlockSpec(memory_space=pltpu.VMEM)

    def limit(mib):
        return pltpu.CompilerParams(vmem_limit_bytes=mib << 20)

    busy = pl.CostEstimate(flops=20 * 10**9, bytes_accessed=0, transcendentals=0)
    gap = pl.pallas_call(
        table_kernel,
        out_shape=jax.ShapeDtypeStruct((ROWS_A, 2 * LANES), jnp.int32),
        out_specs=vmem,
        compiler_params=limit(4),
        cost_estimate=pl.CostEstimate(flops=13 * 10**8, bytes_accessed=0, transcendentals=0),
        name="gap_table",
    )()
    message = jax.ShapeDtypeStruct((REACH * deep + PLAN_ROWS, along), second.dtype)
    tile, gap = lax.optimization_barrier((second, gap))
    low_planes, high_planes = tile[:REACH], tile[planes - REACH:]
    to_pair, to_other, plan = pl.pallas_call(
        send_kernel,
        out_shape=(message, message, jax.ShapeDtypeStruct((8, LANES), jnp.int32)),
        in_specs=[vmem] * 5,
        out_specs=(vmem,) * 3,
        compiler_params=limit(4),
        cost_estimate=busy,
        name="planes_to_send",
    )(windows[None], shifts, gap, low_planes, high_planes)
    from_other = lax.ppermute(to_other, "span", others)
    from_pair = lax.ppermute(to_pair, "span", pairs)
    mask_rows = 2 * (ROWS_A + ROWS_B + 16)
    frames_a = jax.ShapeDtypeStruct((2, 2, planes + 2 * PAD_A, deep, LANES), jnp.bfloat16)
    state = (
        jax.ShapeDtypeStruct((2, 2, planes + 2 * PAD_B, deep, LANES), jnp.bfloat16),
        jax.ShapeDtypeStruct((slots, mask_rows, LANES), jnp.bfloat16),
        jax.ShapeDtypeStruct((slots, 3 * ROWS_A + 16, 2 * LANES), jnp.float32),
        jax.ShapeDtypeStruct((slots, ROWS_A, LANES), jnp.float32),
        jax.ShapeDtypeStruct((slots, ROWS_B, LANES), jnp.float32),
    )
    scratch = [
        pltpu.SMEM((FIELDS, LANES), jnp.int32),
        pltpu.SMEM(((3 * own + 1) * (W // CHUNK) + PAIR,), jnp.int32),
    ]
    fr_a, *held = pl.pallas_call(
        inner_kernel,
        out_shape=(frames_a, *state),
        in_specs=[vmem] * 3,
        out_specs=(vmem,) * 6,
        scratch_shapes=[
            pltpu.VMEM((FIELDS, LANES), jnp.int32), *scratch, pltpu.SemaphoreType.DMA],
        compiler_params=limit(8),
        cost_estimate=busy,
        name="inner_sums",
    )(plan, first, second)
    sums, fields, *held = pl.pallas_call(
        outer_kernel,
        out_shape=(
            jax.ShapeDtypeStruct((24, LANES), jnp.float32),
            jax.ShapeDtypeStruct((FIELDS, LANES), jnp.int32), *state),
        in_specs=[vmem] * 10,
        out_specs=(vmem,) * 7,
        input_output_aliases={5 + i: 2 + i for i in range(5)},
        scratch_shapes=[
            *scratch, pltpu.SMEM((slots + CLOSE,), jnp.int32), pltpu.SemaphoreType.DMA],
        compiler_params=limit(8),
        name="outer_sums",
    )(plan, from_pair, from_other, gap, fr_a, *held)
    other_sums = lax.ppermute(sums, "span", others)
    pair_sums = lax.ppermute(sums, "span", pairs)
    rest, *_ = pl.pallas_call(
        rest_kernel,
        out_shape=(jax.ShapeDtypeStruct((24, LANES), jnp.float32), *state[2:]),
        in_specs=[vmem] * 8,
        out_specs=(vmem,) * 4,
        input_output_aliases={5 + i: 1 + i for i in range(3)},
        scratch_shapes=[
            *scratch, pltpu.SMEM((slots + CLOSE,), jnp.int32), pltpu.SemaphoreType.DMA],
        compiler_params=limit(8),
        cost_estimate=busy,
        name="rest_of_sums",
    )(fields, gap, fr_a, *held)
    field = pl.pallas_call(
        functools.partial(update_kernel, own),
        out_shape=jax.ShapeDtypeStruct((planes // STRIDE, 3, GZX), jnp.float32),
        in_specs=[vmem] * 4,
        out_specs=vmem,
        compiler_params=limit(4),
        name="smoothed_update",
    )(sums, rest, pair_sums, other_sums)
    return jnp.transpose(field, (1, 0, 2))


def solution(mesh):
    in_specs = (
        P(("grp", "span"), None, None),
        P(("grp", "span"), None, None),
        P(("grp", "span")),
        P(None, ("grp", "span")),
    )
    out_specs = P(None, ("grp", "span"), None)
    return jax.shard_map(shards, mesh=mesh, in_specs=in_specs, out_specs=out_specs, check_vma=False)
```
